32 devices in a mesh: rep: 8 (over y, x, core), shard: 4 (over z).
Axes of the slice: x: 2, y: 2, z: 4, core: 2. Of those that a mesh axis runs over, the one named last changes fastest.
Arguments:
- tokens: bfloat16 [2, 4096, 2048], P(None, ('rep', 'shard')), may hold values from -6 to 6
- attn_gain: float32 [2048], P('shard'), may hold values from 0.25 to 1.75
- q_weight: float32 [3072, 2048], P(None, 'shard'), may hold values from -0.125 to 0.125
- kva_weight: float32 [576, 2048], P(None, 'shard'), may hold values from -0.125 to 0.125
- kv_gain: float32 [512], P('shard'), may hold values from 0.25 to 1.75
- kvb_weight: float32 [512, 4096], P('shard'), may hold values from -0.25 to 0.25
- out_weight: float32 [2048, 2048], P('shard'), may hold values from -2 to 2
- ffn_gain: float32 [2048], P('shard'), may hold values from 0.25 to 1.75
- router_weight: float32 [64, 2048], P(None, 'shard'), may hold values from -0.066 to 0.066
- shared_gate: float32 [1408, 2048], P('shard'), may hold values from -0.125 to 0.125
- shared_up: float32 [1408, 2048], P('shard'), may hold values from -0.125 to 0.125
- shared_down: float32 [1408, 2048], P('shard'), may hold values from -0.15625 to 0.15625
- expert_gate: float32 [2, 1408, 2048], P(None, 'shard'), may hold values from -0.125 to 0.125
- expert_up: float32 [2, 1408, 2048], P(None, 'shard'), may hold values from -0.125 to 0.125
- expert_down: float32 [2, 1408, 2048], P(None, 'shard'), may hold values from -12 to 12
- expert_ids: int32 [2, 4096, 6], P(None, ('rep', 'shard')), may hold values from 0 to 63, as said below
- cotangent: bfloat16 [2, 4096, 2048], P(None, ('rep', 'shard')), may hold values from -6 to 6
Outputs:
- layer_output: bfloat16 [2, 4096, 2048], P(None, ('rep', 'shard'))
- input_grad: bfloat16 [2, 4096, 2048], P(None, ('rep', 'shard'))
- attn_gain_grad: float32 [2048], P('shard')
- q_weight_grad: float32 [3072, 2048], P(None, 'shard')
- kva_weight_grad: float32 [576, 2048], P(None, 'shard')
- kv_gain_grad: float32 [512], P('shard')
- kvb_weight_grad: float32 [512, 4096], P('shard')
- out_weight_grad: float32 [2048, 2048], P('shard')
- ffn_gain_grad: float32 [2048], P('shard')
- router_weight_grad: float32 [64, 2048], P(None, 'shard')
- shared_gate_grad: float32 [1408, 2048], P('shard')
- shared_up_grad: float32 [1408, 2048], P('shard')
- shared_down_grad: float32 [1408, 2048], P('shard')
- expert_gate_grad: float32 [2, 1408, 2048], P(None, 'shard')
- expert_up_grad: float32 [2, 1408, 2048], P(None, 'shard')
- expert_down_grad: float32 [2, 1408, 2048], P(None, 'shard')
The draws below stay inside these ranges and needn't reach their ends.
Inputs may be any that keep to these rules, and one draw needn't show every extreme that they name: `expert_ids`: each row names 6 different experts. In each micro-batch the 128 rows of one device name each expert below 2 at least 8 and at most 16 times, and for each expert below 2 the rows of some device and micro-batch name it exactly 16 times.
All inputs are finite; a program needn't handle non-finite values.
Results may differ from the reference program's by a relative error of at most 0.04.
Values may be sent and summed in bfloat16 or wider, within the bound.
A program may use at most 384 MiB of HBM per device.

```python
import jax
import jax.numpy as jnp
from jax import lax

D = 2048
HEADS = 16
NOPE = 128
ROPE = 64
VDIM = 128
RANK = 512
FF = 1408
EXPERTS = 64
TOPK = 6
EXP_WIN = 2
MICRO = 2
MASK_BLOCK = 256
TOK_DEV = 128
CAP = 16
TOKENS = 4096
N_REP = 8
N_SHARD = 4


def draw_expert_ids(key, part):
    key = jax.random.fold_in(key, 11)
    blocks = MICRO * TOKENS // TOK_DEV
    count_key, forced_key, member_key, other_key, column_key = jax.random.split(key, 5)
    counts = CAP - jax.random.randint(count_key, (blocks, EXP_WIN), 0, CAP // 2 + 1)
    forced = jax.random.randint(forced_key, (EXP_WIN,), 0, blocks)
    counts = jnp.where(jnp.arange(blocks)[:, None] == forced[None, :], CAP, counts)
    shuffle_keys = jax.random.split(member_key, blocks * EXP_WIN)
    shuffles = jax.vmap(lambda k: jax.random.permutation(k, TOK_DEV))(shuffle_keys).reshape(blocks, EXP_WIN, TOK_DEV)
    places = jnp.argsort(shuffles, axis=-1)
    member = jnp.swapaxes(places < counts[:, :, None], 1, 2)
    window_ids = jnp.arange(EXP_WIN, dtype=jnp.int32)
    window_scores = jnp.where(member, (1 << 29) + window_ids, -1 - window_ids)
    others = jax.random.randint(other_key, (blocks, TOK_DEV, EXPERTS - EXP_WIN), 0, 1 << 20) * EXPERTS + jnp.arange(EXPERTS - EXP_WIN, dtype=jnp.int32)
    all_scores = jnp.concatenate([window_scores, others], axis=-1)
    chosen = lax.top_k(all_scores, TOPK)[1]
    column_scores = jax.random.randint(column_key, (blocks, TOK_DEV, TOPK), 0, 1 << 20) * TOPK + jnp.arange(TOPK, dtype=jnp.int32)
    columns = jnp.argsort(column_scores, axis=-1)
    chosen = jnp.take_along_axis(chosen, columns, axis=-1)
    return chosen.reshape(MICRO, TOKENS, TOPK).astype(jnp.int32)


def block_scale(key, shape, cuts, smallest, largest):
    level = 1.0
    for position, blocks in cuts:
        steps = jax.random.uniform(jax.random.fold_in(jax.random.fold_in(key, 6), position), (blocks,), jnp.float32, smallest / len(cuts), largest / len(cuts))
        level = level * jnp.repeat(jnp.exp(steps), shape[position] // blocks).reshape((-1,) + (1,) * (len(shape) - 1 - position))
    return level


def normal_values(key, extent, scale, limit, shards=(), held_as=jnp.bfloat16):
    array = jax.random.normal(key, extent, jnp.float32) * scale
    if len(shards) > 0:
        array = block_scale(key, extent, shards, -0.22, 0.18) * array
    return jnp.clip(array, min=-limit, max=limit).astype(held_as)


def setup_inputs(seed: int = 0) -> dict:
    arg_keys = jax.random.split(jax.random.key(seed), 18)
    tokens = normal_values(arg_keys[0], (MICRO, TOKENS, D), 1.0, 6.0, ((1, 32),))
    attn_gain = jnp.clip(1.0 + 0.15 * jax.random.normal(arg_keys[1], (D,), jnp.float32), 0.25, 1.75)
    q_weight = normal_values(arg_keys[2], (HEADS * (NOPE + ROPE), D), D ** -0.5, 0.125, ((1, 4),), jnp.float32)
    kva_weight = normal_values(arg_keys[3], (RANK + ROPE, D), D ** -0.5, 0.125, ((1, 4),), jnp.float32)
    kv_gain = jnp.clip(1.0 + 0.15 * jax.random.normal(arg_keys[4], (RANK,), jnp.float32), 0.25, 1.75)
    kvb_weight = normal_values(arg_keys[5], (RANK, HEADS * (NOPE + VDIM)), RANK ** -0.5, 0.25, ((0, 4),), jnp.float32)
    out_weight = normal_values(arg_keys[6], (HEADS * VDIM, D), 8 ** -0.5, 2.0, ((0, 4),), jnp.float32)
    ffn_gain = jnp.clip(1.0 + 0.15 * jax.random.normal(arg_keys[7], (D,), jnp.float32), 0.25, 1.75)
    router_weight = normal_values(arg_keys[8], (EXPERTS, D), 0.011, 0.066, ((1, 4),), jnp.float32)
    shared_gate = normal_values(arg_keys[9], (FF, D), D ** -0.5, 0.125, ((0, 4),), jnp.float32)
    shared_up = normal_values(arg_keys[10], (FF, D), D ** -0.5, 0.125, ((0, 4),), jnp.float32)
    shared_down = normal_values(arg_keys[11], (FF, D), FF ** -0.5, 0.15625, ((0, 4),), jnp.float32)
    expert_gate = normal_values(arg_keys[12], (EXP_WIN, FF, D), D ** -0.5, 0.125, ((1, 4),), jnp.float32)
    expert_up = normal_values(arg_keys[13], (EXP_WIN, FF, D), D ** -0.5, 0.125, ((1, 4),), jnp.float32)
    expert_down = normal_values(arg_keys[14], (EXP_WIN, FF, D), 2.0, 12.0, ((1, 4),), jnp.float32)
    expert_ids = draw_expert_ids(jax.random.fold_in(arg_keys[17], 71), 0)
    cotangent = normal_values(arg_keys[16], (MICRO, TOKENS, D), 1.0, 6.0, ((1, 32),))
    return dict(tokens=tokens, attn_gain=attn_gain, q_weight=q_weight, kva_weight=kva_weight, kv_gain=kv_gain, kvb_weight=kvb_weight, out_weight=out_weight, ffn_gain=ffn_gain, router_weight=router_weight, shared_gate=shared_gate, shared_up=shared_up, shared_down=shared_down, expert_gate=expert_gate, expert_up=expert_up, expert_down=expert_down, expert_ids=expert_ids, cotangent=cotangent)


epsilon = 1e-06
rope_base = 10000.0
masked_score = -1e+30
highest = lax.Precision.HIGHEST

@jax.custom_vjp
def low(v):
    return lax.optimization_barrier(v.astype(jnp.bfloat16)).astype(jnp.float32)

@jax.custom_vjp
def low_back(v):
    return v

def low_keep(v):
    return (low(v), None)

def low_pass(kept, grad):
    return (grad,)

def back_keep(v):
    return (v, None)

def back_low(kept, grad):
    return (low(grad),)
low.defvjp(low_keep, low_pass)
low_back.defvjp(back_keep, back_low)

def rms_scale(tensor):
    return lax.rsqrt(lax.optimization_barrier(jnp.mean(tensor * tensor, axis=-1, keepdims=True)) + epsilon)

def rotary_tables(positions, rope_width):
    half_width = rope_width // 2
    frequency = jnp.exp(-jnp.log(rope_base) * (2.0 * jnp.arange(half_width, dtype=jnp.float32) / rope_width))
    angles = positions.astype(jnp.float32)[:, None] * frequency[None, :]
    return (jnp.cos(angles), jnp.sin(angles))

def rotate(tensor, cosine, sine_tab):
    half_width = tensor.shape[-1] // 2
    first_half = tensor[..., :half_width]
    second_half = tensor[..., half_width:]
    return jnp.concatenate([first_half * cosine - second_half * sine_tab, second_half * cosine + first_half * sine_tab], axis=-1)

def slot_table(expert_rows):
    window_ids = jnp.arange(EXP_WIN, dtype=jnp.int32)
    member = jnp.any(expert_rows[..., None, :] == window_ids[:, None], axis=-1).astype(jnp.int32)
    member = jnp.swapaxes(member, -1, -2)
    placed = jnp.cumsum(member, axis=-1) - 1
    slot_ids = jnp.arange(CAP, dtype=jnp.int32)
    hits = (member[None] == 1) & (placed[None] == slot_ids[:, None, None, None])
    return hits.astype(jnp.float32)

def sequence_layer(x_seq, ids_seq, params):
    attn_gain, q_weight, kva_weight, kv_gain, kvb_weight, out_weight, ffn_gain, router_weight, shared_gate, shared_up, shared_down, expert_gate, expert_up, expert_down = params
    length = x_seq.shape[0]
    positions = jnp.arange(length, dtype=jnp.int32)
    cosine, sine_tab = rotary_tables(positions, ROPE)
    h_attn = low(x_seq * rms_scale(x_seq) * low(attn_gain))
    q_raw = low_back(jnp.dot(h_attn, q_weight.T, precision=highest)).reshape(length, HEADS, NOPE + ROPE)
    queries = low(jnp.concatenate([q_raw[..., :NOPE], rotate(q_raw[..., NOPE:], cosine[:, None], sine_tab[:, None])], axis=-1))
    kv_down = low_back(jnp.dot(h_attn, kva_weight.T, precision=highest))
    latent = kv_down[:, :RANK]
    latent_norm = low(latent * rms_scale(latent) * low(kv_gain))
    kv_up = low(low_back(jnp.dot(latent_norm, kvb_weight, precision=highest))).reshape(length, HEADS, NOPE + VDIM)
    key_rope = low(rotate(kv_down[:, RANK:], cosine, sine_tab))
    key_rows = jnp.concatenate([kv_up[..., :NOPE], jnp.broadcast_to(key_rope[:, None, :], (length, HEADS, ROPE))], axis=-1)
    value_rows = kv_up[..., NOPE:]
    score_scale = (NOPE + ROPE) ** (-0.5)
    q_rows = 512 if length % 512 == 0 else length

    def attend(block_item):
        q_block, q_pos = block_item
        scores = low_back(jnp.einsum('qhd,khd->hqk', q_block, key_rows, precision=highest) * score_scale)
        visible = q_pos[:, None] // MASK_BLOCK >= positions[None, :] // MASK_BLOCK
        scores = jnp.where(visible[None], scores, masked_score)
        attn_probs = low(jax.nn.softmax(scores, axis=-1))
        return jnp.einsum('hqk,khd->qhd', attn_probs, value_rows, precision=highest)
    attended = lax.map(jax.checkpoint(attend), (queries.reshape(length // q_rows, q_rows, HEADS, NOPE + ROPE), positions.reshape(length // q_rows, q_rows)))
    attended = low(low_back(attended.reshape(length, HEADS * VDIM)))
    x_mid = x_seq + low_back(jnp.dot(attended, out_weight, precision=highest))
    h_ffn = low(x_mid * rms_scale(x_mid) * low(ffn_gain))
    logits = low_back(jnp.dot(h_ffn, router_weight.T, precision=highest))
    router_probs = jax.nn.softmax(logits, axis=-1)
    gate_pre = low_back(jnp.dot(h_ffn, shared_gate.T, precision=highest))
    up_pre = low_back(jnp.dot(h_ffn, shared_up.T, precision=highest))
    shared_out = jnp.dot(low(jax.nn.silu(gate_pre) * up_pre), shared_down, precision=highest)
    select = slot_table(ids_seq.reshape(N_SHARD, TOK_DEV, TOPK))
    rows_in = h_ffn.reshape(N_SHARD, TOK_DEV, D)
    slot_rows = jnp.einsum('cbet,btd->cbed', select, rows_in, precision=highest)
    slot_gates = jnp.einsum('cbet,bte->cbe', select, router_probs.reshape(N_SHARD, TOK_DEV, EXPERTS)[..., :EXP_WIN], precision=highest)
    expert_pre = low_back(jnp.einsum('cbed,efd->cbef', slot_rows, expert_gate, precision=highest))
    expert_upv = low_back(jnp.einsum('cbed,efd->cbef', slot_rows, expert_up, precision=highest))
    expert_hidden = low(jax.nn.silu(expert_pre) * expert_upv)
    expert_out = low_back(jnp.einsum('cbef,efd->cbed', expert_hidden, expert_down, precision=highest))
    routed = jnp.einsum('cbet,cbe,cbed->btd', select, slot_gates, expert_out, precision=highest).reshape(length, D)
    return x_mid + shared_out + routed

def reference(tokens, attn_gain, q_weight, kva_weight, kv_gain, kvb_weight, out_weight, ffn_gain, router_weight, shared_gate, shared_up, shared_down, expert_gate, expert_up, expert_down, expert_ids, cotangent):
    seq_count = MICRO * N_REP
    length = TOK_DEV * N_SHARD
    x_all = tokens.astype(jnp.float32).reshape(seq_count, length, D)
    ids_all = expert_ids.reshape(seq_count, length, TOPK)
    params = (attn_gain.astype(jnp.float32), q_weight.astype(jnp.float32), kva_weight.astype(jnp.float32), kv_gain.astype(jnp.float32), kvb_weight.astype(jnp.float32), out_weight.astype(jnp.float32), ffn_gain.astype(jnp.float32), router_weight.astype(jnp.float32), shared_gate.astype(jnp.float32), shared_up.astype(jnp.float32), shared_down.astype(jnp.float32), expert_gate.astype(jnp.float32), expert_up.astype(jnp.float32), expert_down.astype(jnp.float32))

    def forward(x_in, weights):

        def per_sequence(carried, seq_item):
            return (carried, jax.checkpoint(sequence_layer)(seq_item[0], seq_item[1], weights))
        return lax.scan(per_sequence, None, (x_in, ids_all))[1]
    result, pullback = jax.vjp(forward, x_all, params)
    gradients = pullback(cotangent.astype(jnp.float32).reshape(seq_count, length, D))
    weight_grads = gradients[1]
    layer_output = result.reshape(MICRO, TOKENS, D).astype(jnp.bfloat16)
    input_grad = gradients[0].reshape(MICRO, TOKENS, D).astype(jnp.bfloat16)
    return (layer_output, input_grad, weight_grads[0], weight_grads[1], weight_grads[2], weight_grads[3], weight_grads[4], weight_grads[5], weight_grads[6], weight_grads[7], weight_grads[8], weight_grads[9], weight_grads[10], weight_grads[11], weight_grads[12], weight_grads[13])
```

```python
import functools

import jax
import jax.numpy as jnp
from jax import lax
from jax.experimental import pallas as pl
from jax.experimental.pallas import tpu as pltpu
from jax.sharding import PartitionSpec as P

HEADS = 16
NOPE = 128
ROPE = 64
VDIM = 128
RANK = 512
EXPERTS = 64
EXP_WIN = 2
MASK_BLOCK = 256
CAP = 16

epsilon = 1e-06
rope_base = 10000.0
masked_score = -1e30
highest = lax.Precision.HIGHEST
bf16 = jnp.bfloat16
f32 = jnp.float32
MESH = pl.DeviceIdType.MESH
HBM = pltpu.HBM
HALF_ROPE = ROPE // 2
HEAD_GROUP = 4
GROUP_LANES = HEAD_GROUP * HALF_ROPE


def dot(a, b, ca, cb):
    return lax.dot_general(a, b, (((ca,), (cb,)), ((), ())), preferred_element_type=f32)


def rms_scale(tensor):
    return lax.rsqrt(jnp.mean(tensor * tensor, axis=-1, keepdims=True) + epsilon)


def norm_back(tensor, inv_rms, gain_vec, gradient):
    scaled_grad = gradient * gain_vec
    inner_mean = jnp.mean(scaled_grad * tensor, axis=-1, keepdims=True)
    input_part = inv_rms * scaled_grad - tensor * (inv_rms * inv_rms * inv_rms) * inner_mean
    gain_part = jnp.sum(gradient * tensor * inv_rms, axis=0)
    return (input_part, gain_part)


def swiglu_back(gate_pre, up_pre, hidden_grad):
    sigmoid_gate = jax.nn.sigmoid(gate_pre)
    silu_gate = gate_pre * sigmoid_gate
    slope = sigmoid_gate * (1.0 + gate_pre * (1.0 - sigmoid_gate))
    return (
        (hidden_grad * up_pre * slope).astype(bf16),
        (hidden_grad * silu_gate).astype(bf16),
    )


def head_scores(qn, q1, q2, kv, k1, k2, limit, scale, head):
    lane = lax.broadcasted_iota(jnp.int32, (1, GROUP_LANES), 1)
    mine = (lane >= head * HALF_ROPE) & (lane < (head + 1) * HALF_ROPE)
    width = NOPE + VDIM
    q_head = qn[:, head * NOPE : (head + 1) * NOPE]
    k_head = kv[:, head * width : head * width + NOPE]
    v_head = kv[:, head * width + NOPE : (head + 1) * width]
    q1m = jnp.where(mine, q1, jnp.zeros_like(q1))
    q2m = jnp.where(mine, q2, jnp.zeros_like(q2))
    scores = dot(q_head, k_head, 1, 1) + dot(q1m, k1, 1, 1) + dot(q2m, k2, 1, 1)
    column = lax.broadcasted_iota(jnp.int32, scores.shape, 1)
    scores = jnp.where(column < limit, scores * scale, masked_score)
    top = jnp.max(scores, axis=-1, keepdims=True)
    expo = jnp.exp(scores - top)
    probs = expo / jnp.sum(expo, axis=-1, keepdims=True)
    return probs, q_head, k_head, v_head, q1m, q2m, mine


def attend_kernel(scale, lim_ref, qn_ref, q1_ref, q2_ref, lat_ref, k1_ref, k2_ref, kvb_ref, out_ref):
    kv = dot(lat_ref[0], kvb_ref[...], 1, 0).astype(bf16)
    for head in range(HEAD_GROUP):
        probs, _, _, v_head, _, _, _ = head_scores(
            qn_ref[0], q1_ref[0], q2_ref[0], kv, k1_ref[0], k2_ref[0], lim_ref[0], scale, head
        )
        out_ref[0, :, head * VDIM : (head + 1) * VDIM] = dot(
            probs.astype(bf16), v_head, 1, 0
        ).astype(bf16)


def attend_back_kernel(
    scale,
    lim_ref,
    qn_ref,
    q1_ref,
    q2_ref,
    lat_ref,
    k1_ref,
    k2_ref,
    kvb_ref,
    do_ref,
    dqn_ref,
    dq1_ref,
    dq2_ref,
    dlat_ref,
    dk1_ref,
    dk2_ref,
    dkvb_ref,
    kvg_ref,
    acc_ref,
):
    group, micro = pl.program_id(0), pl.program_id(1)
    width = NOPE + VDIM

    @pl.when(group == 0)
    def _():
        dlat_ref[micro] = jnp.zeros(dlat_ref.shape[1:], f32)
        dk1_ref[micro] = jnp.zeros(dk1_ref.shape[1:], f32)
        dk2_ref[micro] = jnp.zeros(dk2_ref.shape[1:], f32)

    lat = lat_ref[0]
    kvb = kvb_ref[...]
    kv = dot(lat, kvb, 1, 0).astype(bf16)
    k1, k2 = k1_ref[0], k2_ref[0]
    dq1 = jnp.zeros(dq1_ref.shape[1:], f32)
    dq2 = jnp.zeros(dq2_ref.shape[1:], f32)
    dk1 = jnp.zeros(k1.shape, f32)
    dk2 = jnp.zeros(k2.shape, f32)
    for head in range(HEAD_GROUP):
        probs, q_head, k_head, v_head, q1m, q2m, mine = head_scores(
            qn_ref[0], q1_ref[0], q2_ref[0], kv, k1, k2, lim_ref[0], scale, head
        )
        d_out = do_ref[0, :, head * VDIM : (head + 1) * VDIM]
        dprobs = dot(d_out, v_head, 1, 1)
        delta = jnp.sum(probs * dprobs, axis=-1, keepdims=True)
        ds = (probs * (dprobs - delta)).astype(bf16)
        dqn_ref[0, :, head * NOPE : (head + 1) * NOPE] = (dot(ds, k_head, 1, 0) * scale).astype(bf16)
        dq1 = dq1 + jnp.where(mine, dot(ds, k1, 1, 0), 0.0)
        dq2 = dq2 + jnp.where(mine, dot(ds, k2, 1, 0), 0.0)
        dk1 = dk1 + dot(ds, q1m, 0, 0)
        dk2 = dk2 + dot(ds, q2m, 0, 0)
        kvg_ref[:, head * width : head * width + NOPE] = (dot(ds, q_head, 0, 0) * scale).astype(bf16)
        kvg_ref[:, head * width + NOPE : (head + 1) * width] = dot(
            probs.astype(bf16), d_out, 0, 0
        ).astype(bf16)
    dq1_ref[0] = dq1 * scale
    dq2_ref[0] = dq2 * scale
    dk1_ref[micro] += dk1 * scale
    dk2_ref[micro] += dk2 * scale
    kvg = kvg_ref[...]
    dlat_ref[micro] += dot(kvg, kvb, 1, 1)
    part = dot(lat, kvg, 0, 0)

    @pl.when(micro == 0)
    def _():
        acc_ref[...] = part

    @pl.when(micro > 0)
    def _():
        acc_ref[...] += part

    @pl.when(micro == pl.num_programs(1) - 1)
    def _():
        dkvb_ref[...] = acc_ref[...].astype(bf16)


def attention_specs(micros, rows, length):
    groups = HEADS // HEAD_GROUP
    wide = HEAD_GROUP * NOPE
    specs = [
        pl.BlockSpec(memory_space=pltpu.SMEM),
        pl.BlockSpec((1, rows, wide), lambda g, m: (m, 0, g)),
        pl.BlockSpec((1, rows, GROUP_LANES), lambda g, m: (m, 0, g)),
        pl.BlockSpec((1, rows, GROUP_LANES), lambda g, m: (m, 0, g)),
        pl.BlockSpec((1, length, RANK), lambda g, m: (m, 0, 0)),
        pl.BlockSpec((1, length, GROUP_LANES), lambda g, m: (m, 0, 0)),
        pl.BlockSpec((1, length, GROUP_LANES), lambda g, m: (m, 0, 0)),
        pl.BlockSpec((RANK, HEAD_GROUP * (NOPE + VDIM)), lambda g, m: (0, g)),
    ]
    return (groups, micros), specs, pl.BlockSpec((1, rows, wide), lambda g, m: (m, 0, g))


def attend(limit, qn, q1, q2, lat, k1, k2, kvb, scale):
    micros, rows, _ = qn.shape
    length = lat.shape[1]
    grid, specs, out_spec = attention_specs(micros, rows, length)
    return pl.pallas_call(
        functools.partial(attend_kernel, scale),
        grid=grid,
        in_specs=specs,
        out_specs=out_spec,
        out_shape=jax.ShapeDtypeStruct(qn.shape, bf16),
        compiler_params=pltpu.CompilerParams(vmem_limit_bytes=48 << 20),
        name="attend",
    )(limit, qn, q1, q2, lat, k1, k2, kvb)


def attend_back(limit, qn, q1, q2, lat, k1, k2, kvb, d_out, scale):
    micros, rows, _ = qn.shape
    length = lat.shape[1]
    grid, specs, out_spec = attention_specs(micros, rows, length)
    whole = lambda g, m: (0, 0, 0)
    return pl.pallas_call(
        functools.partial(attend_back_kernel, scale),
        grid=grid,
        in_specs=specs + [out_spec],
        out_specs=[
            out_spec,
            pl.BlockSpec((1, rows, GROUP_LANES), lambda g, m: (m, 0, g)),
            pl.BlockSpec((1, rows, GROUP_LANES), lambda g, m: (m, 0, g)),
            pl.BlockSpec(lat.shape, whole),
            pl.BlockSpec(k1.shape, whole),
            pl.BlockSpec(k2.shape, whole),
            pl.BlockSpec((RANK, HEAD_GROUP * (NOPE + VDIM)), lambda g, m: (0, g)),
        ],
        out_shape=[
            jax.ShapeDtypeStruct(qn.shape, bf16),
            jax.ShapeDtypeStruct(q1.shape, f32),
            jax.ShapeDtypeStruct(q2.shape, f32),
            jax.ShapeDtypeStruct(lat.shape, f32),
            jax.ShapeDtypeStruct(k1.shape, f32),
            jax.ShapeDtypeStruct(k2.shape, f32),
            jax.ShapeDtypeStruct(kvb.shape, bf16),
        ],
        scratch_shapes=[
            pltpu.VMEM((length, HEAD_GROUP * (NOPE + VDIM)), bf16),
            pltpu.VMEM((RANK, HEAD_GROUP * (NOPE + VDIM)), f32),
        ],
        compiler_params=pltpu.CompilerParams(vmem_limit_bytes=48 << 20),
        name="attend_back",
    )(limit, qn, q1, q2, lat, k1, k2, kvb, d_out)


class Place:
    def __init__(self):
        self.r = lax.axis_index("rep")
        self.z = lax.axis_index("shard")
        self.core = self.r % 2
        self.chip = self.r // 2
        self.x = self.chip % 2
        self.y = self.chip // 2
        self.peer = (self.r + 1 - 2 * self.core, self.z)
        self.across = {
            "x": (self.r + 2 - 4 * self.x, self.z),
            "y": (self.r + 4 - 8 * self.y, self.z),
        }
        cx = self.chip + 1 - 2 * self.x
        cy = self.chip + 2 - 4 * self.y
        self.chips = {"": self.chip, "x": cx, "y": cy, "xy": cx + 2 - 4 * self.y}

    def along(self, step):
        return (self.r, (self.z + step) % 4)

    def shard_at(self, step):
        return (self.z + step) % 4


class Sems:
    def __init__(self, send, recv):
        self.send, self.recv = send, recv
        self.count = 0
        self.pending = []

    def slot(self):
        self.count += 1
        return self.count - 1

    def copy(self, src, dst, slot, device):
        return pltpu.make_async_remote_copy(
            src_ref=src,
            dst_ref=dst,
            send_sem=self.send.at[slot],
            recv_sem=self.recv.at[slot],
            device_id=device,
            device_id_type=MESH,
        )

    def push(self, src, dst, slot, device):
        copy = self.copy(src, dst, slot, device)
        copy.start()
        self.pending.append(copy)

    def arrived(self, dst, slot, device):
        self.copy(dst, dst, slot, device).wait_recv()

    def drain(self):
        for copy in self.pending:
            copy.wait_send()
        self.pending = []


def greet(devices):
    barrier = pltpu.get_barrier_semaphore()
    for device in devices:
        pl.semaphore_signal(barrier, inc=1, device_id=device, device_id_type=MESH)
    pl.semaphore_wait(barrier, len(devices))


def lanes(start, size):
    return pl.ds(pl.multiple_of(start, 128), size)


def rows16(start, size):
    return pl.ds(pl.multiple_of(start, 16), size)


class PlaneGather:
    def __init__(self, sems, place, part, half, by):
        self.sems, self.place, self.part, self.half, self.by = sems, place, part, half, by
        self.slots = {k: sems.slot() for k in ("x", "y", "xy", "core")}

    def first(self, src=None):
        p = self.place
        mine = self.part(p.core, p.chip)
        for axis in ("x", "y"):
            self.sems.push(mine if src is None else src, mine, self.slots[axis], p.across[axis])

    def second(self):
        p = self.place
        for axis in ("x", "y"):
            got = self.part(p.core, p.chips[axis])
            self.sems.arrived(got, self.slots[axis], p.across[axis])
        via = self.by
        other = "y" if via == "x" else "x"
        got = self.part(p.core, p.chips[via])
        self.sems.push(got, got, self.slots["xy"], p.across[other])

    def third(self):
        p = self.place
        got = self.part(p.core, p.chips["xy"])
        self.sems.arrived(got, self.slots["xy"], p.across["y" if self.by == "x" else "x"])
        half = self.half(p.core)
        self.sems.push(half, half, self.slots["core"], p.peer)

    def fourth(self):
        p = self.place
        self.sems.arrived(self.half(1 - p.core), self.slots["core"], p.peer)


def weight_regions(place, refs, shard):
    q, kr, kvb, out, sh = refs
    ds = q.shape[1] // 4
    cols = lanes(shard * ds, ds)

    def row_split(ref, n):
        half = ref.shape[0] // 2
        return (
            lambda core, chip: ref.at[rows16(core * half + chip * n, n), cols],
            lambda core: ref.at[rows16(core * half, half), cols],
        )

    def col_split(ref, full):
        rows = full // 4
        half = ref.shape[-1] // 2
        n = half // 4
        lead = (slice(None),) * (len(ref.shape) - 2)
        span = rows16(shard * rows, rows)
        return (
            lambda core, chip: ref.at[(*lead, span, lanes(core * half + chip * n, n))],
            lambda core: ref.at[(*lead, span, lanes(core * half, half))],
        )

    return [
        row_split(q, q.shape[0] // 8),
        row_split(kr, kr.shape[0] // 8),
        col_split(kvb, kvb.shape[0]),
        col_split(out, out.shape[0]),
        col_split(sh, sh.shape[1]),
    ]


def own_part(refs, place):
    q, kr, kvb, out, sh = refs
    res = []
    for ref in (q, kr):
        n = ref.shape[0] // 8
        res.append(ref.at[rows16(place.core * 4 * n + place.chip * n, n)])
    for ref in (kvb, out, sh):
        n = ref.shape[-1] // 8
        lead = (slice(None),) * (len(ref.shape) - 1)
        res.append(ref.at[(*lead, lanes(place.core * 4 * n + place.chip * n, n))])
    return res


ITEMS = 5
GATHER_SEMS = 1 + 3 + ITEMS * (3 + 3 * 4)


def gather_kernel(*refs):
    ins, gain = refs[:ITEMS], refs[ITEMS]
    outs, gains = refs[ITEMS + 1 : 2 * ITEMS + 1], refs[2 * ITEMS + 1]
    send, recv, local = refs[2 * ITEMS + 2 :]
    place = Place()
    sems = Sems(send, recv)
    greet([place.peer, place.across["x"], place.across["y"]] + [place.along(k) for k in (1, 2, 3)])
    mine = own_part(ins, place)
    ds = ins[0].shape[1]
    own = [
        outs[0].at[:, lanes(place.z * ds, ds)],
        outs[1].at[:, lanes(place.z * ds, ds)],
        outs[2].at[rows16(place.z * ins[2].shape[0], ins[2].shape[0])],
        outs[3].at[rows16(place.z * ins[3].shape[0], ins[3].shape[0])],
        outs[4].at[:, rows16(place.z * ins[4].shape[1], ins[4].shape[1])],
    ]
    kept = [pltpu.make_async_copy(ins[i], own[i], local.at[i]) for i in range(ITEMS)]
    kept.append(pltpu.make_async_copy(gain, gains.at[place.z], local.at[ITEMS]))
    zslots = [[sems.slot() for _ in range(3)] for _ in range(ITEMS + 1)]
    here = weight_regions(place, outs, place.z)
    for k in (1, 2, 3):
        sems.push(gain, gains.at[place.z], zslots[ITEMS][k - 1], place.along(k))
    for i in range(ITEMS):
        for k in (1, 2, 3):
            sems.push(mine[i], here[i][0](place.core, place.chip), zslots[i][k - 1], place.along(k))
    for copy in kept:
        copy.start()
    units = []
    flips = [["x", "y", "x"], ["x", "y", "y"], ["x", "y", "y"], ["x", "y", "x"], ["x", "y", "y"]]
    for i in range(ITEMS):
        for k in (1, 2, 3):
            shard = place.shard_at(4 - k)
            part, half = weight_regions(place, outs, shard)[i]
            units.append((i, k, part, PlaneGather(sems, place, part, half, flips[i][k - 1])))
    n = len(units)
    for step in range(n + 6):
        if step < n:
            i, k, part, g = units[step]
            sems.arrived(part(place.core, place.chip), zslots[i][k - 1], place.along(4 - k))
            g.first()
        if 0 <= step - 2 < n:
            units[step - 2][3].second()
        if 0 <= step - 4 < n:
            units[step - 4][3].third()
        if 0 <= step - 6 < n:
            units[step - 6][3].fourth()
    for k in (1, 2, 3):
        sems.arrived(gains.at[place.shard_at(4 - k)], zslots[ITEMS][k - 1], place.along(4 - k))
    sems.drain()
    for copy in kept:
        copy.wait()


def gather_weights(q, kr, kvb, out, sh, gain, fast):
    if not fast:
        every = lambda w, axis: lax.all_gather(w, "shard", axis=axis, tiled=True)
        return (
            every(q, 1),
            every(kr, 1),
            every(kvb, 0),
            every(out, 0),
            every(sh, 1),
            lax.all_gather(gain, "shard", axis=0),
        )
    shape = jax.ShapeDtypeStruct
    return pl.pallas_call(
        gather_kernel,
        in_specs=[pl.BlockSpec(memory_space=HBM)] * 6,
        out_specs=[pl.BlockSpec(memory_space=HBM)] * 6,
        out_shape=[
            shape((q.shape[0], q.shape[1] * 4), bf16),
            shape((kr.shape[0], kr.shape[1] * 4), bf16),
            shape((kvb.shape[0] * 4, kvb.shape[1]), bf16),
            shape((out.shape[0] * 4, out.shape[1]), bf16),
            shape((3, sh.shape[1] * 4, sh.shape[2]), bf16),
            shape((4,) + gain.shape, bf16),
        ],
        scratch_shapes=[
            pltpu.SemaphoreType.DMA((GATHER_SEMS + 32,)),
            pltpu.SemaphoreType.DMA((GATHER_SEMS + 32,)),
            pltpu.SemaphoreType.DMA((ITEMS + 1,)),
        ],
        compiler_params=pltpu.CompilerParams(collective_id=0, has_side_effects=True),
        name="gather_weights",
    )(q, kr, kvb, out, sh, gain)


def z_gather_kernel(count, *refs):
    ins, outs = refs[:count], refs[count : 2 * count]
    send, recv, local = refs[2 * count :]
    place = Place()
    sems = Sems(send, recv)
    greet([place.along(k) for k in (1, 2, 3)])

    def block(i, shard):
        rows = ins[i].shape[1]
        return outs[i].at[:, rows16(shard * rows, rows)]

    kept = [pltpu.make_async_copy(ins[i], block(i, place.z), local.at[i]) for i in range(count)]
    slots = [[sems.slot() for _ in range(3)] for _ in range(count)]
    for i in range(count):
        for k in (1, 2, 3):
            sems.push(ins[i], block(i, place.z), slots[i][k - 1], place.along(k))
        kept[i].start()
    for i in range(count):
        for k in (1, 2, 3):
            sems.arrived(block(i, place.shard_at(4 - k)), slots[i][k - 1], place.along(4 - k))
        kept[i].wait()
    sems.drain()


def z_gather(arrays, fast, ident):
    if not fast:
        return [lax.all_gather(a, "shard", axis=1, tiled=True) for a in arrays]
    count = len(arrays)
    return pl.pallas_call(
        functools.partial(z_gather_kernel, count),
        in_specs=[pl.BlockSpec(memory_space=HBM)] * count,
        out_specs=[pl.BlockSpec(memory_space=HBM)] * count,
        out_shape=[
            jax.ShapeDtypeStruct((a.shape[0], a.shape[1] * 4, a.shape[2]), a.dtype) for a in arrays
        ],
        scratch_shapes=[
            pltpu.SemaphoreType.DMA((3 * count,)),
            pltpu.SemaphoreType.DMA((3 * count,)),
            pltpu.SemaphoreType.DMA((count,)),
        ],
        compiler_params=pltpu.CompilerParams(collective_id=ident, has_side_effects=True),
        name="z_gather",
    )(*arrays)


def z_scatter_kernel(count, *refs):
    ins, outs = refs[:count], refs[count : 2 * count]
    send, recv, local = refs[2 * count :]
    place = Place()
    sems = Sems(send, recv)
    greet([place.along(k) for k in (1, 2, 3)])

    def block(i, shard):
        rows = ins[i].shape[1] // 4
        return ins[i].at[:, rows16(shard * rows, rows)]

    kept = [
        pltpu.make_async_copy(block(i, place.z), outs[i].at[0], local.at[i]) for i in range(count)
    ]
    slots = [[sems.slot() for _ in range(3)] for _ in range(count)]
    for i in range(count):
        for k in (1, 2, 3):
            sems.push(block(i, place.shard_at(k)), outs[i].at[k], slots[i][k - 1], place.along(k))
        kept[i].start()
    for i in range(count):
        for k in (1, 2, 3):
            sems.arrived(outs[i].at[k], slots[i][k - 1], place.along(4 - k))
        kept[i].wait()
    sems.drain()


def z_scatter(arrays, fast, ident):
    if not fast:
        return [
            lax.psum_scatter(a.astype(f32), "shard", scatter_dimension=1, tiled=True)
            for a in arrays
        ]
    count = len(arrays)
    parts = pl.pallas_call(
        functools.partial(z_scatter_kernel, count),
        in_specs=[pl.BlockSpec(memory_space=HBM)] * count,
        out_specs=[pl.BlockSpec(memory_space=HBM)] * count,
        out_shape=[
            jax.ShapeDtypeStruct((4, a.shape[0], a.shape[1] // 4, a.shape[2]), a.dtype)
            for a in arrays
        ],
        scratch_shapes=[
            pltpu.SemaphoreType.DMA((3 * count,)),
            pltpu.SemaphoreType.DMA((3 * count,)),
            pltpu.SemaphoreType.DMA((count,)),
        ],
        compiler_params=pltpu.CompilerParams(collective_id=ident, has_side_effects=True),
        name="z_scatter",
    )(*arrays)
    return [jnp.sum(p.astype(f32), axis=0) for p in parts]


def swap_kernel(count, *refs):
    ins, outs = refs[:count], refs[count : 2 * count]
    send, recv, local = refs[2 * count :]
    place = Place()
    sems = Sems(send, recv)
    greet([place.peer])
    for i in range(count):
        sems.push(ins[i].at[1 - place.core], outs[i].at[1], sems.slot(), place.peer)
    kept = [
        pltpu.make_async_copy(ins[i].at[place.core], outs[i].at[0], local.at[i])
        for i in range(count)
    ]
    for copy in kept:
        copy.start()
    for i in range(count):
        sems.arrived(outs[i].at[1], i, place.peer)
    sems.drain()
    for copy in kept:
        copy.wait()


def core_swap(arrays, fast, ident):
    count = len(arrays)
    if not fast:
        reps = lax.axis_size("rep")
        core = lax.axis_index("rep") % 2
        res = []
        for a in arrays:
            keep = lax.dynamic_index_in_dim(a, core, 0, keepdims=False)
            give = lax.dynamic_index_in_dim(a, 1 - core, 0, keepdims=False)
            got = lax.ppermute(give, "rep", [(i, i ^ 1) for i in range(reps)])
            res.append(jnp.stack([keep, got]))
        return res
    return pl.pallas_call(
        functools.partial(swap_kernel, count),
        in_specs=[pl.BlockSpec(memory_space=HBM)] * count,
        out_specs=[pl.BlockSpec(memory_space=HBM)] * count,
        out_shape=[jax.ShapeDtypeStruct(a.shape, a.dtype) for a in arrays],
        scratch_shapes=[
            pltpu.SemaphoreType.DMA((count,)),
            pltpu.SemaphoreType.DMA((count,)),
            pltpu.SemaphoreType.DMA((count,)),
        ],
        compiler_params=pltpu.CompilerParams(collective_id=ident, has_side_effects=True),
        name="core_swap",
    )(*arrays)


def add_rows(dst, terms, rows):
    lead = dst.shape[:-2]
    steps = dst.shape[-2] // rows

    def body(step, carry):
        span = pl.ds(pl.multiple_of(step * rows, rows), rows)
        where = (slice(None),) * len(lead) + (span,)
        total = terms[0][where].astype(f32)
        for t in terms[1:]:
            total = total + t[where].astype(f32)
        dst[where] = total.astype(dst.dtype)
        return carry

    lax.fori_loop(0, steps, body, 0)


RS_ITEMS = 6
LOOK = 3


def reduce_kernel(*refs):
    grads, gain = refs[:RS_ITEMS], refs[RS_ITEMS]
    outs, gain_out = refs[RS_ITEMS + 1 : 2 * RS_ITEMS + 1], refs[2 * RS_ITEMS + 1]
    rest = refs[2 * RS_ITEMS + 2 :]
    own, got1, got2, got3 = (rest[i * RS_ITEMS : (i + 1) * RS_ITEMS] for i in range(4))
    gz, gp, gs, send, recv, load, keep = rest[4 * RS_ITEMS :]
    place = Place()
    sems = Sems(send, recv)
    others = [(place.chip * 2 + 1 - place.core, place.z)]
    for axes in ("x", "y", "xy"):
        for core in (0, 1):
            flip = place.core if core == 0 else 1 - place.core
            others.append((place.chips[axes] * 2 + flip, place.z))
    greet(others + [place.along(k) for k in (1, 2, 3)])

    def grad_part(i, s, chip):
        g = grads[i]
        if i < 2:
            n, ds = g.shape[0] // 4, g.shape[1] // 4
            return g.at[rows16(chip * n, n), lanes(s * ds, ds)]
        n = g.shape[-1] // 4
        if i == 5:
            return g.at[s, :, lanes(chip * n, n)]
        rows = g.shape[-2] // 4
        lead = (slice(None),) * (len(g.shape) - 2)
        return g.at[(*lead, rows16(s * rows, rows), lanes(chip * n, n))]

    def out_split(i):
        o = outs[i]
        if i < 2:
            half = o.shape[0] // 2
            n = half // 4
            return (
                lambda core, chip: o.at[rows16(core * half + chip * n, n)],
                lambda core: o.at[rows16(core * half, half)],
            )
        half = o.shape[-1] // 2
        n = half // 4
        lead = (slice(None),) * (len(o.shape) - 1)
        return (
            lambda core, chip: o.at[(*lead, lanes(core * half + chip * n, n))],
            lambda core: o.at[(*lead, lanes(core * half, half))],
        )

    gain_slots = [sems.slot() for _ in range(3 + 7)]
    for k in (1, 2, 3):
        sems.push(gain.at[place.shard_at(k)], gz.at[k], gain_slots[k - 1], place.along(k))
    first_gain = pltpu.make_async_copy(gain.at[place.z], gz.at[0], keep.at[RS_ITEMS])
    first_gain.start()

    order = [4, 5, 3, 2, 1, 0]
    units = []
    loads = 0
    for i in order:
        if i == 5:
            steps = [(u, u, None) for u in range(6)]
        else:
            steps = [(k % 4, place.shard_at(k), k % 4) for k in (1, 2, 3, 4)]
        for n, (u, s, k) in enumerate(steps):
            axis = "x" if (n + i) % 2 == 0 else "y"
            units.append(
                dict(
                    i=i,
                    u=u,
                    s=s,
                    k=k,
                    last=n == len(steps) - 1,
                    axis=axis,
                    other="y" if axis == "x" else "x",
                    slots=[sems.slot() for _ in range(4)],
                    loads=[loads, loads + 1],
                )
            )
            loads += 2
    for unit in units:
        i, u = unit["i"], unit["u"]
        unit["copies"] = [
            pltpu.make_async_copy(
                grad_part(i, unit["s"], place.chips["" if n == 0 else unit["other"]]),
                own[i].at[u, n],
                load.at[unit["loads"][n]],
            )
            for n in (0, 1)
        ]
        for copy in unit["copies"]:
            copy.start()

    def stage1(unit):
        i, u, axis = unit["i"], unit["u"], unit["axis"]
        for n, chip in enumerate((axis, "xy")):
            sems.push(
                grad_part(i, unit["s"], place.chips[chip]),
                got1[i].at[u, n],
                unit["slots"][n],
                place.across[axis],
            )

    def stage2(unit):
        i, u, axis, other = unit["i"], unit["u"], unit["axis"], unit["other"]
        for copy in unit["copies"]:
            copy.wait()
        for n in (1, 0):
            sems.arrived(got1[i].at[u, n], unit["slots"][n], place.across[axis])
            add_rows(own[i].at[u, n], [own[i].at[u, n], got1[i].at[u, n]], 16)
            if n == 1:
                sems.push(own[i].at[u, 1], got2[i].at[u], unit["slots"][2], place.across[other])

    def stage3(unit):
        i, u = unit["i"], unit["u"]
        sems.arrived(got2[i].at[u], unit["slots"][2], place.across[unit["other"]])
        add_rows(own[i].at[u, 0], [own[i].at[u, 0], got2[i].at[u]], 16)
        if unit["k"]:
            sems.push(
                own[i].at[u, 0],
                got3[i].at[unit["k"] - 1],
                unit["slots"][3],
                place.along(unit["k"]),
            )

    gathers = []

    def stage4(unit):
        i = unit["i"]
        if not unit["last"]:
            return
        part, half = out_split(i)
        mine = part(place.core, place.chip)
        if i == 5:
            src = own[i].at[:, 0]
        else:
            for other in units:
                if other["i"] == i and other["k"]:
                    k = other["k"]
                    sems.arrived(got3[i].at[k - 1], other["slots"][3], place.along(4 - k))
            src = own[i].at[0, 0]
            add_rows(src, [src] + [got3[i].at[n] for n in range(3)], 16)
        stay = pltpu.make_async_copy(src, mine, keep.at[i])
        stay.start()
        g = PlaneGather(sems, place, part, half, "x" if i % 2 == 0 else "y")
        g.first(src)
        gathers.append((g, stay))

    n = len(units)
    done = 0
    for step in range(n + 3 * LOOK):
        if step < n:
            stage1(units[step])
        if 0 <= step - LOOK < n:
            stage2(units[step - LOOK])
        if 0 <= step - 2 * LOOK < n:
            stage3(units[step - 2 * LOOK])
        if 0 <= step - 3 * LOOK < n:
            stage4(units[step - 3 * LOOK])
    first_gain.wait()
    for k in (1, 2, 3):
        sems.arrived(gz.at[k], gain_slots[k - 1], place.along(4 - k))
    gs[...] = gz[0] + gz[1] + gz[2] + gz[3]
    for n, device in enumerate(others):
        sems.push(gs, gp.at[n], gain_slots[3 + n], device)
    for g, stay in gathers:
        g.second()
    for g, stay in gathers:
        stay.wait()
        g.third()
    for g, stay in gathers:
        g.fourth()
    total = gs[...]
    for n, device in enumerate(others):
        sems.arrived(gp.at[n], gain_slots[3 + n], device)
        total = total + gp[n]
    gain_out[...] = total
    sems.drain()


def reduce_grads(grads, gain, fast):
    if not fast:
        core = lax.axis_index("rep") % 2

        def whole(g, axis):
            wide = jnp.zeros(g.shape[:axis] + (g.shape[axis] * 2,) + g.shape[axis + 1 :], f32)
            return lax.dynamic_update_slice_in_dim(
                wide, g.astype(f32), core * g.shape[axis], axis
            )

        q, kr, kvb, out, sh, ex = grads

        def total(g, axis, along):
            g = lax.psum_scatter(whole(g, axis), "shard", scatter_dimension=along, tiled=True)
            return lax.psum(g, "rep")

        return (
            total(q, 0, 1),
            total(kr, 0, 1),
            total(kvb, 1, 0),
            total(out, 1, 0),
            total(sh, 2, 1),
            lax.psum(whole(ex, 2), "rep"),
            lax.psum(lax.psum_scatter(gain, "shard", scatter_dimension=0, tiled=True), "rep")[0],
        )
    q, kr, kvb, out, sh, ex = grads
    shape = jax.ShapeDtypeStruct
    parts = [
        (q.shape[0] // 4, q.shape[1] // 4),
        (kr.shape[0] // 4, kr.shape[1] // 4),
        (kvb.shape[0] // 4, kvb.shape[1] // 4),
        (out.shape[0] // 4, out.shape[1] // 4),
        (3, sh.shape[1] // 4, sh.shape[2] // 4),
        (ex.shape[1], ex.shape[2] // 4),
    ]
    counts = [4] * 5 + [6]
    scratch = [pltpu.VMEM((n, 2) + p, bf16) for n, p in zip(counts, parts)]
    scratch += [pltpu.VMEM((n, 2) + p, bf16) for n, p in zip(counts, parts)]
    scratch += [pltpu.VMEM((n,) + p, bf16) for n, p in zip(counts, parts)]
    scratch += [pltpu.VMEM((3,) + (p if i < 5 else (16, 128)), bf16) for i, p in enumerate(parts)]
    slots = 10 + 26 * 4 + RS_ITEMS * 4
    return pl.pallas_call(
        reduce_kernel,
        in_specs=[pl.BlockSpec(memory_space=HBM)] * 7,
        out_specs=[pl.BlockSpec(memory_space=HBM)] * 6 + [pl.BlockSpec(memory_space=pltpu.VMEM)],
        out_shape=[
            shape((q.shape[0] * 2, q.shape[1] // 4), bf16),
            shape((kr.shape[0] * 2, kr.shape[1] // 4), bf16),
            shape((kvb.shape[0] // 4, kvb.shape[1] * 2), bf16),
            shape((out.shape[0] // 4, out.shape[1] * 2), bf16),
            shape((3, sh.shape[1] // 4, sh.shape[2] * 2), bf16),
            shape((6, ex.shape[1], ex.shape[2] * 2), bf16),
            shape(gain.shape[1:], f32),
        ],
        scratch_shapes=scratch
        + [
            pltpu.VMEM((4,) + gain.shape[1:], f32),
            pltpu.VMEM((7,) + gain.shape[1:], f32),
            pltpu.VMEM(gain.shape[1:], f32),
            pltpu.SemaphoreType.DMA((slots,)),
            pltpu.SemaphoreType.DMA((slots,)),
            pltpu.SemaphoreType.DMA((52,)),
            pltpu.SemaphoreType.DMA((RS_ITEMS + 1,)),
        ],
        compiler_params=pltpu.CompilerParams(
            collective_id=1, has_side_effects=True, vmem_limit_bytes=56 << 20
        ),
        name="reduce_grads",
    )(q, kr, kvb, out, sh, ex, gain)


def head_split(weight):
    per_head = weight.reshape(HEADS, NOPE + ROPE, weight.shape[1])
    cuts = (0, NOPE, NOPE + HALF_ROPE, NOPE + ROPE)
    return jnp.concatenate(
        [per_head[:, a:b].reshape(-1, weight.shape[1]) for a, b in zip(cuts[:-1], cuts[1:])]
    )


def head_join(weight):
    cols = weight.shape[1]
    nope = weight[: HEADS * NOPE].reshape(HEADS, NOPE, cols)
    first = weight[HEADS * NOPE : HEADS * (NOPE + HALF_ROPE)].reshape(HEADS, HALF_ROPE, cols)
    second = weight[HEADS * (NOPE + HALF_ROPE) :].reshape(HEADS, HALF_ROPE, cols)
    return jnp.concatenate([nope, first, second], axis=1).reshape(-1, cols)


def halves(tensor, axis):
    size = tensor.shape[axis] // 2
    return jnp.stack(
        [
            lax.slice_in_dim(tensor, 0, size, axis=axis),
            lax.slice_in_dim(tensor, size, 2 * size, axis=axis),
        ]
    )


def shards(
    tokens,
    attn_gain,
    q_weight,
    kva_weight,
    kv_gain,
    kvb_weight,
    out_weight,
    ffn_gain,
    router_weight,
    shared_gate,
    shared_up,
    shared_down,
    expert_gate,
    expert_up,
    expert_down,
    expert_ids,
    cotangent,
):
    shard_count = lax.axis_size("shard")
    shard_index = lax.axis_index("shard")
    core = lax.axis_index("rep") % 2
    fast = lax.axis_size("rep") == 8 and shard_count == 4
    micros, rows, width = tokens.shape
    toks = micros * rows
    scale = (NOPE + ROPE) ** (-0.5)
    ga, gk = attn_gain.shape[0], kv_gain.shape[0]

    gain_pack = jnp.concatenate([attn_gain, ffn_gain, kv_gain]).astype(bf16)
    gain_pack = jnp.broadcast_to(gain_pack[None], (16, gain_pack.shape[0]))
    query_mat, kr_mat, kvb_mat, out_mat, sh_mat, gains = gather_weights(
        head_split(q_weight).astype(bf16),
        jnp.concatenate([kva_weight, router_weight]).astype(bf16),
        kvb_weight.astype(bf16),
        out_weight.astype(bf16),
        jnp.stack([shared_gate, shared_up, shared_down]).astype(bf16),
        gain_pack,
        fast,
    )
    gain_rows = gains[:, 0].astype(f32)
    attn_gain_f = gain_rows[:, :ga].reshape(-1)
    ffn_gain_f = gain_rows[:, ga : 2 * ga].reshape(-1)
    kv_gain_f = gain_rows[:, 2 * ga :].reshape(-1)
    kv_down_mat, router_mat = kr_mat[: RANK + ROPE], kr_mat[RANK + ROPE :]
    gate_mat, up_mat, down_mat = sh_mat[0], sh_mat[1], sh_mat[2]

    x_in = tokens.reshape(toks, width).astype(f32)
    inv_one = rms_scale(x_in)
    h_attn = (x_in * inv_one * attn_gain_f).astype(bf16)
    positions = (shard_index * rows + jnp.arange(rows, dtype=jnp.int32)).astype(f32)
    frequency = jnp.exp(
        -jnp.log(rope_base) * (2.0 * jnp.arange(HALF_ROPE, dtype=f32) / ROPE)
    )
    angles = positions[:, None] * frequency[None, :]
    cosine = jnp.tile(jnp.cos(angles), (micros, 1))
    sine = jnp.tile(jnp.sin(angles), (micros, 1))
    cos_all, sin_all = jnp.tile(cosine, (1, HEADS)), jnp.tile(sine, (1, HEADS))
    q_raw = dot(h_attn, query_mat, 1, 1)
    n1, n2 = HEADS * NOPE, HEADS * (NOPE + HALF_ROPE)
    q_first, q_second = q_raw[:, n1:n2], q_raw[:, n2:]
    by_micro = lambda t: t.reshape(micros, rows, t.shape[-1])
    qn = by_micro(q_raw[:, :n1].astype(bf16))
    q1 = by_micro((q_first * cos_all - q_second * sin_all).astype(bf16))
    q2 = by_micro((q_second * cos_all + q_first * sin_all).astype(bf16))
    kv_down = dot(h_attn, kv_down_mat, 1, 1)
    latent = kv_down[:, :RANK]
    inv_kv = rms_scale(latent)
    latent_norm = (latent * inv_kv * kv_gain_f).astype(bf16)
    k_first, k_second = kv_down[:, RANK : RANK + HALF_ROPE], kv_down[:, RANK + HALF_ROPE :]
    latent_pack = jnp.concatenate(
        [
            latent_norm,
            (k_first * cosine - k_second * sine).astype(bf16),
            (k_second * cosine + k_first * sine).astype(bf16),
            jnp.zeros((toks, ROPE), bf16),
        ],
        axis=-1,
    )
    (packs,) = z_gather([by_micro(latent_pack)], fast, 2)
    length = packs.shape[1]
    lat_all = packs[..., :RANK]
    k1 = jnp.tile(packs[..., RANK : RANK + HALF_ROPE], (1, 1, HEAD_GROUP))
    k2 = jnp.tile(packs[..., RANK + HALF_ROPE : RANK + ROPE], (1, 1, HEAD_GROUP))
    limit = ((shard_index * rows) // MASK_BLOCK + 1) * MASK_BLOCK
    limit = jnp.minimum(limit, length).astype(jnp.int32).reshape(1)
    attended = attend(limit, qn, q1, q2, lat_all, k1, k2, kvb_mat, scale).reshape(toks, -1)

    x_mid = x_in + dot(attended, out_mat, 1, 0)
    inv_two = rms_scale(x_mid)
    h_ffn = (x_mid * inv_two * ffn_gain_f).astype(bf16)
    router_probs = jax.nn.softmax(dot(h_ffn, router_mat, 1, 1), axis=-1)
    grad_b = cotangent.reshape(toks, width)

    member = jnp.any(
        expert_ids[:, :, None, :] == jnp.arange(EXP_WIN, dtype=jnp.int32)[None, None, :, None], axis=-1
    ).astype(jnp.int32)
    placed = jnp.cumsum(member, axis=1) - 1
    hits = (member[:, :, :, None] == 1) & (
        placed[:, :, :, None] == jnp.arange(CAP, dtype=jnp.int32)
    )
    select = jnp.transpose(hits, (2, 0, 3, 1)).astype(f32)
    select_b = select.astype(bf16)
    h3, c3 = by_micro(h_ffn), by_micro(grad_b)
    gather_slots = lambda t: jnp.einsum(
        "emct,mtd->emcd", select_b, t, preferred_element_type=f32
    )
    slot_rows = gather_slots(h3).astype(bf16)
    picked = gather_slots(c3)
    slot_gates = jnp.einsum(
        "emct,mte->emc", select, by_micro(router_probs)[..., :EXP_WIN], precision=highest
    )
    slot_dy = (slot_gates[..., None] * picked).astype(bf16)
    flat = lambda t: t.reshape(EXP_WIN, micros * CAP, width)
    rows_all, dy_all = z_gather([flat(slot_rows), flat(slot_dy)], fast, 3)
    eg, eu, ed = expert_gate.astype(bf16), expert_up.astype(bf16), expert_down.astype(bf16)
    bdot = lambda a, b, ca, cb: lax.dot_general(
        a, b, (((ca,), (cb,)), ((0,), (0,))), preferred_element_type=f32
    )
    expert_pre = bdot(rows_all, eg, 2, 2)
    expert_upv = bdot(rows_all, eu, 2, 2)
    expert_hidden = (jax.nn.silu(expert_pre) * expert_upv).astype(bf16)
    expert_part = bdot(expert_hidden, ed, 2, 1).astype(bf16)
    expert_hidden_grad = bdot(dy_all, ed, 2, 2)
    expert_gate_b, expert_up_b = swiglu_back(expert_pre, expert_upv, expert_hidden_grad)
    slot_part = (bdot(expert_gate_b, eg, 2, 1) + bdot(expert_up_b, eu, 2, 1)).astype(bf16)
    expert_out, slot_grad = z_scatter([expert_part, slot_part], fast, 4)
    back = lambda t: t.reshape(EXP_WIN, micros, CAP, width)
    expert_out, slot_grad = back(expert_out), back(slot_grad)

    gate_pre = dot(h_ffn, gate_mat, 1, 1)
    up_pre = dot(h_ffn, up_mat, 1, 1)
    shared_hidden = (jax.nn.silu(gate_pre) * up_pre).astype(bf16)
    shared_out = dot(shared_hidden, down_mat, 1, 0)
    routed = jnp.einsum("emct,emcd->mtd", select, slot_gates[..., None] * expert_out, precision=highest)
    layer_output = (x_mid + shared_out + routed.reshape(toks, width)).astype(bf16)

    shared_hidden_grad = dot(grad_b, down_mat, 1, 1)
    gate_grad_b, up_grad_b = swiglu_back(gate_pre, up_pre, shared_hidden_grad)
    ffn_grad = dot(gate_grad_b, gate_mat, 1, 0) + dot(up_grad_b, up_mat, 1, 0)
    gate_weight_grad = jnp.sum(picked * expert_out, axis=-1)
    ffn_grad = ffn_grad + jnp.einsum(
        "emct,emcd->mtd", select, slot_grad, precision=highest
    ).reshape(toks, width)
    probs_grad = jnp.einsum("emct,emc->mte", select, gate_weight_grad, precision=highest)
    probs_grad = jnp.pad(
        probs_grad.reshape(toks, EXP_WIN), ((0, 0), (0, EXPERTS - EXP_WIN))
    )
    logit_grad = (
        router_probs * (probs_grad - jnp.sum(router_probs * probs_grad, axis=-1, keepdims=True))
    ).astype(bf16)
    ffn_grad = ffn_grad + dot(logit_grad, router_mat, 1, 0)
    mid_part, ffn_gain_grad = norm_back(x_mid, inv_two, ffn_gain_f, ffn_grad)
    mid_grad = grad_b.astype(f32) + mid_part
    attn_out_grad = mid_grad.astype(bf16)
    attended_grad = by_micro(dot(attn_out_grad, out_mat, 1, 1).astype(bf16))

    dqn, dq1, dq2, dlat, dk1, dk2, dkvb = attend_back(
        limit, qn, q1, q2, lat_all, k1, k2, kvb_mat, attended_grad, scale
    )
    fold = lambda t: jnp.sum(t.reshape(micros, length, HEAD_GROUP, HALF_ROPE), axis=2)
    back_pack = jnp.concatenate(
        [dlat, fold(dk1), fold(dk2), jnp.zeros((micros, length, ROPE), f32)], axis=-1
    ).astype(bf16)
    (own_back,) = z_scatter([back_pack], fast, 5)
    own_back = own_back.reshape(toks, -1)
    latent_grad, kv_gain_grad = norm_back(latent, inv_kv, kv_gain_f, own_back[:, :RANK])
    g1, g2 = own_back[:, RANK : RANK + HALF_ROPE], own_back[:, RANK + HALF_ROPE : RANK + ROPE]
    kv_down_grad = jnp.concatenate(
        [latent_grad, g1 * cosine + g2 * sine, g2 * cosine - g1 * sine], axis=-1
    ).astype(bf16)
    dq1, dq2 = dq1.reshape(toks, -1), dq2.reshape(toks, -1)
    q_raw_grad = jnp.concatenate(
        [
            dqn.reshape(toks, -1),
            (dq1 * cos_all + dq2 * sin_all).astype(bf16),
            (dq2 * cos_all - dq1 * sin_all).astype(bf16),
        ],
        axis=-1,
    )
    attn_in_grad = dot(q_raw_grad, query_mat, 1, 0) + dot(kv_down_grad, kv_down_mat, 1, 0)
    x_part, attn_gain_grad = norm_back(x_in, inv_one, attn_gain_f, attn_in_grad)
    input_grad = (mid_grad + x_part).astype(bf16)

    both = lambda t: jnp.broadcast_to(t[None], (2,) + t.shape)
    kr_grad = jnp.concatenate(
        [dot(kv_down_grad, h_attn, 0, 0), dot(logit_grad, h_ffn, 0, 0)]
    ).astype(bf16)
    swapped = core_swap(
        [
            both(h_attn),
            halves(q_raw_grad, 1),
            halves(kr_grad, 0),
            halves(dkvb, 1),
            both(attended),
            halves(attn_out_grad, 1),
            both(jnp.concatenate([gate_grad_b, up_grad_b, shared_hidden], axis=1)),
            halves(h_ffn, 1),
            halves(grad_b, 1),
            both(jnp.concatenate([expert_gate_b, expert_up_b, expert_hidden], axis=-1).reshape(
                EXP_WIN * rows_all.shape[1], -1
            )),
            halves(rows_all.reshape(-1, width), 1),
            halves(dy_all.reshape(-1, width), 1),
        ],
        fast,
        6,
    )
    (h_s, qg_s, krg_s, kvbg_s, att_s, og_s, sh_s, hf_s, cot_s, ex_s, row_s, dy_s) = swapped
    tall = lambda t: t.reshape(-1, t.shape[-1])
    grad_q = dot(tall(qg_s), tall(h_s), 0, 0).astype(bf16)
    grad_kr = (krg_s[0].astype(f32) + krg_s[1].astype(f32)).astype(bf16)
    grad_kvb = (kvbg_s[0].astype(f32) + kvbg_s[1].astype(f32)).astype(bf16)
    grad_out = dot(tall(att_s), tall(og_s), 0, 0).astype(bf16)
    ff = shared_hidden.shape[1]
    sh_s = tall(sh_s)
    hf_s, cot_s = tall(hf_s), tall(cot_s)
    grad_sh = jnp.stack(
        [
            dot(sh_s[:, :ff], hf_s, 0, 0).astype(bf16),
            dot(sh_s[:, ff : 2 * ff], hf_s, 0, 0).astype(bf16),
            dot(sh_s[:, 2 * ff :], cot_s, 0, 0).astype(bf16),
        ]
    )
    fe = expert_hidden.shape[-1]
    by_expert = lambda t: t.reshape(2, EXP_WIN, -1, t.shape[-1])
    ex_s, row_s, dy_s = by_expert(ex_s), by_expert(row_s), by_expert(dy_s)
    edot = lambda a, b: jnp.einsum("senf,send->efd", a, b, preferred_element_type=f32).astype(bf16)
    grad_ex = jnp.concatenate(
        [
            edot(ex_s[..., :fe], row_s),
            edot(ex_s[..., fe : 2 * fe], row_s),
            edot(ex_s[..., 2 * fe :], dy_s),
        ]
    )
    lane_rows = lambda t: t.reshape(shard_count, -1)
    gain_grad = jnp.concatenate(
        [lane_rows(attn_gain_grad), lane_rows(ffn_gain_grad), lane_rows(kv_gain_grad)], axis=1
    )
    gain_len = gain_grad.shape[1]
    gain_grad = jnp.pad(gain_grad, ((0, 0), (0, 16 * 128 - gain_len))).reshape(-1, 16, 128)
    gq, gkr, gkvb, gout, gsh, gex, gg = reduce_grads(
        (grad_q, grad_kr, grad_kvb, grad_out, grad_sh, grad_ex), gain_grad, fast
    )
    gg = gg.reshape(-1)[:gain_len]
    gkr = gkr.astype(f32)
    gsh = gsh.astype(f32)
    gex = gex.astype(f32)
    return (
        by_micro(layer_output),
        by_micro(input_grad),
        gg[:ga],
        head_join(gq).astype(f32),
        gkr[: RANK + ROPE],
        gg[2 * ga :],
        gkvb.astype(f32),
        gout.astype(f32),
        gg[ga : 2 * ga],
        gkr[RANK + ROPE :],
        gsh[0],
        gsh[1],
        gsh[2],
        gex[:2],
        gex[2:4],
        gex[4:],
    )


def solution(mesh):
    token_spec = P(None, ("rep", "shard"), None)
    row_spec, col_spec, gain_spec = P("shard", None), P(None, "shard"), P("shard")
    expert_spec = P(None, "shard", None)
    weight_specs = (
        gain_spec,
        col_spec,
        col_spec,
        gain_spec,
        row_spec,
        row_spec,
        gain_spec,
        col_spec,
        row_spec,
        row_spec,
        row_spec,
        expert_spec,
        expert_spec,
        expert_spec,
    )
    return jax.shard_map(
        shards,
        mesh=mesh,
        in_specs=(token_spec,) + weight_specs + (token_spec, token_spec),
        out_specs=(token_spec, token_spec) + weight_specs,
        check_vma=False,
    )
```

```python
import functools

import jax
import jax.numpy as jnp
from jax import lax
from jax.experimental import pallas as pl
from jax.experimental.pallas import tpu as pltpu
from jax.sharding import PartitionSpec as P

HEADS = 16
NOPE = 128
ROPE = 64
VDIM = 128
RANK = 512
EXPERTS = 64
EXP_WIN = 2
MASK_BLOCK = 256
CAP = 16

epsilon = 1e-06
rope_base = 10000.0
masked_score = -1e30
highest = lax.Precision.HIGHEST
bf16 = jnp.bfloat16
f32 = jnp.float32
MESH = pl.DeviceIdType.MESH
HBM = pltpu.HBM
HALF_ROPE = ROPE // 2
HEAD_GROUP = 4
GROUP_LANES = HEAD_GROUP * HALF_ROPE


def dot(a, b, ca, cb):
    return lax.dot_general(a, b, (((ca,), (cb,)), ((), ())), preferred_element_type=f32)


def rms_scale(tensor):
    return lax.rsqrt(jnp.mean(tensor * tensor, axis=-1, keepdims=True) + epsilon)


def norm_back(tensor, inv_rms, gain_vec, gradient):
    scaled_grad = gradient * gain_vec
    inner_mean = jnp.mean(scaled_grad * tensor, axis=-1, keepdims=True)
    input_part = inv_rms * scaled_grad - tensor * (inv_rms * inv_rms * inv_rms) * inner_mean
    gain_part = jnp.sum(gradient * tensor * inv_rms, axis=0)
    return (input_part, gain_part)


def swiglu_back(gate_pre, up_pre, hidden_grad):
    sigmoid_gate = jax.nn.sigmoid(gate_pre)
    silu_gate = gate_pre * sigmoid_gate
    slope = sigmoid_gate * (1.0 + gate_pre * (1.0 - sigmoid_gate))
    return (
        (hidden_grad * up_pre * slope).astype(bf16),
        (hidden_grad * silu_gate).astype(bf16),
    )


def head_scores(qn, q1, q2, kv, k1, k2, seen, scale, head):
    lane = lax.broadcasted_iota(jnp.int32, (1, GROUP_LANES), 1)
    mine = (lane >= head * HALF_ROPE) & (lane < (head + 1) * HALF_ROPE)
    width = NOPE + VDIM
    q_head = qn[:, head * NOPE : (head + 1) * NOPE]
    k_head = kv[:, head * width : head * width + NOPE]
    v_head = kv[:, head * width + NOPE : (head + 1) * width]
    q1m = jnp.where(mine, q1, jnp.zeros_like(q1))
    q2m = jnp.where(mine, q2, jnp.zeros_like(q2))
    scores = dot(q_head, k_head, 1, 1) + dot(q1m, k1, 1, 1) + dot(q2m, k2, 1, 1)
    scores = jnp.where(seen > 0.0, scores * scale, masked_score)
    top = jnp.max(scores, axis=-1, keepdims=True)
    expo = jnp.exp(scores - top)
    probs = expo / jnp.sum(expo, axis=-1, keepdims=True)
    return probs, q_head, k_head, v_head, q1m, q2m, mine


def attend_kernel(scale, seen_ref, qn_ref, q1_ref, q2_ref, lat_ref, k1_ref, k2_ref, kvb_ref, out_ref):
    kv = dot(lat_ref[0], kvb_ref[...], 1, 0).astype(bf16)
    for head in range(HEAD_GROUP):
        probs, _, _, v_head, _, _, _ = head_scores(
            qn_ref[0], q1_ref[0], q2_ref[0], kv, k1_ref[0], k2_ref[0], seen_ref[...], scale, head
        )
        out_ref[0, :, head * VDIM : (head + 1) * VDIM] = dot(
            probs.astype(bf16), v_head, 1, 0
        ).astype(bf16)


def attend_back_kernel(
    scale,
    seen_ref,
    qn_ref,
    q1_ref,
    q2_ref,
    lat_ref,
    k1_ref,
    k2_ref,
    kvb_ref,
    do_ref,
    dqn_ref,
    dq1_ref,
    dq2_ref,
    dlat_ref,
    dk1_ref,
    dk2_ref,
    dkvb_ref,
    kvg_ref,
    acc_ref,
):
    group, micro = pl.program_id(0), pl.program_id(1)
    width = NOPE + VDIM

    @pl.when(group == 0)
    def _():
        dlat_ref[micro] = jnp.zeros(dlat_ref.shape[1:], f32)
        dk1_ref[micro] = jnp.zeros(dk1_ref.shape[1:], f32)
        dk2_ref[micro] = jnp.zeros(dk2_ref.shape[1:], f32)

    lat = lat_ref[0]
    kvb = kvb_ref[...]
    kv = dot(lat, kvb, 1, 0).astype(bf16)
    k1, k2 = k1_ref[0], k2_ref[0]
    dq1 = jnp.zeros(dq1_ref.shape[1:], f32)
    dq2 = jnp.zeros(dq2_ref.shape[1:], f32)
    dk1 = jnp.zeros(k1.shape, f32)
    dk2 = jnp.zeros(k2.shape, f32)
    for head in range(HEAD_GROUP):
        probs, q_head, k_head, v_head, q1m, q2m, mine = head_scores(
            qn_ref[0], q1_ref[0], q2_ref[0], kv, k1, k2, seen_ref[...], scale, head
        )
        d_out = do_ref[0, :, head * VDIM : (head + 1) * VDIM]
        dprobs = dot(d_out, v_head, 1, 1)
        delta = jnp.sum(probs * dprobs, axis=-1, keepdims=True)
        ds = (probs * (dprobs - delta)).astype(bf16)
        dqn_ref[0, :, head * NOPE : (head + 1) * NOPE] = (dot(ds, k_head, 1, 0) * scale).astype(bf16)
        dq1 = dq1 + jnp.where(mine, dot(ds, k1, 1, 0), 0.0)
        dq2 = dq2 + jnp.where(mine, dot(ds, k2, 1, 0), 0.0)
        dk1 = dk1 + dot(ds, q1m, 0, 0)
        dk2 = dk2 + dot(ds, q2m, 0, 0)
        kvg_ref[:, head * width : head * width + NOPE] = (dot(ds, q_head, 0, 0) * scale).astype(bf16)
        kvg_ref[:, head * width + NOPE : (head + 1) * width] = dot(
            probs.astype(bf16), d_out, 0, 0
        ).astype(bf16)
    dq1_ref[0] = dq1 * scale
    dq2_ref[0] = dq2 * scale
    dk1_ref[micro] += dk1 * scale
    dk2_ref[micro] += dk2 * scale
    kvg = kvg_ref[...]
    dlat_ref[micro] += dot(kvg, kvb, 1, 1)
    part = dot(lat, kvg, 0, 0)

    @pl.when(micro == 0)
    def _():
        acc_ref[...] = part

    @pl.when(micro > 0)
    def _():
        acc_ref[...] += part

    @pl.when(micro == pl.num_programs(1) - 1)
    def _():
        dkvb_ref[...] = acc_ref[...].astype(bf16)


def attention_specs(micros, rows, length):
    groups = HEADS // HEAD_GROUP
    wide = HEAD_GROUP * NOPE
    specs = [
        pl.BlockSpec((1, length), lambda g, m: (0, 0)),
        pl.BlockSpec((1, rows, wide), lambda g, m: (m, 0, g)),
        pl.BlockSpec((1, rows, GROUP_LANES), lambda g, m: (m, 0, g)),
        pl.BlockSpec((1, rows, GROUP_LANES), lambda g, m: (m, 0, g)),
        pl.BlockSpec((1, length, RANK), lambda g, m: (m, 0, 0)),
        pl.BlockSpec((1, length, GROUP_LANES), lambda g, m: (m, 0, 0)),
        pl.BlockSpec((1, length, GROUP_LANES), lambda g, m: (m, 0, 0)),
        pl.BlockSpec((RANK, HEAD_GROUP * (NOPE + VDIM)), lambda g, m: (0, g)),
    ]
    return (groups, micros), specs, pl.BlockSpec((1, rows, wide), lambda g, m: (m, 0, g))


def attend(seen, qn, q1, q2, lat, k1, k2, kvb, scale):
    micros, rows, _ = qn.shape
    length = lat.shape[1]
    grid, specs, out_spec = attention_specs(micros, rows, length)
    return pl.pallas_call(
        functools.partial(attend_kernel, scale),
        grid=grid,
        in_specs=specs,
        out_specs=out_spec,
        out_shape=jax.ShapeDtypeStruct(qn.shape, bf16),
        compiler_params=pltpu.CompilerParams(vmem_limit_bytes=48 << 20),
        name="attend",
    )(seen, qn, q1, q2, lat, k1, k2, kvb)


def attend_back(seen, qn, q1, q2, lat, k1, k2, kvb, d_out, scale):
    micros, rows, _ = qn.shape
    length = lat.shape[1]
    grid, specs, out_spec = attention_specs(micros, rows, length)
    whole = lambda g, m: (0, 0, 0)
    return pl.pallas_call(
        functools.partial(attend_back_kernel, scale),
        grid=grid,
        in_specs=specs + [out_spec],
        out_specs=[
            out_spec,
            pl.BlockSpec((1, rows, GROUP_LANES), lambda g, m: (m, 0, g)),
            pl.BlockSpec((1, rows, GROUP_LANES), lambda g, m: (m, 0, g)),
            pl.BlockSpec(lat.shape, whole),
            pl.BlockSpec(k1.shape, whole),
            pl.BlockSpec(k2.shape, whole),
            pl.BlockSpec((RANK, HEAD_GROUP * (NOPE + VDIM)), lambda g, m: (0, g)),
        ],
        out_shape=[
            jax.ShapeDtypeStruct(qn.shape, bf16),
            jax.ShapeDtypeStruct(q1.shape, f32),
            jax.ShapeDtypeStruct(q2.shape, f32),
            jax.ShapeDtypeStruct(lat.shape, f32),
            jax.ShapeDtypeStruct(k1.shape, f32),
            jax.ShapeDtypeStruct(k2.shape, f32),
            jax.ShapeDtypeStruct(kvb.shape, bf16),
        ],
        scratch_shapes=[
            pltpu.VMEM((length, HEAD_GROUP * (NOPE + VDIM)), bf16),
            pltpu.VMEM((RANK, HEAD_GROUP * (NOPE + VDIM)), f32),
        ],
        compiler_params=pltpu.CompilerParams(vmem_limit_bytes=48 << 20),
        name="attend_back",
    )(seen, qn, q1, q2, lat, k1, k2, kvb, d_out)


class Place:
    def __init__(self):
        self.r = lax.axis_index("rep")
        self.z = lax.axis_index("shard")
        self.core = self.r % 2
        self.chip = self.r // 2
        self.x = self.chip % 2
        self.y = self.chip // 2
        self.peer = (self.r + 1 - 2 * self.core, self.z)
        self.across = {
            "x": (self.r + 2 - 4 * self.x, self.z),
            "y": (self.r + 4 - 8 * self.y, self.z),
        }
        cx = self.chip + 1 - 2 * self.x
        cy = self.chip + 2 - 4 * self.y
        self.chips = {"": self.chip, "x": cx, "y": cy, "xy": cx + 2 - 4 * self.y}

    def along(self, step):
        return (self.r, (self.z + step) % 4)

    def shard_at(self, step):
        return (self.z + step) % 4


class Sems:
    def __init__(self, send, recv):
        self.send, self.recv = send, recv
        self.count = 0
        self.pending = []

    def slot(self):
        self.count += 1
        return self.count - 1

    def copy(self, src, dst, slot, device):
        return pltpu.make_async_remote_copy(
            src_ref=src,
            dst_ref=dst,
            send_sem=self.send.at[slot],
            recv_sem=self.recv.at[slot],
            device_id=device,
            device_id_type=MESH,
        )

    def push(self, src, dst, slot, device, when=None):
        under(when, lambda: self.copy(src, dst, slot, device).start())
        self.pending.append((lambda: self.copy(src, dst, slot, device).wait_send(), when))
        return self.pending[-1]

    def settle(self, entry):
        self.pending.remove(entry)
        under(entry[1], entry[0])

    def arrived(self, dst, slot, device, when=None):
        under(when, lambda: self.copy(dst, dst, slot, device).wait_recv())

    def drain(self):
        for wait, when in self.pending:
            under(when, wait)
        self.pending = []


def inside(z):
    return jnp.minimum(jnp.maximum(z, 0), 3)


def under(condition, act):
    if condition is None:
        act()
    else:
        pl.when(condition)(act)


def greet(devices):
    barrier = pltpu.get_barrier_semaphore()
    for device in devices:
        pl.semaphore_signal(barrier, inc=1, device_id=device, device_id_type=MESH)
    pl.semaphore_wait(barrier, len(devices))


def lanes(start, size):
    return pl.ds(pl.multiple_of(start, 128), size)


def rows16(start, size):
    return pl.ds(pl.multiple_of(start, 16), size)


class Through:
    def __init__(self, src, buffer, dst, sem):
        self.into = pltpu.make_async_copy(src, buffer, sem)
        self.out = pltpu.make_async_copy(buffer, dst, sem)

    def start(self):
        self.into.start()

    def turn(self):
        self.into.wait()
        self.out.start()

    def wait(self):
        self.out.wait()


class PlaneGather:
    def __init__(self, sems, place, part, half, by, when=None):
        self.sems, self.place, self.part, self.half, self.by = sems, place, part, half, by
        self.when = when
        self.slots = {k: sems.slot() for k in ("x", "y", "xy", "core")}

    def first(self, src=None):
        p = self.place
        mine = self.part(p.core, p.chip)
        for axis in ("x", "y"):
            self.push(mine if src is None else src, mine, self.slots[axis], p.across[axis])

    def push(self, src, dst, slot, device):
        self.sems.push(src, dst, slot, device, self.when)

    def arrived(self, dst, slot, device):
        self.sems.arrived(dst, slot, device, self.when)

    def second(self):
        p = self.place
        for axis in ("x", "y"):
            got = self.part(p.core, p.chips[axis])
            self.arrived(got, self.slots[axis], p.across[axis])
        via = self.by
        other = "y" if via == "x" else "x"
        got = self.part(p.core, p.chips[via])
        self.push(got, got, self.slots["xy"], p.across[other])

    def third(self):
        p = self.place
        got = self.part(p.core, p.chips["xy"])
        self.arrived(got, self.slots["xy"], p.across["y" if self.by == "x" else "x"])
        half = self.half(p.core)
        self.push(half, half, self.slots["core"], p.peer)

    def fourth(self):
        p = self.place
        self.arrived(self.half(1 - p.core), self.slots["core"], p.peer)


def weight_regions(place, refs, shard):
    q, kr, kvb, out = refs
    ds = q.shape[1] // 4
    cols = lanes(shard * ds, ds)

    def row_split(ref, n):
        half = ref.shape[0] // 2
        return (
            lambda core, chip: ref.at[rows16(core * half + chip * n, n), cols],
            lambda core: ref.at[rows16(core * half, half), cols],
        )

    def col_split(ref, full):
        rows = full // 4
        half = ref.shape[-1] // 2
        n = half // 4
        lead = (slice(None),) * (len(ref.shape) - 2)
        span = rows16(shard * rows, rows)
        return (
            lambda core, chip: ref.at[(*lead, span, lanes(core * half + chip * n, n))],
            lambda core: ref.at[(*lead, span, lanes(core * half, half))],
        )

    return [
        row_split(q, q.shape[0] // 8),
        row_split(kr, kr.shape[0] // 8),
        col_split(kvb, kvb.shape[0]),
        col_split(out, out.shape[0]),
    ]


def own_part(refs, place):
    q, kr, kvb, out, sh = refs
    res = []
    for ref in (q, kr):
        n = ref.shape[0] // 8
        res.append(ref.at[rows16(place.core * 4 * n + place.chip * n, n)])
    for ref in (kvb, out):
        n = ref.shape[-1] // 8
        res.append(ref.at[:, lanes(place.core * 4 * n + place.chip * n, n)])
    n = sh.shape[-1] // 8
    res.append(sh.at[:, :, lanes(place.r * n, n)])
    return res


ITEMS = 4
GATHER_ORDER = (1, 0, 2, 3)
GATHER_SEMS = 6 + ITEMS * 6 * 5
LAG = 6


class WeightGather:
    def __init__(self, place, sems, mine, outs):
        self.place, self.sems, self.mine, self.outs = place, sems, mine, outs
        z = place.z
        self.here = weight_regions(place, outs, z)
        self.slots = {}
        units = []
        for i in GATHER_ORDER:
            for d in (1, 2, 3):
                for s in (1, -1):
                    self.slots[i, d, s] = sems.slot()
                    exists = z >= d if s == 1 else z + d <= 3
                    part, half = weight_regions(place, outs, inside(z - s * d))[i]
                    by = "x" if (d + i) % 2 == 0 else "y"
                    units.append(
                        (i, d, s, exists, part, PlaneGather(sems, place, part, half, by, exists))
                    )
        for i in GATHER_ORDER[:2]:
            self.own(i)
        self.units = units

    def run(self, late):
        units = self.units
        for n in range(len(units) + 3 * LAG):
            if n == 3 * len(units) // 4:
                late()
            if n < len(units):
                if n % 6 == 0 and n // 6 + 2 < ITEMS:
                    self.own(GATHER_ORDER[n // 6 + 2])
                self.along(units[n])
            for lag, name in ((LAG, "second"), (2 * LAG, "third"), (3 * LAG, "fourth")):
                if 0 <= n - lag < len(units):
                    getattr(units[n - lag][5], name)()

    def onward(self, src, dst, i, d, s, exists=None):
        if d > 3:
            return
        z = self.place.z
        more = z < 3 if s == 1 else z > 0
        if exists is not None:
            more = more & exists
        device = (self.place.r, inside(z + s))
        self.sems.push(src, dst, self.slots[i, d, s], device, more)

    def own(self, i):
        for s in (1, -1):
            self.onward(self.mine[i], self.here[i][0](self.place.core, self.place.chip), i, 1, s)

    def along(self, unit):
        i, d, s, exists, part, spread = unit
        z = self.place.z
        got = part(self.place.core, self.place.chip)
        device = (self.place.r, inside(z - s))
        self.sems.arrived(got, self.slots[i, d, s], device, exists)
        self.onward(got, got, i, d + 1, s, exists)
        spread.first()


def gather_kernel(*refs):
    ins, shared, gain = refs[:ITEMS], refs[ITEMS], refs[ITEMS + 1]
    refs = refs[ITEMS + 2 :]
    outs, shared_out, gains = refs[:ITEMS], refs[ITEMS], refs[ITEMS + 1]
    refs = refs[ITEMS + 2 :]
    buffers, (gain_buffer, send, recv, local) = refs[:ITEMS], refs[ITEMS:]
    place = Place()
    sems = Sems(send, recv)
    greet([place.peer, place.across["x"], place.across["y"]] + [place.along(k) for k in (1, 2, 3)])
    mine = own_part((*ins, shared), place)
    ds = ins[0].shape[1]
    own = [
        outs[0].at[:, lanes(place.z * ds, ds)],
        outs[1].at[:, lanes(place.z * ds, ds)],
        outs[2].at[rows16(place.z * ins[2].shape[0], ins[2].shape[0])],
        outs[3].at[rows16(place.z * ins[3].shape[0], ins[3].shape[0])],
    ]
    kept = [Through(ins[i], buffers[i], own[i], local.at[i]) for i in range(ITEMS)]
    kept.append(Through(gain, gain_buffer, gains.at[place.z], local.at[ITEMS]))
    gain_slots = [sems.slot() for _ in range(3)]
    shared_slots = [sems.slot() for _ in range(3)]
    for k in (1, 2, 3):
        sems.push(gain, gains.at[place.z], gain_slots[k - 1], place.along(k))
    job = WeightGather(place, sems, mine, outs)
    for copy in kept:
        copy.start()
    for copy in kept:
        copy.turn()

    def late():
        for k in (1, 2, 3):
            sems.push(mine[ITEMS], shared_out.at[:, k - 1], shared_slots[k - 1], place.along(k))

    job.run(late)
    for k in (1, 2, 3):
        sems.arrived(gains.at[place.shard_at(4 - k)], gain_slots[k - 1], place.along(4 - k))
        sems.arrived(shared_out.at[:, k - 1], shared_slots[k - 1], place.along(4 - k))
    sems.drain()
    for copy in kept:
        copy.wait()


def gather_weights(q, kr, kvb, out, sh, gain, fast):
    if not fast:
        every = lambda w, axis: lax.all_gather(w, "shard", axis=axis, tiled=True)
        return (
            every(q, 1),
            every(kr, 1),
            every(kvb, 0),
            every(out, 0),
            every(sh, 1),
            lax.all_gather(gain, "shard", axis=0),
        )
    shape = jax.ShapeDtypeStruct
    *whole, rest, gains = pl.pallas_call(
        gather_kernel,
        in_specs=[pl.BlockSpec(memory_space=HBM)] * 6,
        out_specs=[pl.BlockSpec(memory_space=HBM)] * 6,
        out_shape=[
            shape((q.shape[0], q.shape[1] * 4), bf16),
            shape((kr.shape[0], kr.shape[1] * 4), bf16),
            shape((kvb.shape[0] * 4, kvb.shape[1]), bf16),
            shape((out.shape[0] * 4, out.shape[1]), bf16),
            shape((3, 3, sh.shape[1], sh.shape[2] // 8), bf16),
            shape((4,) + gain.shape, bf16),
        ],
        scratch_shapes=[pltpu.VMEM(w.shape, bf16) for w in (q, kr, kvb, out, gain)]
        + [
            pltpu.SemaphoreType.DMA((GATHER_SEMS,)),
            pltpu.SemaphoreType.DMA((GATHER_SEMS,)),
            pltpu.SemaphoreType.DMA((ITEMS + 1,)),
        ],
        compiler_params=pltpu.CompilerParams(
            collective_id=0, has_side_effects=True, vmem_limit_bytes=32 << 20
        ),
        name="gather_weights",
    )(q, kr, kvb, out, sh, gain)
    rest = lax.all_gather(rest, "rep", axis=3, tiled=True)
    return (*whole, rest.reshape(3, -1, sh.shape[2]), gains)


def along_z(tensor, step):
    return lax.ppermute(tensor, "shard", [(i, (i + step) % 4) for i in range(4)])


def over(tensor, mask):
    return lax.ppermute(tensor, "rep", [(i, i ^ mask) for i in range(8)])


def z_all(tensor, fast):
    if not fast:
        return lax.all_gather(tensor, "shard", axis=1, tiled=True)
    return jnp.concatenate([tensor] + [along_z(tensor, k) for k in (1, 2, 3)], axis=1)


def z_home(tensor, fast):
    if not fast:
        return lax.psum_scatter(tensor.astype(f32), "shard", scatter_dimension=1, tiled=True)
    rows = tensor.shape[1] // 4
    blocks = [lax.slice_in_dim(tensor, k * rows, (k + 1) * rows, axis=1) for k in range(4)]
    got = [along_z(blocks[k], -k).astype(f32) for k in (1, 2, 3)]
    return blocks[0].astype(f32) + got[0] + got[1] + got[2]


def swap_kernel(count, axes, *refs):
    ins, outs, buffers = (refs[n * count : (n + 1) * count] for n in range(3))
    send, recv, local = refs[3 * count :]
    place = Place()
    sems = Sems(send, recv)
    greet([place.peer])

    def cut(i, core):
        if axes[i] is None:
            return ins[i]
        n = ins[i].shape[axes[i]] // 2
        if axes[i] == 0:
            return ins[i].at[rows16(core * n, n)]
        return ins[i].at[:, lanes(core * n, n)]

    for i in range(count):
        sems.push(cut(i, 1 - place.core), outs[i].at[1], sems.slot(), place.peer)
    kept = [
        Through(cut(i, place.core), buffers[i], outs[i].at[0], local.at[i]) for i in range(count)
    ]
    for copy in kept:
        copy.start()
    for copy in kept:
        copy.turn()
    for i in range(count):
        sems.arrived(outs[i].at[1], i, place.peer)
    sems.drain()
    for copy in kept:
        copy.wait()


def core_swap(arrays, axes, fast, ident):
    count = len(arrays)
    if not fast:
        reps = lax.axis_size("rep")
        core = lax.axis_index("rep") % 2
        res = []
        for a, axis in zip(arrays, axes):
            keep = give = a
            if axis is not None:
                n = a.shape[axis] // 2
                keep = lax.dynamic_slice_in_dim(a, core * n, n, axis)
                give = lax.dynamic_slice_in_dim(a, (1 - core) * n, n, axis)
            got = lax.ppermute(give, "rep", [(i, i + 1 - 2 * (i % 2)) for i in range(reps)])
            res.append(jnp.stack([keep, got]))
        return res
    shapes = [
        tuple(n // 2 if d == axis else n for d, n in enumerate(a.shape))
        for a, axis in zip(arrays, axes)
    ]
    return pl.pallas_call(
        functools.partial(swap_kernel, count, axes),
        in_specs=[pl.BlockSpec(memory_space=HBM)] * count,
        out_specs=[pl.BlockSpec(memory_space=HBM)] * count,
        out_shape=[jax.ShapeDtypeStruct((2,) + s, a.dtype) for s, a in zip(shapes, arrays)],
        scratch_shapes=[pltpu.VMEM(s, a.dtype) for s, a in zip(shapes, arrays)]
        + [
            pltpu.SemaphoreType.DMA((count,)),
            pltpu.SemaphoreType.DMA((count,)),
            pltpu.SemaphoreType.DMA((count,)),
        ],
        compiler_params=pltpu.CompilerParams(
            collective_id=ident, has_side_effects=True, vmem_limit_bytes=32 << 20
        ),
        name="core_swap",
    )(*arrays)


def add_rows(dst, terms):
    lead = dst.shape[:-2]
    rows = max(n for n in (16, 32, 48, 64, 80) if dst.shape[-2] % n == 0)
    steps = dst.shape[-2] // rows

    def body(step, carry):
        span = pl.ds(pl.multiple_of(step * rows, rows), rows)
        where = (slice(None),) * len(lead) + (span,)
        total = terms[0][where].astype(f32)
        for t in terms[1:]:
            total = total + t[where].astype(f32)
        dst[where] = total.astype(dst.dtype)
        return carry

    lax.fori_loop(0, steps, body, 0)


def reduce_anywhere(q, kr, kvb, out, sh, ex, gain):
    core = lax.axis_index("rep") % 2

    def whole(g, axis):
        wide = jnp.zeros(g.shape[:axis] + (g.shape[axis] * 2,) + g.shape[axis + 1 :], f32)
        return lax.dynamic_update_slice_in_dim(wide, g.astype(f32), core * g.shape[axis], axis)

    def total(g, axis, along):
        g = lax.psum_scatter(whole(g, axis), "shard", scatter_dimension=along, tiled=True)
        return lax.psum(g, "rep")

    return (
        total(q, 0, 1),
        total(kr, 0, 1),
        total(kvb, 1, 0),
        total(out, 1, 0),
        total(sh, 2, 1),
        lax.psum(whole(ex, 2), "rep"),
        lax.psum(lax.psum_scatter(gain, "shard", scatter_dimension=0, tiled=True), "rep")[0],
    )


class Unit:
    def __init__(self, job, name, u, axis, part, got1, got2, own=None, home=None, got3=None, last=None):
        self.job, self.name, self.u = job, name, u
        self.axis, self.other = axis, "y" if axis == "x" else "x"
        self.part, self.got1, self.got2, self.own = part, got1, got2, own
        self.home, self.got3, self.last = home, got3, last
        self.slots = [job.sems.slot() for _ in range(4)]

    def stage1(self):
        job = self.job
        place = job.place
        for n, chip in enumerate((self.axis, "xy")):
            job.sems.push(
                self.part(place.chips[chip]), self.got1.at[n], self.slots[n], place.across[self.axis]
            )
        if self.own is not None:
            ring, sem = self.own
            self.loads = [
                pltpu.make_async_copy(
                    self.part(place.chips["" if n == 0 else self.other]), ring.at[n], sem.at[n]
                )
                for n in (0, 1)
            ]
            for copy in self.loads:
                copy.start()
            self.mine = [ring.at[0], ring.at[1]]
        else:
            self.mine = [self.part(place.chips[""]), self.part(place.chips[self.other])]

    def stage2(self):
        sems, place = self.job.sems, self.job.place
        for n in (1, 0):
            if self.own is not None:
                self.loads[n].wait()
            sems.arrived(self.got1.at[n], self.slots[n], place.across[self.axis])
            add_rows(self.got1.at[n], [self.got1.at[n], self.mine[n]])
            if n == 1:
                sems.push(self.got1.at[1], self.got2, self.slots[2], place.across[self.other])

    def stage3(self):
        sems, place = self.job.sems, self.job.place
        sems.arrived(self.got2, self.slots[2], place.across[self.other])
        add_rows(self.got1.at[0], [self.got1.at[0], self.got2])
        if self.home:
            sems.push(self.got1.at[0], self.got3.at[self.home - 1], self.slots[3], place.along(self.home))

    def stage4(self):
        if self.last is None:
            return
        job = self.job
        place = job.place
        for unit in job.units:
            if unit.name == self.name and unit.home:
                got = unit.got3.at[unit.home - 1]
                job.sems.arrived(got, unit.slots[3], place.along(4 - unit.home))
        if self.got3 is not None:
            add_rows(self.got1.at[0], [self.got1.at[0]] + [self.got3.at[n] for n in range(3)])
        src, part, half, sem, by = self.last
        self.stay = pltpu.make_async_copy(src, part(place.core, place.chip), sem)
        self.stay.start()
        self.spread = PlaneGather(job.sems, place, part, half, by)
        self.spread.first(src)

    def stage5(self):
        if self.last is not None:
            self.spread.second()

    def stage6(self):
        if self.last is not None:
            self.stay.wait()
            self.spread.third()

    def stage7(self):
        if self.last is not None:
            self.spread.fourth()


class Pump:
    LAGS = (0, 3, 3, 2, 1, 1, 1)

    def __init__(self, place, sems):
        self.place, self.sems = place, sems
        self.units = []
        self.at = [0] * 7

    def tick(self, flush=False):
        for n in range(7):
            ahead = len(self.units) if n == 0 else self.at[n - 1]
            if self.at[n] < ahead - (0 if flush else self.LAGS[n]):
                getattr(self.units[self.at[n]], "stage%d" % (n + 1))()
                self.at[n] += 1

    def run(self, count):
        for _ in range(count):
            self.tick()

    def end(self):
        while self.at[-1] < len(self.units):
            before = list(self.at)
            self.tick()
            if self.at == before:
                self.tick(True)


BACK_IN = (
    "gsh",
    "gex",
    "gout",
    "q",
    "kvb",
    "kq",
    "kkr",
    "x",
    "mid",
    "lat",
    "k1",
    "k2",
    "seen",
    "do",
    "ha",
    "latent",
    "kgain",
    "again",
    "fgain",
    "cos",
    "sin",
    "rtr",
)
BACK_HBM = 9
BACK_OUT = (
    "oq",
    "okr",
    "okvb",
    "oout",
    "osh",
    "osd",
    "oex",
    "zsh",
    "ogain",
    "ograd",
)
BACK_SLOTS = 3 + 3 + 5 + 10 + 28 * 4 + 7 * 4
EARLY = 2


def back_kernel(scale, names, *refs):
    r = dict(zip(names, refs))
    place = Place()
    sems = Sems(r["send"], r["recv"])
    others = [place.peer]
    for axes in ("x", "y", "xy"):
        for flip in (place.core, 1 - place.core):
            others.append((place.chips[axes] * 2 + flip, place.z))
    greet(others + [place.along(k) for k in (1, 2, 3)])
    load = r["load"]
    pump = Pump(place, sems)
    core = place.core
    toks = r["ha"].shape[0]
    rows = toks // 2

    ff = r["gsh"].shape[1] // 4
    shared_slots = [sems.slot() for _ in range(3)]
    for k in (1, 2, 3):
        sems.push(
            r["gsh"].at[:EARLY, k * ff : (k + 1) * ff], r["zsh"].at[k - 1], shared_slots[k - 1], place.along(4 - k)
        )
    swap = {name: sems.slot() for name in ("ha", "kvb", "q", "kvd", "rtr")}
    sems.push(r["ha"], r["s_ha"], swap["ha"], place.peer)
    sems.push(r["rtr"], r["s_rtr"], swap["rtr"], place.peer)
    begin = [
        pltpu.make_async_copy(r["q"], r["qs"], load.at[0]),
        pltpu.make_async_copy(r["kvb"], r["kvbs"], load.at[1]),
    ]
    for copy in begin:
        copy.start()

    def out_split(o, by_rows):
        if by_rows:
            half = o.shape[0] // 2
            n = half // 4
            return (
                lambda c, chip: o.at[rows16(c * half + chip * n, n)],
                lambda c: o.at[rows16(c * half, half)],
            )
        half = o.shape[-1] // 2
        n = half // 4
        lead = (slice(None),) * (len(o.shape) - 1)
        return (
            lambda c, chip: o.at[(*lead, lanes(c * half + chip * n, n))],
            lambda c: o.at[(*lead, lanes(c * half, half))],
        )

    rings = 0

    def ring(shape_ref):
        nonlocal rings
        slot = rings % 4
        rings += 1
        return slot

    def add_matrices(name, source, count, out, by, ringed):
        for u in range(count):
            n = source.shape[-1] // 4
            own = None
            if ringed:
                slot = ring(None)
                own = (r["ring_" + name].at[slot], r["ringsem"].at[slot])
            last = None
            if u == count - 1:
                last = (r["got1_" + name].at[:, 0], *out_split(out, False), r["keep"].at[len(pump.units) % 8], by)
            pump.units.append(
                Unit(
                    pump,
                    name,
                    u,
                    "x" if u % 2 == 0 else "y",
                    lambda chip, u=u: source.at[u, :, lanes(chip * n, n)],
                    r["got1_" + name].at[u],
                    r["got2_" + name].at[u],
                    own=own,
                    last=last,
                )
            )

    def add_sharded(name, part_of, out, by_rows, by, ringed=None):
        for n, k in enumerate((1, 2, 3, 4)):
            u, s = k % 4, place.shard_at(k)
            own = None
            if ringed:
                slot = ring(None)
                own = (r["ring_" + ringed].at[slot], r["ringsem"].at[slot])
            last = None
            if k == 4:
                last = (r["got1_" + name].at[0, 0], *out_split(out, by_rows), r["keep"].at[len(pump.units) % 8], by)
            pump.units.append(
                Unit(
                    pump,
                    name,
                    u,
                    "x" if n % 2 == 0 else "y",
                    lambda chip, s=s, k=k: part_of(s, k, chip),
                    r["got1_" + name].at[u],
                    r["got2_" + name].at[u],
                    own=own,
                    home=k % 4,
                    got3=r["got3_" + name],
                    last=last,
                )
            )

    add_matrices("ex", r["gex"], r["gex"].shape[0], r["oex"], "x", True)
    block = r["gout"].shape[0] // 4
    n_out = r["gout"].shape[1] // 4
    add_sharded(
        "out",
        lambda s, k, chip: r["gout"].at[rows16(s * block, block), lanes(chip * n_out, n_out)],
        r["oout"],
        False,
        "y",
        "out",
    )
    n_sd = r["gsh"].shape[2] // 4
    add_sharded(
        "sd",
        lambda s, k, chip: r["gsh"].at[
            EARLY, (4 - k) % 4 * ff : ((4 - k) % 4 + 1) * ff, lanes(chip * n_sd, n_sd)
        ],
        r["osd"],
        False,
        "x",
        "ex",
    )
    pump.run(3)
    for copy in begin:
        copy.wait()

    qs, kvbs, kvg, acc, dlat, dkvb = (r[n] for n in ("qs", "kvbs", "kvg", "acc", "dlat", "dkvb"))
    n1 = HEADS * NOPE
    n2 = HEADS * (NOPE + HALF_ROPE)
    width = NOPE + VDIM
    lane = lax.broadcasted_iota(jnp.int32, (1, GROUP_LANES), 1)

    def attention_step(group, micro):
        span = slice(micro * rows, (micro + 1) * rows)
        at = group * GROUP_LANES
        lat, k1, k2 = r["lat"][micro], r["k1"][micro], r["k2"][micro]
        q1, q2 = qs[span, n1 + at : n1 + at + GROUP_LANES], qs[span, n2 + at : n2 + at + GROUP_LANES]
        dq1 = jnp.zeros(q1.shape, f32)
        dq2 = jnp.zeros(q2.shape, f32)
        dk1 = jnp.zeros(k1.shape, f32)
        dk2 = jnp.zeros(k2.shape, f32)
        for pair in (0, 1):
            cols = slice((group * 4 + pair * 2) * width, (group * 4 + pair * 2 + 2) * width)
            weight = kvbs[:, cols]
            kv = dot(lat, weight, 1, 0).astype(bf16)
            for n in (0, 1):
                head = pair * 2 + n
                here = slice((group * 4 + head) * NOPE, (group * 4 + head + 1) * NOPE)
                mine = (lane >= head * HALF_ROPE) & (lane < (head + 1) * HALF_ROPE)
                q_head = qs[span, here]
                k_head = kv[:, n * width : n * width + NOPE]
                v_head = kv[:, n * width + NOPE : (n + 1) * width]
                q1m = jnp.where(mine, q1, jnp.zeros_like(q1))
                q2m = jnp.where(mine, q2, jnp.zeros_like(q2))
                scores = dot(q_head, k_head, 1, 1) + dot(q1m, k1, 1, 1) + dot(q2m, k2, 1, 1)
                scores = jnp.where(r["seen"][...] > 0.0, scores * scale, masked_score)
                expo = jnp.exp(scores - jnp.max(scores, axis=-1, keepdims=True))
                probs = expo / jnp.sum(expo, axis=-1, keepdims=True)
                d_out = r["do"][micro, :, here]
                dprobs = dot(d_out, v_head, 1, 1)
                delta = jnp.sum(probs * dprobs, axis=-1, keepdims=True)
                ds = (probs * (dprobs - delta)).astype(bf16)
                qs[span, here] = (dot(ds, k_head, 1, 0) * scale).astype(bf16)
                dq1 = dq1 + jnp.where(mine, dot(ds, k1, 1, 0), 0.0)
                dq2 = dq2 + jnp.where(mine, dot(ds, k2, 1, 0), 0.0)
                dk1 = dk1 + dot(ds, q1m, 0, 0)
                dk2 = dk2 + dot(ds, q2m, 0, 0)
                kvg[:, n * width : n * width + NOPE] = (dot(ds, q_head, 0, 0) * scale).astype(bf16)
                kvg[:, n * width + NOPE : (n + 1) * width] = dot(
                    probs.astype(bf16), d_out, 0, 0
                ).astype(bf16)
            terms = kvg[...]
            if group == 0 and pair == 0:
                dlat[micro] = dot(terms, weight, 1, 1)
            else:
                dlat[micro] += dot(terms, weight, 1, 1)
            part = dot(lat, terms, 0, 0)
            hold = slice(pair * 2 * width, (pair + 1) * 2 * width)
            if micro == 0:
                acc[:, hold] = part
            else:
                dkvb[:, cols] = (acc[:, hold] + part).astype(bf16)
        dq1, dq2 = dq1 * scale, dq2 * scale
        cosine, sine = r["cos"][...], r["sin"][...]
        qs[span, n1 + at : n1 + at + GROUP_LANES] = (dq1 * cosine + dq2 * sine).astype(bf16)
        qs[span, n2 + at : n2 + at + GROUP_LANES] = (dq2 * cosine - dq1 * sine).astype(bf16)
        for ref, value in ((r["dk1"], dk1), (r["dk2"], dk2)):
            if group == 0:
                ref[micro] = value * scale
            else:
                ref[micro] += value * scale

    for group in range(HEADS // HEAD_GROUP):
        for micro in (0, 1):
            attention_step(group, micro)
            pump.run(1)

    pack, zs = r["pack"], r["zs"]
    fold = lambda t: sum(t[:, n * HALF_ROPE : (n + 1) * HALF_ROPE] for n in range(HEAD_GROUP))
    for micro in (0, 1):
        pack[micro, :, :RANK] = dlat[micro].astype(bf16)
        pack[micro, :, RANK : RANK + HALF_ROPE] = fold(r["dk1"][micro]).astype(bf16)
        pack[micro, :, RANK + HALF_ROPE : RANK + ROPE] = fold(r["dk2"][micro]).astype(bf16)
        pack[micro, :, RANK + ROPE :] = jnp.zeros((pack.shape[1], ROPE), bf16)
    z_slots = [sems.slot() for _ in range(3)]
    for k in (1, 2, 3):
        sems.push(pack.at[:, k * rows : (k + 1) * rows], zs.at[k - 1], z_slots[k - 1], place.along(4 - k))
    half_q, half_kvb = qs.shape[1] // 2, dkvb.shape[1] // 2
    sems.push(qs.at[:, lanes((1 - core) * half_q, half_q)], r["s_q"], swap["q"], place.peer)
    kvb_push = sems.push(
        dkvb.at[:, lanes((1 - core) * half_kvb, half_kvb)], r["s_kvb"], swap["kvb"], place.peer
    )
    pump.run(1)

    sems.arrived(r["s_kvb"], swap["kvb"], place.peer)
    add_rows(r["s_kvb"], [r["s_kvb"], dkvb.at[:, lanes(core * half_kvb, half_kvb)]])
    n_kvb, b_kvb = half_kvb // 4, dkvb.shape[0] // 4
    add_sharded(
        "kvb",
        lambda s, k, chip: r["s_kvb"].at[rows16(s * b_kvb, b_kvb), lanes(chip * n_kvb, n_kvb)],
        r["okvb"],
        False,
        "x",
    )
    sems.arrived(r["s_ha"], swap["ha"], place.peer)
    sems.arrived(r["s_q"], swap["q"], place.peer)
    gq, ha, s_ha = r["gq"], r["ha"], r["s_ha"]

    def q_tile(t, carry):
        own = qs[:, lanes(core * half_q + t * 128, 128)]
        got = r["s_q"][:, lanes(t * 128, 128)]
        gq[rows16(t * 128, 128)] = (dot(own, ha[...], 0, 0) + dot(got, s_ha[...], 0, 0)).astype(bf16)
        return carry

    for part in range(4):
        lax.fori_loop(part * 3, part * 3 + 3, q_tile, 0)
        pump.run(1)
    r_q, c_q = gq.shape[0] // 4, gq.shape[1] // 4
    add_sharded(
        "q",
        lambda s, k, chip: gq.at[rows16(chip * r_q, r_q), lanes(s * c_q, c_q)],
        r["oq"],
        True,
        "y",
    )
    pump.run(4)

    for k in (1, 2, 3):
        sems.arrived(zs.at[k - 1], z_slots[k - 1], place.along(k))
    kvd, gains = r["kvd"], r["gains"]
    kv_gain_grad = jnp.zeros((1, RANK), f32)
    for micro in (0, 1):
        span = slice(micro * rows, (micro + 1) * rows)
        total = pack[micro, :rows].astype(f32)
        for k in range(3):
            total = total + zs[k, micro].astype(f32)
        upstream, latent = total[:, :RANK], r["latent"][span]
        inv = rms_scale(latent)
        scaled = upstream * r["kgain"][...]
        inner = jnp.mean(scaled * latent, axis=-1, keepdims=True)
        kvd[span, :RANK] = (inv * scaled - latent * (inv * inv * inv) * inner).astype(bf16)
        kv_gain_grad = kv_gain_grad + jnp.sum(upstream * latent * inv, axis=0, keepdims=True)
        g1, g2 = total[:, RANK : RANK + HALF_ROPE], total[:, RANK + HALF_ROPE : RANK + ROPE]
        cosine, sine = r["cos"][:, :HALF_ROPE], r["sin"][:, :HALF_ROPE]
        kvd[span, RANK : RANK + HALF_ROPE] = (g1 * cosine + g2 * sine).astype(bf16)
        kvd[span, RANK + HALF_ROPE : RANK + ROPE] = (g2 * cosine - g1 * sine).astype(bf16)
        kvd[span, RANK + ROPE :] = jnp.zeros((rows, ROPE), bf16)
    sems.push(kvd, r["s_kvd"], swap["kvd"], place.peer)

    tile = 384
    tiles = [("kq", t * tile, tile) for t in range(qs.shape[1] // tile)]
    tiles += [("kkr", 0, tile), ("kkr", tile, r["kkr"].shape[0] - tile)]
    wide = ha.shape[1]
    half_w = wide // 2

    def fetch(t):
        name, start, n = tiles[t]
        return pltpu.make_async_copy(
            r[name].at[start : start + n],
            kvbs.at[:n, (t % 2) * wide : (t % 2 + 1) * wide],
            load.at[2 + t % 2],
        )

    fetch(0).start()
    for t, (name, start, n) in enumerate(tiles):
        fetch(t).wait()
        if t + 1 < len(tiles):
            fetch(t + 1).start()
        left = (qs if name == "kq" else kvd)[:, start : start + n]
        for half in (0, 1):
            base = (t % 2) * wide + half * half_w
            value = dot(left, kvbs[:n, base : base + half_w], 1, 0)
            where = slice(half * toks, (half + 1) * toks)
            if t == 0:
                acc[where] = value
            else:
                acc[where] += value
        if t % 2 == 1:
            pump.run(1)

    for k in (1, 2, 3):
        sems.arrived(r["zsh"].at[k - 1], shared_slots[k - 1], place.along(k))
    cols = r["gsh"].shape[2]
    for j in range(EARLY):
        copies = [pltpu.make_async_copy(r["gsh"].at[j, :ff], kvbs.at[:ff, :cols], load.at[6])]
        for k in range(3):
            copies.append(
                pltpu.make_async_copy(
                    r["zsh"].at[k, j], kvbs.at[:ff, (k + 1) * cols : (k + 2) * cols], load.at[7 + k]
                )
            )
        for copy in copies:
            copy.start()
        for copy in copies:
            copy.wait()
        add_rows(r["gshs"].at[j], [kvbs.at[:ff, k * cols : (k + 1) * cols] for k in range(4)])
    add_matrices("sh", r["gshs"], EARLY, r["osh"], "y", False)
    pump.run(2)

    sems.arrived(r["s_kvd"], swap["kvd"], place.peer)
    sems.arrived(r["s_rtr"], swap["rtr"], place.peer)
    sems.settle(kvb_push)
    half_kr = r["kkr"].shape[0] // 2
    r_kr, c_kr = half_kr // 4, wide // 4
    edges = sorted(set(list(range(0, 2 * half_kr + 1, 128)) + [half_kr]))
    for start, stop in zip(edges[:-1], edges[1:]):
        value = dot(kvd[:, start:stop], ha[...], 0, 0)
        value = value + dot(r["s_kvd"][:, start:stop], s_ha[...], 0, 0)
        n = start // half_kr
        if stop == 2 * half_kr:
            first = RANK + ROPE - start
            both = r["rtr"][...].astype(f32) + r["s_rtr"][...].astype(f32)
            value = jnp.concatenate([value[:first], both])
        dkvb[start - n * half_kr : stop - n * half_kr, n * wide : (n + 1) * wide] = value.astype(bf16)
    add_sharded(
        "kr",
        lambda s, k, chip: dkvb.at[rows16(chip * r_kr, r_kr), lanes(core * wide + s * c_kr, c_kr)],
        r["okr"],
        True,
        "x",
    )
    pump.run(2)

    again = r["again"][...]
    attn_gain_grad = jnp.zeros((1, wide), f32)
    step = 32
    for start in range(0, toks, step):
        fetched = [
            pltpu.make_async_copy(r[a].at[start : start + step], r[b], load.at[4 + n])
            for n, (a, b) in enumerate((("x", "xb"), ("mid", "mb")))
        ]
        for copy in fetched:
            copy.start()
        for copy in fetched:
            copy.wait()
        x = r["xb"][...].astype(f32)
        upstream = jnp.concatenate(
            [acc[start : start + step], acc[toks + start : toks + start + step]], axis=1
        )
        inv = rms_scale(x)
        scaled = upstream * again
        inner = jnp.mean(scaled * x, axis=-1, keepdims=True)
        part = inv * scaled - x * (inv * inv * inv) * inner
        r["ograd"][start : start + step] = (r["mb"][...] + part).astype(bf16)
        attn_gain_grad = attn_gain_grad + jnp.sum(upstream * x * inv, axis=0, keepdims=True)
    n_a, n_k = wide // 4, RANK // 4
    gains[...] = jnp.zeros(gains.shape, f32)
    for s in range(4):
        gains[s, 0:1, :n_a] = attn_gain_grad[:, s * n_a : (s + 1) * n_a]
        gains[s, 0:1, n_a : 2 * n_a] = r["fgain"][:, s * n_a : (s + 1) * n_a]
        gains[s, 0:1, 2 * n_a :] = kv_gain_grad[:, s * n_k : (s + 1) * n_k]
    gain_slots = [sems.slot() for _ in range(3 + 7)]
    gz, gp, gs = r["gz"], r["gp"], r["gs"]
    for k in (1, 2, 3):
        sems.push(gains.at[place.shard_at(k)], gz.at[k - 1], gain_slots[k - 1], place.along(k))
    pump.run(2)

    for k in (1, 2, 3):
        sems.arrived(gz.at[k - 1], gain_slots[k - 1], place.along(4 - k))
    gs[...] = gains[place.z] + gz[0] + gz[1] + gz[2]
    for n, device in enumerate(others):
        sems.push(gs, gp.at[n], gain_slots[3 + n], device)
    pump.end()
    total = gs[...]
    for n, device in enumerate(others):
        sems.arrived(gp.at[n], gain_slots[3 + n], device)
        total = total + gp[n]
    r["ogain"][...] = total
    sems.drain()


def back_all(args, scale):
    shape = jax.ShapeDtypeStruct
    gsh, gex, gout, q, kvb, kq, kkr = (args[n] for n in BACK_IN[:7])
    toks, wide = args["ha"].shape
    micros, length, rank = args["lat"].shape
    fe, ff = gex.shape[1], gsh.shape[1] // 4
    rows = toks // micros
    n_a = wide // 4
    gain_shape = (8, 2 * n_a + rank // 4)
    outs = dict(
        oq=shape((q.shape[1], wide // 4), bf16),
        okr=shape((kkr.shape[0], wide // 4), bf16),
        okvb=shape((rank // 4, kvb.shape[1]), bf16),
        oout=shape((gout.shape[0] // 4, wide), bf16),
        osh=shape((EARLY, ff, wide), bf16),
        osd=shape((ff, wide), bf16),
        oex=shape((gex.shape[0], fe, wide), bf16),
        zsh=shape((3, EARLY, ff, wide // 2), bf16),
        ogain=shape(gain_shape, f32),
        ograd=shape((toks, wide), bf16),
    )
    vm = pltpu.VMEM
    parts = dict(
        out=(gout.shape[0] // 4, wide // 8),
        sd=(ff, wide // 8),
        kvb=(rank // 4, kvb.shape[1] // 8),
        q=(q.shape[1] // 8, wide // 4),
        kr=(kkr.shape[0] // 8, wide // 4),
    )
    scratch = dict(
        qs=vm(q.shape, bf16),
        kvbs=vm(kvb.shape, bf16),
        kvg=vm((length, 2 * (NOPE + VDIM)), bf16),
        acc=vm((2 * toks, wide // 2), f32),
        dlat=vm((micros, length, rank), f32),
        dk1=vm((micros, length, GROUP_LANES), f32),
        dk2=vm((micros, length, GROUP_LANES), f32),
        dkvb=vm(kvb.shape, bf16),
        pack=vm((micros, length, rank + 2 * ROPE), bf16),
        zs=vm((3, micros, rows, rank + 2 * ROPE), bf16),
        kvd=vm((toks, rank + 2 * ROPE), bf16),
        s_ha=vm((toks, wide), bf16),
        s_q=vm((toks, q.shape[1] // 2), bf16),
        s_kvb=vm((rank, kvb.shape[1] // 2), bf16),
        s_kvd=vm((toks, rank + 2 * ROPE), bf16),
        s_rtr=vm(args["rtr"].shape, bf16),
        gq=vm((q.shape[1] // 2, wide), bf16),
        gshs=vm((EARLY, ff, wide // 2), bf16),
        xb=vm((32, wide), bf16),
        mb=vm((32, wide), f32),
        gains=vm((4,) + gain_shape, f32),
        gz=vm((3,) + gain_shape, f32),
        gp=vm((7,) + gain_shape, f32),
        gs=vm(gain_shape, f32),
        ring_ex=vm((4, 2, fe, wide // 8), bf16),
        ring_out=vm((4, 2) + parts["out"], bf16),
        got1_ex=vm((gex.shape[0], 2, fe, wide // 8), bf16),
        got2_ex=vm((gex.shape[0], fe, wide // 8), bf16),
        got1_sh=vm((EARLY, 2, ff, wide // 8), bf16),
        got2_sh=vm((EARLY, ff, wide // 8), bf16),
    )
    for name, part in parts.items():
        scratch["got1_" + name] = vm((4, 2) + part, bf16)
        scratch["got2_" + name] = vm((4,) + part, bf16)
        scratch["got3_" + name] = vm((3,) + part, bf16)
    dma = pltpu.SemaphoreType.DMA
    scratch.update(
        send=dma((BACK_SLOTS,)), recv=dma((BACK_SLOTS,)), load=dma((10,)), keep=dma((8,)), ringsem=dma((4, 2))
    )
    names = (*BACK_IN, *BACK_OUT, *scratch)
    hbm, vmem = pl.BlockSpec(memory_space=HBM), pl.BlockSpec(memory_space=pltpu.VMEM)
    res = pl.pallas_call(
        functools.partial(back_kernel, scale, names),
        in_specs=[hbm] * BACK_HBM + [vmem] * (len(BACK_IN) - BACK_HBM),
        out_specs=[hbm if n not in ("ogain", "ograd") else vmem for n in BACK_OUT],
        out_shape=[outs[n] for n in BACK_OUT],
        scratch_shapes=list(scratch.values()),
        compiler_params=pltpu.CompilerParams(
            collective_id=1, has_side_effects=True, vmem_limit_bytes=61 << 20
        ),
        name="back_all",
    )(*(args[n] for n in BACK_IN))
    return dict(zip(BACK_OUT, res))


def head_split(weight):
    per_head = weight.reshape(HEADS, NOPE + ROPE, weight.shape[1])
    cuts = (0, NOPE, NOPE + HALF_ROPE, NOPE + ROPE)
    return jnp.concatenate(
        [per_head[:, a:b].reshape(-1, weight.shape[1]) for a, b in zip(cuts[:-1], cuts[1:])]
    )


def head_join(weight):
    cols = weight.shape[1]
    nope = weight[: HEADS * NOPE].reshape(HEADS, NOPE, cols)
    first = weight[HEADS * NOPE : HEADS * (NOPE + HALF_ROPE)].reshape(HEADS, HALF_ROPE, cols)
    second = weight[HEADS * (NOPE + HALF_ROPE) :].reshape(HEADS, HALF_ROPE, cols)
    return jnp.concatenate([nope, first, second], axis=1).reshape(-1, cols)


def shards(
    tokens,
    attn_gain,
    q_weight,
    kva_weight,
    kv_gain,
    kvb_weight,
    out_weight,
    ffn_gain,
    router_weight,
    shared_gate,
    shared_up,
    shared_down,
    expert_gate,
    expert_up,
    expert_down,
    expert_ids,
    cotangent,
):
    shard_count = lax.axis_size("shard")
    shard_index = lax.axis_index("shard")
    core = lax.axis_index("rep") % 2
    fast = lax.axis_size("rep") == 8 and shard_count == 4
    micros, rows, width = tokens.shape
    toks = micros * rows
    scale = (NOPE + ROPE) ** (-0.5)
    ga, gk = attn_gain.shape[0], kv_gain.shape[0]

    gain_pack = jnp.concatenate([attn_gain, ffn_gain, kv_gain]).astype(bf16)
    gain_pack = jnp.broadcast_to(gain_pack[None], (16, gain_pack.shape[0]))
    sh_own = jnp.stack([shared_gate, shared_up, shared_down]).astype(bf16)
    query_mat, kr_mat, kvb_mat, out_mat, sh_rest, gains = gather_weights(
        head_split(q_weight).astype(bf16),
        jnp.concatenate([kva_weight, router_weight]).astype(bf16),
        kvb_weight.astype(bf16),
        out_weight.astype(bf16),
        sh_own,
        gain_pack,
        fast,
    )
    gain_rows = gains[:, 0].astype(f32)
    attn_gain_f = gain_rows[:, :ga].reshape(-1)
    ffn_gain_f = gain_rows[:, ga : 2 * ga].reshape(-1)
    kv_gain_f = gain_rows[:, 2 * ga :].reshape(-1)
    kv_down_mat, router_mat = kr_mat[: RANK + ROPE], kr_mat[RANK + ROPE :]
    sh_mats = [sh_own, sh_rest] if fast else [sh_rest]

    def hidden(t, index):
        return jnp.concatenate([dot(t, m[index], 1, 1) for m in sh_mats], axis=1)

    def unhidden(t, index):
        at, total = 0, 0.0
        for m in sh_mats:
            total = total + dot(t[:, at : at + m.shape[1]], m[index], 1, 0)
            at += m.shape[1]
        return total


    x_in = tokens.reshape(toks, width).astype(f32)
    inv_one = rms_scale(x_in)
    h_attn = (x_in * inv_one * attn_gain_f).astype(bf16)
    positions = (shard_index * rows + jnp.arange(rows, dtype=jnp.int32)).astype(f32)
    frequency = jnp.exp(
        -jnp.log(rope_base) * (2.0 * jnp.arange(HALF_ROPE, dtype=f32) / ROPE)
    )
    angles = positions[:, None] * frequency[None, :]
    cosine = jnp.tile(jnp.cos(angles), (micros, 1))
    sine = jnp.tile(jnp.sin(angles), (micros, 1))
    cos_all, sin_all = jnp.tile(cosine, (1, HEADS)), jnp.tile(sine, (1, HEADS))
    q_raw = dot(h_attn, query_mat, 1, 1)
    n1, n2 = HEADS * NOPE, HEADS * (NOPE + HALF_ROPE)
    q_first, q_second = q_raw[:, n1:n2], q_raw[:, n2:]
    by_micro = lambda t: t.reshape(micros, rows, t.shape[-1])
    qn = by_micro(q_raw[:, :n1].astype(bf16))
    q1 = by_micro((q_first * cos_all - q_second * sin_all).astype(bf16))
    q2 = by_micro((q_second * cos_all + q_first * sin_all).astype(bf16))
    kv_down = dot(h_attn, kv_down_mat, 1, 1)
    latent = kv_down[:, :RANK]
    inv_kv = rms_scale(latent)
    latent_norm = (latent * inv_kv * kv_gain_f).astype(bf16)
    k_first, k_second = kv_down[:, RANK : RANK + HALF_ROPE], kv_down[:, RANK + HALF_ROPE :]
    latent_pack = jnp.concatenate(
        [
            latent_norm,
            (k_first * cosine - k_second * sine).astype(bf16),
            (k_second * cosine + k_first * sine).astype(bf16),
            jnp.zeros((toks, ROPE), bf16),
        ],
        axis=-1,
    )
    packs = z_all(by_micro(latent_pack), fast)
    length = packs.shape[1]
    lat_all = packs[..., :RANK]
    k1 = jnp.tile(packs[..., RANK : RANK + HALF_ROPE], (1, 1, HEAD_GROUP))
    k2 = jnp.tile(packs[..., RANK + HALF_ROPE : RANK + ROPE], (1, 1, HEAD_GROUP))
    key_shard = jnp.arange(length, dtype=jnp.int32) // rows
    if fast:
        key_shard = (shard_index - key_shard) % 4
    key_block = (key_shard * rows + jnp.arange(length, dtype=jnp.int32) % rows) // MASK_BLOCK
    seen = (key_block <= (shard_index * rows) // MASK_BLOCK).astype(f32).reshape(1, length)
    attended = attend(seen, qn, q1, q2, lat_all, k1, k2, kvb_mat, scale).reshape(toks, -1)

    x_mid = x_in + dot(attended, out_mat, 1, 0)
    inv_two = rms_scale(x_mid)
    h_ffn = (x_mid * inv_two * ffn_gain_f).astype(bf16)
    router_probs = jax.nn.softmax(dot(h_ffn, router_mat, 1, 1), axis=-1)
    grad_b = cotangent.reshape(toks, width)

    member = jnp.any(
        expert_ids[:, :, None, :] == jnp.arange(EXP_WIN, dtype=jnp.int32)[None, None, :, None], axis=-1
    ).astype(jnp.int32)
    placed = jnp.cumsum(member, axis=1) - 1
    hits = (member[:, :, :, None] == 1) & (
        placed[:, :, :, None] == jnp.arange(CAP, dtype=jnp.int32)
    )
    select = jnp.transpose(hits, (2, 0, 3, 1)).astype(f32)
    select_b = select.astype(bf16)
    h3, c3 = by_micro(h_ffn), by_micro(grad_b)
    gather_slots = lambda t: jnp.einsum(
        "emct,mtd->emcd", select_b, t, preferred_element_type=f32
    ).astype(bf16)
    flat = lambda t: t.reshape(EXP_WIN, micros * CAP, t.shape[-1])
    tall = lambda t: t.reshape(-1, t.shape[-1])
    picked_all = z_all(flat(gather_slots(c3)), fast)
    rows_all = z_all(flat(gather_slots(h3)), fast)

    gate_pre, up_pre = hidden(h_ffn, 0), hidden(h_ffn, 1)
    shared_hidden = (jax.nn.silu(gate_pre) * up_pre).astype(bf16)
    shared_hidden_grad = hidden(grad_b, 2)
    gate_grad_b, up_grad_b = swiglu_back(gate_pre, up_pre, shared_hidden_grad)
    sh_s, hf_s, cot_s = core_swap(
        [jnp.concatenate([gate_grad_b, up_grad_b, shared_hidden], axis=1), h_ffn, grad_b],
        (None, 1, 1),
        fast,
        7,
    )
    ff = shared_hidden.shape[1]
    sh_s, hf_s, cot_s = tall(sh_s), tall(hf_s), tall(cot_s)
    grad_sh = jnp.stack(
        [
            dot(sh_s[:, :ff], hf_s, 0, 0).astype(bf16),
            dot(sh_s[:, ff : 2 * ff], hf_s, 0, 0).astype(bf16),
            dot(sh_s[:, 2 * ff :], cot_s, 0, 0).astype(bf16),
        ]
    )
    picked_all = picked_all.astype(f32)
    slot_probs = jax.nn.softmax(
        jnp.einsum("end,xd->enx", rows_all, router_mat, preferred_element_type=f32), axis=-1
    )
    gates_all = jnp.stack([slot_probs[e, :, e] for e in range(EXP_WIN)])[..., None]
    dy_all = (gates_all * picked_all).astype(bf16)
    eg, eu, ed = expert_gate.astype(bf16), expert_up.astype(bf16), expert_down.astype(bf16)
    bdot = lambda a, b, ca, cb: lax.dot_general(
        a, b, (((ca,), (cb,)), ((0,), (0,))), preferred_element_type=f32
    )
    expert_pre = bdot(rows_all, eg, 2, 2)
    expert_upv = bdot(rows_all, eu, 2, 2)
    expert_hidden = (jax.nn.silu(expert_pre) * expert_upv).astype(bf16)
    expert_part = bdot(expert_hidden, ed, 2, 1)
    gate_part = jnp.sum(picked_all * expert_part, axis=-1, keepdims=True)
    gate_high = gate_part.astype(bf16)
    gate_low = (gate_part - gate_high.astype(f32)).astype(bf16)
    expert_hidden_grad = bdot(dy_all, ed, 2, 2)
    expert_gate_b, expert_up_b = swiglu_back(expert_pre, expert_upv, expert_hidden_grad)
    slot_part = (bdot(expert_gate_b, eg, 2, 1) + bdot(expert_up_b, eu, 2, 1)).astype(bf16)
    slot_part = jnp.concatenate(
        [slot_part, gate_high, gate_low, jnp.zeros(slot_part.shape[:2] + (126,), bf16)], axis=-1
    )
    slot_back = z_home(slot_part, fast)
    expert_back = z_home(expert_part.astype(bf16), fast)

    ex_s, row_s, dy_s = core_swap(
        [
            tall(jnp.concatenate([expert_gate_b, expert_up_b, expert_hidden], axis=-1)),
            tall(rows_all),
            tall(dy_all),
        ],
        (None, 1, 1),
        fast,
        8,
    )
    fe = expert_hidden.shape[-1]
    by_expert = lambda t: t.reshape(2, EXP_WIN, -1, t.shape[-1])
    ex_s, row_s, dy_s = by_expert(ex_s), by_expert(row_s), by_expert(dy_s)
    edot = lambda a, b: jnp.einsum("senf,send->efd", a, b, preferred_element_type=f32).astype(bf16)
    grad_ex = jnp.concatenate(
        [
            edot(ex_s[..., :fe], row_s),
            edot(ex_s[..., fe : 2 * fe], row_s),
            edot(ex_s[..., 2 * fe :], dy_s),
        ]
    )
    ffn_grad = unhidden(gate_grad_b, 0) + unhidden(up_grad_b, 1)
    back = lambda t: t.reshape(EXP_WIN, micros, CAP, t.shape[-1])
    slot_grad = back(slot_back[..., :width])
    gate_weight_grad = back(slot_back[..., width : width + 2]).sum(axis=-1)
    ffn_grad = ffn_grad + jnp.einsum(
        "emct,emcd->mtd", select, slot_grad, precision=highest
    ).reshape(toks, width)
    probs_grad = jnp.einsum("emct,emc->mte", select, gate_weight_grad, precision=highest)
    probs_grad = jnp.pad(
        probs_grad.reshape(toks, EXP_WIN), ((0, 0), (0, EXPERTS - EXP_WIN))
    )
    logit_grad = (
        router_probs * (probs_grad - jnp.sum(router_probs * probs_grad, axis=-1, keepdims=True))
    ).astype(bf16)
    ffn_grad = ffn_grad + dot(logit_grad, router_mat, 1, 0)
    mid_part, ffn_gain_grad = norm_back(x_mid, inv_two, ffn_gain_f, ffn_grad)
    mid_grad = grad_b.astype(f32) + mid_part
    attn_out_grad = mid_grad.astype(bf16)
    attended_grad = by_micro(dot(attn_out_grad, out_mat, 1, 1).astype(bf16))

    att_s, og_s = core_swap([attended, attn_out_grad], (None, 1), fast, 2)
    grad_out = dot(tall(att_s), tall(og_s), 0, 0).astype(bf16)
    expert_out = back(expert_back)
    slot_gates = jnp.einsum(
        "emct,mte->emc", select, by_micro(router_probs)[..., :EXP_WIN], precision=highest
    )
    routed = jnp.einsum("emct,emcd->mtd", select, slot_gates[..., None] * expert_out, precision=highest)
    layer_output = x_mid + unhidden(shared_hidden, 2) + routed.reshape(toks, width)
    layer_output = layer_output.astype(bf16)

    lane_rows = lambda t: t.reshape(shard_count, -1)
    if fast:
        row = lambda t: t.reshape(1, -1)
        group_tab = lambda t: jnp.tile(t[:rows], (1, HEAD_GROUP))
        res = back_all(
            dict(
                gsh=grad_sh,
                gex=grad_ex,
                gout=grad_out,
                q=jnp.concatenate([t.reshape(toks, -1) for t in (qn, q1, q2)], axis=1),
                kvb=kvb_mat,
                kq=query_mat,
                kkr=kr_mat,
                x=tokens.reshape(toks, width),
                mid=mid_grad,
                lat=lat_all,
                k1=k1,
                k2=k2,
                seen=seen,
                do=attended_grad,
                ha=h_attn,
                latent=latent,
                kgain=row(kv_gain_f),
                again=row(attn_gain_f),
                fgain=row(ffn_gain_grad),
                cos=group_tab(cosine),
                sin=group_tab(sine),
                rtr=dot(logit_grad, h_ffn, 0, 0).astype(bf16),
            ),
            scale,
        )
        gq, gkr, gkvb, gout = (res[n] for n in ("oq", "okr", "okvb", "oout"))
        gsh = (res["osh"][0], res["osh"][1], res["osd"])
        gex, gg = res["oex"], res["ogain"][0]
        input_grad = res["ograd"]
    else:
        dqn, dq1, dq2, dlat, dk1, dk2, dkvb = attend_back(
            seen, qn, q1, q2, lat_all, k1, k2, kvb_mat, attended_grad, scale
        )
        fold = lambda t: jnp.sum(t.reshape(micros, length, HEAD_GROUP, HALF_ROPE), axis=2)
        back_pack = jnp.concatenate(
            [dlat, fold(dk1), fold(dk2), jnp.zeros((micros, length, ROPE), f32)], axis=-1
        ).astype(bf16)
        own_back = z_home(back_pack, fast).reshape(toks, -1)
        latent_grad, kv_gain_grad = norm_back(latent, inv_kv, kv_gain_f, own_back[:, :RANK])
        g1, g2 = own_back[:, RANK : RANK + HALF_ROPE], own_back[:, RANK + HALF_ROPE : RANK + ROPE]
        kv_down_grad = jnp.concatenate(
            [latent_grad, g1 * cosine + g2 * sine, g2 * cosine - g1 * sine], axis=-1
        ).astype(bf16)
        dq1, dq2 = dq1.reshape(toks, -1), dq2.reshape(toks, -1)
        q_raw_grad = jnp.concatenate(
            [
                dqn.reshape(toks, -1),
                (dq1 * cos_all + dq2 * sin_all).astype(bf16),
                (dq2 * cos_all - dq1 * sin_all).astype(bf16),
            ],
            axis=-1,
        )
        attn_in_grad = dot(q_raw_grad, query_mat, 1, 0) + dot(kv_down_grad, kv_down_mat, 1, 0)
        x_part, attn_gain_grad = norm_back(x_in, inv_one, attn_gain_f, attn_in_grad)
        input_grad = (mid_grad + x_part).astype(bf16)

        kr_grad = jnp.concatenate(
            [dot(kv_down_grad, h_attn, 0, 0), dot(logit_grad, h_ffn, 0, 0)]
        ).astype(bf16)
        h_s, qg_s, krg_s, kvbg_s = core_swap(
            [h_attn, q_raw_grad, kr_grad, dkvb], (None, 1, 0, 1), fast, 6
        )
        grad_q = dot(tall(qg_s), tall(h_s), 0, 0).astype(bf16)
        grad_kr = (krg_s[0].astype(f32) + krg_s[1].astype(f32)).astype(bf16)
        grad_kvb = (kvbg_s[0].astype(f32) + kvbg_s[1].astype(f32)).astype(bf16)
        gain_grad = jnp.concatenate(
            [lane_rows(attn_gain_grad), lane_rows(ffn_gain_grad), lane_rows(kv_gain_grad)], axis=1
        )
        gain_len = gain_grad.shape[1]
        gain_grad = jnp.pad(gain_grad, ((0, 0), (0, 16 * 128 - gain_len))).reshape(-1, 16, 128)
        gq, gkr, gkvb, gout, gsh, gex, gg = reduce_anywhere(
            grad_q, grad_kr, grad_kvb, grad_out, grad_sh, grad_ex, gain_grad
        )
        gg = gg.reshape(-1)
    wide = lambda t: t.astype(f32)
    return (
        by_micro(layer_output),
        by_micro(input_grad),
        gg[:ga],
        wide(head_join(gq)),
        wide(gkr[: RANK + ROPE]),
        gg[2 * ga : 2 * ga + gk],
        wide(gkvb),
        wide(gout),
        gg[ga : 2 * ga],
        wide(gkr[RANK + ROPE :]),
        wide(gsh[0]),
        wide(gsh[1]),
        wide(gsh[2]),
        wide(gex[:2]),
        wide(gex[2:4]),
        wide(gex[4:]),
    )


def solution(mesh):
    token_spec = P(None, ("rep", "shard"), None)
    row_spec, col_spec, gain_spec = P("shard", None), P(None, "shard"), P("shard")
    expert_spec = P(None, "shard", None)
    weight_specs = (
        gain_spec,
        col_spec,
        col_spec,
        gain_spec,
        row_spec,
        row_spec,
        gain_spec,
        col_spec,
        row_spec,
        row_spec,
        row_spec,
        expert_spec,
        expert_spec,
        expert_spec,
    )
    return jax.shard_map(
        shards,
        mesh=mesh,
        in_specs=(token_spec,) + weight_specs + (token_spec, token_spec),
        out_specs=(token_spec, token_spec) + weight_specs,
        check_vma=False,
    )
```

```python
import functools

import jax
import jax.numpy as jnp
from jax import lax
from jax.experimental import pallas as pl
from jax.experimental.pallas import tpu as pltpu
from jax.sharding import PartitionSpec as P

HEADS = 16
NOPE = 128
ROPE = 64
VDIM = 128
RANK = 512
EXPERTS = 64
EXP_WIN = 2
MASK_BLOCK = 256
CAP = 16

epsilon = 1e-06
rope_base = 10000.0
masked_score = -1e30
highest = lax.Precision.HIGHEST
bf16 = jnp.bfloat16
f32 = jnp.float32
MESH = pl.DeviceIdType.MESH
HBM = pltpu.HBM
HALF_ROPE = ROPE // 2
HEAD_GROUP = 4
GROUP_LANES = HEAD_GROUP * HALF_ROPE


def dot(a, b, ca, cb):
    return lax.dot_general(a, b, (((ca,), (cb,)), ((), ())), preferred_element_type=f32)


def rms_scale(tensor):
    return lax.rsqrt(jnp.mean(tensor * tensor, axis=-1, keepdims=True) + epsilon)


def norm_back(tensor, inv_rms, gain_vec, gradient):
    scaled_grad = gradient * gain_vec
    inner_mean = jnp.mean(scaled_grad * tensor, axis=-1, keepdims=True)
    input_part = inv_rms * scaled_grad - tensor * (inv_rms * inv_rms * inv_rms) * inner_mean
    gain_part = jnp.sum(gradient * tensor * inv_rms, axis=0)
    return (input_part, gain_part)


def swiglu_back(gate_pre, up_pre, hidden_grad):
    sigmoid_gate = jax.nn.sigmoid(gate_pre)
    silu_gate = gate_pre * sigmoid_gate
    slope = sigmoid_gate * (1.0 + gate_pre * (1.0 - sigmoid_gate))
    return (
        (hidden_grad * up_pre * slope).astype(bf16),
        (hidden_grad * silu_gate).astype(bf16),
    )


def head_scores(qn, q1, q2, kv, k1, k2, seen, scale, head):
    lane = lax.broadcasted_iota(jnp.int32, (1, GROUP_LANES), 1)
    mine = (lane >= head * HALF_ROPE) & (lane < (head + 1) * HALF_ROPE)
    width = NOPE + VDIM
    q_head = qn[:, head * NOPE : (head + 1) * NOPE]
    k_head = kv[:, head * width : head * width + NOPE]
    v_head = kv[:, head * width + NOPE : (head + 1) * width]
    q1m = jnp.where(mine, q1, jnp.zeros_like(q1))
    q2m = jnp.where(mine, q2, jnp.zeros_like(q2))
    scores = dot(q_head, k_head, 1, 1) + dot(q1m, k1, 1, 1) + dot(q2m, k2, 1, 1)
    scores = jnp.where(seen > 0.0, scores * scale, masked_score)
    top = jnp.max(scores, axis=-1, keepdims=True)
    expo = jnp.exp(scores - top)
    probs = expo / jnp.sum(expo, axis=-1, keepdims=True)
    return probs, q_head, k_head, v_head, q1m, q2m, mine


def attend_kernel(scale, seen_ref, qn_ref, q1_ref, q2_ref, lat_ref, k1_ref, k2_ref, kvb_ref, out_ref):
    kv = dot(lat_ref[0], kvb_ref[...], 1, 0).astype(bf16)
    for head in range(HEAD_GROUP):
        probs, _, _, v_head, _, _, _ = head_scores(
            qn_ref[0], q1_ref[0], q2_ref[0], kv, k1_ref[0], k2_ref[0], seen_ref[...], scale, head
        )
        out_ref[0, :, head * VDIM : (head + 1) * VDIM] = dot(
            probs.astype(bf16), v_head, 1, 0
        ).astype(bf16)


def attend_back_kernel(
    scale,
    seen_ref,
    qn_ref,
    q1_ref,
    q2_ref,
    lat_ref,
    k1_ref,
    k2_ref,
    kvb_ref,
    do_ref,
    dqn_ref,
    dq1_ref,
    dq2_ref,
    dlat_ref,
    dk1_ref,
    dk2_ref,
    dkvb_ref,
    kvg_ref,
    acc_ref,
):
    group, micro = pl.program_id(0), pl.program_id(1)
    width = NOPE + VDIM

    @pl.when(group == 0)
    def _():
        dlat_ref[micro] = jnp.zeros(dlat_ref.shape[1:], f32)
        dk1_ref[micro] = jnp.zeros(dk1_ref.shape[1:], f32)
        dk2_ref[micro] = jnp.zeros(dk2_ref.shape[1:], f32)

    lat = lat_ref[0]
    kvb = kvb_ref[...]
    kv = dot(lat, kvb, 1, 0).astype(bf16)
    k1, k2 = k1_ref[0], k2_ref[0]
    dq1 = jnp.zeros(dq1_ref.shape[1:], f32)
    dq2 = jnp.zeros(dq2_ref.shape[1:], f32)
    dk1 = jnp.zeros(k1.shape, f32)
    dk2 = jnp.zeros(k2.shape, f32)
    for head in range(HEAD_GROUP):
        probs, q_head, k_head, v_head, q1m, q2m, mine = head_scores(
            qn_ref[0], q1_ref[0], q2_ref[0], kv, k1, k2, seen_ref[...], scale, head
        )
        d_out = do_ref[0, :, head * VDIM : (head + 1) * VDIM]
        dprobs = dot(d_out, v_head, 1, 1)
        delta = jnp.sum(probs * dprobs, axis=-1, keepdims=True)
        ds = (probs * (dprobs - delta)).astype(bf16)
        dqn_ref[0, :, head * NOPE : (head + 1) * NOPE] = (dot(ds, k_head, 1, 0) * scale).astype(bf16)
        dq1 = dq1 + jnp.where(mine, dot(ds, k1, 1, 0), 0.0)
        dq2 = dq2 + jnp.where(mine, dot(ds, k2, 1, 0), 0.0)
        dk1 = dk1 + dot(ds, q1m, 0, 0)
        dk2 = dk2 + dot(ds, q2m, 0, 0)
        kvg_ref[:, head * width : head * width + NOPE] = (dot(ds, q_head, 0, 0) * scale).astype(bf16)
        kvg_ref[:, head * width + NOPE : (head + 1) * width] = dot(
            probs.astype(bf16), d_out, 0, 0
        ).astype(bf16)
    dq1_ref[0] = dq1 * scale
    dq2_ref[0] = dq2 * scale
    dk1_ref[micro] += dk1 * scale
    dk2_ref[micro] += dk2 * scale
    kvg = kvg_ref[...]
    dlat_ref[micro] += dot(kvg, kvb, 1, 1)
    part = dot(lat, kvg, 0, 0)

    @pl.when(micro == 0)
    def _():
        acc_ref[...] = part

    @pl.when(micro > 0)
    def _():
        acc_ref[...] += part

    @pl.when(micro == pl.num_programs(1) - 1)
    def _():
        dkvb_ref[...] = acc_ref[...].astype(bf16)


def attention_specs(micros, rows, length):
    groups = HEADS // HEAD_GROUP
    wide = HEAD_GROUP * NOPE
    specs = [
        pl.BlockSpec((1, length), lambda g, m: (0, 0)),
        pl.BlockSpec((1, rows, wide), lambda g, m: (m, 0, g)),
        pl.BlockSpec((1, rows, GROUP_LANES), lambda g, m: (m, 0, g)),
        pl.BlockSpec((1, rows, GROUP_LANES), lambda g, m: (m, 0, g)),
        pl.BlockSpec((1, length, RANK), lambda g, m: (m, 0, 0)),
        pl.BlockSpec((1, length, GROUP_LANES), lambda g, m: (m, 0, 0)),
        pl.BlockSpec((1, length, GROUP_LANES), lambda g, m: (m, 0, 0)),
        pl.BlockSpec((RANK, HEAD_GROUP * (NOPE + VDIM)), lambda g, m: (0, g)),
    ]
    return (groups, micros), specs, pl.BlockSpec((1, rows, wide), lambda g, m: (m, 0, g))


def attend(seen, qn, q1, q2, lat, k1, k2, kvb, scale):
    micros, rows, _ = qn.shape
    length = lat.shape[1]
    grid, specs, out_spec = attention_specs(micros, rows, length)
    return pl.pallas_call(
        functools.partial(attend_kernel, scale),
        grid=grid,
        in_specs=specs,
        out_specs=out_spec,
        out_shape=jax.ShapeDtypeStruct(qn.shape, bf16),
        compiler_params=pltpu.CompilerParams(vmem_limit_bytes=48 << 20),
        name="attend",
    )(seen, qn, q1, q2, lat, k1, k2, kvb)


def attend_packed(seen, q, lat, k1, k2, kvb, scale):
    micros, rows, _ = q.shape
    length = lat.shape[1]
    grid, specs, out_spec = attention_specs(micros, rows, length)
    first = HEADS * NOPE // GROUP_LANES
    second = HEADS * (NOPE + HALF_ROPE) // GROUP_LANES
    specs[2] = pl.BlockSpec((1, rows, GROUP_LANES), lambda g, m: (m, 0, first + g))
    specs[3] = pl.BlockSpec((1, rows, GROUP_LANES), lambda g, m: (m, 0, second + g))
    return pl.pallas_call(
        functools.partial(attend_kernel, scale),
        grid=grid,
        in_specs=specs,
        out_specs=out_spec,
        out_shape=jax.ShapeDtypeStruct((micros, rows, HEADS * VDIM), bf16),
        compiler_params=pltpu.CompilerParams(vmem_limit_bytes=48 << 20),
        name="attend",
    )(seen, q, q, q, lat, k1, k2, kvb)


def attend_back(seen, qn, q1, q2, lat, k1, k2, kvb, d_out, scale):
    micros, rows, _ = qn.shape
    length = lat.shape[1]
    grid, specs, out_spec = attention_specs(micros, rows, length)
    whole = lambda g, m: (0, 0, 0)
    return pl.pallas_call(
        functools.partial(attend_back_kernel, scale),
        grid=grid,
        in_specs=specs + [out_spec],
        out_specs=[
            out_spec,
            pl.BlockSpec((1, rows, GROUP_LANES), lambda g, m: (m, 0, g)),
            pl.BlockSpec((1, rows, GROUP_LANES), lambda g, m: (m, 0, g)),
            pl.BlockSpec(lat.shape, whole),
            pl.BlockSpec(k1.shape, whole),
            pl.BlockSpec(k2.shape, whole),
            pl.BlockSpec((RANK, HEAD_GROUP * (NOPE + VDIM)), lambda g, m: (0, g)),
        ],
        out_shape=[
            jax.ShapeDtypeStruct(qn.shape, bf16),
            jax.ShapeDtypeStruct(q1.shape, f32),
            jax.ShapeDtypeStruct(q2.shape, f32),
            jax.ShapeDtypeStruct(lat.shape, f32),
            jax.ShapeDtypeStruct(k1.shape, f32),
            jax.ShapeDtypeStruct(k2.shape, f32),
            jax.ShapeDtypeStruct(kvb.shape, bf16),
        ],
        scratch_shapes=[
            pltpu.VMEM((length, HEAD_GROUP * (NOPE + VDIM)), bf16),
            pltpu.VMEM((RANK, HEAD_GROUP * (NOPE + VDIM)), f32),
        ],
        compiler_params=pltpu.CompilerParams(vmem_limit_bytes=48 << 20),
        name="attend_back",
    )(seen, qn, q1, q2, lat, k1, k2, kvb, d_out)


class Place:
    def __init__(self):
        self.r = lax.axis_index("rep")
        self.z = lax.axis_index("shard")
        self.core = self.r % 2
        self.chip = self.r // 2
        self.x = self.chip % 2
        self.y = self.chip // 2
        self.peer = (self.r + 1 - 2 * self.core, self.z)
        self.across = {
            "x": (self.r + 2 - 4 * self.x, self.z),
            "y": (self.r + 4 - 8 * self.y, self.z),
        }
        cx = self.chip + 1 - 2 * self.x
        cy = self.chip + 2 - 4 * self.y
        self.chips = {"": self.chip, "x": cx, "y": cy, "xy": cx + 2 - 4 * self.y}

    def along(self, step):
        return (self.r, (self.z + step) % 4)

    def shard_at(self, step):
        return (self.z + step) % 4


class Sems:
    def __init__(self, send, recv):
        self.send, self.recv = send, recv
        self.count = 0
        self.pending = []

    def slot(self):
        self.count += 1
        return self.count - 1

    def copy(self, src, dst, slot, device):
        return pltpu.make_async_remote_copy(
            src_ref=src,
            dst_ref=dst,
            send_sem=self.send.at[slot],
            recv_sem=self.recv.at[slot],
            device_id=device,
            device_id_type=MESH,
        )

    def push(self, src, dst, slot, device, when=None):
        under(when, lambda: self.copy(src, dst, slot, device).start())
        self.pending.append((lambda: self.copy(src, dst, slot, device).wait_send(), when))
        return self.pending[-1]

    def settle(self, entry):
        self.pending.remove(entry)
        under(entry[1], entry[0])

    def arrived(self, dst, slot, device, when=None):
        under(when, lambda: self.copy(dst, dst, slot, device).wait_recv())

    def drain(self):
        for wait, when in self.pending:
            under(when, wait)
        self.pending = []


def inside(z):
    return jnp.minimum(jnp.maximum(z, 0), 3)


def under(condition, act):
    if condition is None:
        act()
    else:
        pl.when(condition)(act)


def greet(devices):
    barrier = pltpu.get_barrier_semaphore()
    for device in devices:
        pl.semaphore_signal(barrier, inc=1, device_id=device, device_id_type=MESH)
    pl.semaphore_wait(barrier, len(devices))


def lanes(start, size):
    return pl.ds(pl.multiple_of(start, 128), size)


def rows16(start, size):
    return pl.ds(pl.multiple_of(start, 16), size)


class Through:
    def __init__(self, src, buffer, dst, sem):
        self.into = pltpu.make_async_copy(src, buffer, sem)
        self.out = pltpu.make_async_copy(buffer, dst, sem)

    def start(self):
        self.into.start()

    def turn(self):
        self.into.wait()
        self.out.start()

    def wait(self):
        self.out.wait()


class PlaneGather:
    def __init__(self, sems, place, part, half, by, when=None):
        self.sems, self.place, self.part, self.half, self.by = sems, place, part, half, by
        self.when = when
        self.slots = {k: sems.slot() for k in ("x", "y", "xy", "core")}

    def first(self, src=None):
        p = self.place
        mine = self.part(p.core, p.chip)
        for axis in ("x", "y"):
            self.push(mine if src is None else src, mine, self.slots[axis], p.across[axis])

    def push(self, src, dst, slot, device):
        self.sems.push(src, dst, slot, device, self.when)

    def arrived(self, dst, slot, device):
        self.sems.arrived(dst, slot, device, self.when)

    def second(self):
        p = self.place
        for axis in ("x", "y"):
            got = self.part(p.core, p.chips[axis])
            self.arrived(got, self.slots[axis], p.across[axis])
        via = self.by
        other = "y" if via == "x" else "x"
        got = self.part(p.core, p.chips[via])
        self.push(got, got, self.slots["xy"], p.across[other])

    def third(self):
        p = self.place
        got = self.part(p.core, p.chips["xy"])
        self.arrived(got, self.slots["xy"], p.across["y" if self.by == "x" else "x"])
        half = self.half(p.core)
        self.push(half, half, self.slots["core"], p.peer)

    def fourth(self):
        p = self.place
        self.arrived(self.half(1 - p.core), self.slots["core"], p.peer)


def weight_regions(place, refs, shard):
    q, kr, kvb, out = refs
    ds = q.shape[1] // 4
    cols = lanes(shard * ds, ds)

    def row_split(ref, n):
        half = ref.shape[0] // 2
        return (
            lambda core, chip: ref.at[rows16(core * half + chip * n, n), cols],
            lambda core: ref.at[rows16(core * half, half), cols],
        )

    def col_split(ref, full):
        rows = full // 4
        half = ref.shape[-1] // 2
        n = half // 4
        lead = (slice(None),) * (len(ref.shape) - 2)
        span = rows16(shard * rows, rows)
        return (
            lambda core, chip: ref.at[(*lead, span, lanes(core * half + chip * n, n))],
            lambda core: ref.at[(*lead, span, lanes(core * half, half))],
        )

    return [
        row_split(q, q.shape[0] // 8),
        row_split(kr, kr.shape[0] // 8),
        col_split(kvb, kvb.shape[0]),
        col_split(out, out.shape[0]),
    ]


def own_part(refs, place):
    q, kr, kvb, out, sh = refs
    res = []
    for ref in (q, kr):
        n = ref.shape[0] // 8
        res.append(ref.at[rows16(place.core * 4 * n + place.chip * n, n)])
    for ref in (kvb, out):
        n = ref.shape[-1] // 8
        res.append(ref.at[:, lanes(place.core * 4 * n + place.chip * n, n)])
    n = sh.shape[-1] // 8
    res.append(sh.at[:, :, lanes(place.r * n, n)])
    return res


ITEMS = 4
GATHER_ORDER = (1, 0, 2, 3)
GATHER_SEMS = 6 + ITEMS * 6 * 5
LAG = 6


class WeightGather:
    def __init__(self, place, sems, mine, outs):
        self.place, self.sems, self.mine, self.outs = place, sems, mine, outs
        z = place.z
        self.here = weight_regions(place, outs, z)
        self.slots = {}
        units = []
        for i in GATHER_ORDER:
            for d in (1, 2, 3):
                for s in (1, -1):
                    self.slots[i, d, s] = sems.slot()
                    exists = z >= d if s == 1 else z + d <= 3
                    part, half = weight_regions(place, outs, inside(z - s * d))[i]
                    by = "x" if (d + i) % 2 == 0 else "y"
                    units.append(
                        (i, d, s, exists, part, PlaneGather(sems, place, part, half, by, exists))
                    )
        for i in GATHER_ORDER[:2]:
            self.own(i)
        self.units = units

    def run(self, late):
        units = self.units
        for n in range(len(units) + 3 * LAG):
            if n == 3 * len(units) // 4:
                late()
            if n < len(units):
                if n % 6 == 0 and n // 6 + 2 < ITEMS:
                    self.own(GATHER_ORDER[n // 6 + 2])
                self.along(units[n])
            for lag, name in ((LAG, "second"), (2 * LAG, "third"), (3 * LAG, "fourth")):
                if 0 <= n - lag < len(units):
                    getattr(units[n - lag][5], name)()

    def onward(self, src, dst, i, d, s, exists=None):
        if d > 3:
            return
        z = self.place.z
        more = z < 3 if s == 1 else z > 0
        if exists is not None:
            more = more & exists
        device = (self.place.r, inside(z + s))
        self.sems.push(src, dst, self.slots[i, d, s], device, more)

    def own(self, i):
        for s in (1, -1):
            self.onward(self.mine[i], self.here[i][0](self.place.core, self.place.chip), i, 1, s)

    def along(self, unit):
        i, d, s, exists, part, spread = unit
        z = self.place.z
        got = part(self.place.core, self.place.chip)
        device = (self.place.r, inside(z - s))
        self.sems.arrived(got, self.slots[i, d, s], device, exists)
        self.onward(got, got, i, d + 1, s, exists)
        spread.first()


def gather_kernel(*refs):
    ins, shared, gain = refs[:ITEMS], refs[ITEMS], refs[ITEMS + 1]
    refs = refs[ITEMS + 2 :]
    outs, shared_out, gains = refs[:ITEMS], refs[ITEMS], refs[ITEMS + 1]
    refs = refs[ITEMS + 2 :]
    buffers, (gain_buffer, send, recv, local) = refs[:ITEMS], refs[ITEMS:]
    place = Place()
    sems = Sems(send, recv)
    greet([place.peer, place.across["x"], place.across["y"]] + [place.along(k) for k in (1, 2, 3)])
    mine = own_part((*ins, shared), place)
    ds = ins[0].shape[1]
    own = [
        outs[0].at[:, lanes(place.z * ds, ds)],
        outs[1].at[:, lanes(place.z * ds, ds)],
        outs[2].at[rows16(place.z * ins[2].shape[0], ins[2].shape[0])],
        outs[3].at[rows16(place.z * ins[3].shape[0], ins[3].shape[0])],
    ]
    kept = [Through(ins[i], buffers[i], own[i], local.at[i]) for i in range(ITEMS)]
    kept.append(Through(gain, gain_buffer, gains.at[place.z], local.at[ITEMS]))
    gain_slots = [sems.slot() for _ in range(3)]
    shared_slots = [sems.slot() for _ in range(3)]
    for k in (1, 2, 3):
        sems.push(gain, gains.at[place.z], gain_slots[k - 1], place.along(k))
    job = WeightGather(place, sems, mine, outs)
    for copy in kept:
        copy.start()
    for copy in kept:
        copy.turn()

    def late():
        for k in (1, 2, 3):
            sems.push(mine[ITEMS], shared_out.at[:, k - 1], shared_slots[k - 1], place.along(k))

    job.run(late)
    for k in (1, 2, 3):
        sems.arrived(gains.at[place.shard_at(4 - k)], gain_slots[k - 1], place.along(4 - k))
        sems.arrived(shared_out.at[:, k - 1], shared_slots[k - 1], place.along(4 - k))
    sems.drain()
    for copy in kept:
        copy.wait()


def gather_weights(q, kr, kvb, out, sh, gain, fast):
    if not fast:
        every = lambda w, axis: lax.all_gather(w, "shard", axis=axis, tiled=True)
        return (
            every(q, 1),
            every(kr, 1),
            every(kvb, 0),
            every(out, 0),
            every(sh, 1),
            lax.all_gather(gain, "shard", axis=0),
        )
    shape = jax.ShapeDtypeStruct
    *whole, rest, gains = pl.pallas_call(
        gather_kernel,
        in_specs=[pl.BlockSpec(memory_space=HBM)] * 6,
        out_specs=[pl.BlockSpec(memory_space=HBM)] * 6,
        out_shape=[
            shape((q.shape[0], q.shape[1] * 4), bf16),
            shape((kr.shape[0], kr.shape[1] * 4), bf16),
            shape((kvb.shape[0] * 4, kvb.shape[1]), bf16),
            shape((out.shape[0] * 4, out.shape[1]), bf16),
            shape((3, 3, sh.shape[1], sh.shape[2] // 8), bf16),
            shape((4,) + gain.shape, bf16),
        ],
        scratch_shapes=[pltpu.VMEM(w.shape, bf16) for w in (q, kr, kvb, out, gain)]
        + [
            pltpu.SemaphoreType.DMA((GATHER_SEMS,)),
            pltpu.SemaphoreType.DMA((GATHER_SEMS,)),
            pltpu.SemaphoreType.DMA((ITEMS + 1,)),
        ],
        compiler_params=pltpu.CompilerParams(
            collective_id=0, has_side_effects=True, vmem_limit_bytes=32 << 20
        ),
        name="gather_weights",
    )(q, kr, kvb, out, sh, gain)
    rest = lax.all_gather(rest, "rep", axis=3, tiled=True)
    return (*whole, rest.reshape(3, -1, sh.shape[2]), gains)


def along_z(tensor, step):
    return lax.ppermute(tensor, "shard", [(i, (i + step) % 4) for i in range(4)])


def over(tensor, mask):
    return lax.ppermute(tensor, "rep", [(i, i ^ mask) for i in range(8)])


def z_all(tensor, fast):
    if not fast:
        return lax.all_gather(tensor, "shard", axis=1, tiled=True)
    return jnp.concatenate([tensor] + [along_z(tensor, k) for k in (1, 2, 3)], axis=1)


def z_home(tensor, fast):
    if not fast:
        return lax.psum_scatter(tensor.astype(f32), "shard", scatter_dimension=1, tiled=True)
    rows = tensor.shape[1] // 4
    blocks = [lax.slice_in_dim(tensor, k * rows, (k + 1) * rows, axis=1) for k in range(4)]
    got = [along_z(blocks[k], -k).astype(f32) for k in (1, 2, 3)]
    return blocks[0].astype(f32) + got[0] + got[1] + got[2]


def front_kernel(
    x_ref,
    again_ref,
    kgain_ref,
    kr_ref,
    cos_ref,
    sin_ref,
    mat_ref,
    ha_ref,
    latent_ref,
    q_ref,
    lat_ref,
    k1_ref,
    k2_ref,
    tiles,
    pack,
    packs,
    send,
    recv,
    load,
):
    place = Place()
    sems = Sems(send, recv)
    size = tiles.shape[1]

    def fetch(t):
        return pltpu.make_async_copy(
            mat_ref.at[t * size : (t + 1) * size], tiles.at[t % 2], load.at[t % 2]
        )

    fetch(0).start()
    greet([place.along(k) for k in (1, 2, 3)])

    def normed(t, carry):
        span = pl.ds(pl.multiple_of(t * 32, 32), 32)
        x = x_ref[span].astype(f32)
        ha_ref[span] = (x * rms_scale(x) * again_ref[...]).astype(bf16)
        return carry

    lax.fori_loop(0, x_ref.shape[0] // 32, normed, 0)
    ha = ha_ref[...]
    kv_down = dot(ha, kr_ref[...], 1, 1)
    latent = kv_down[:, :RANK]
    latent_ref[...] = latent
    micros, rows, _ = pack.shape
    normal = (latent * rms_scale(latent) * kgain_ref[...]).astype(bf16)
    first = kv_down[:, RANK : RANK + HALF_ROPE]
    second = kv_down[:, RANK + HALF_ROPE : RANK + ROPE]
    cosine, sine = cos_ref[:, :HALF_ROPE], sin_ref[:, :HALF_ROPE]
    turned = (
        (first * cosine - second * sine).astype(bf16),
        (second * cosine + first * sine).astype(bf16),
    )
    for micro in range(micros):
        span = slice(micro * rows, (micro + 1) * rows)
        pack[micro, :, :RANK] = normal[span]
        pack[micro, :, RANK : RANK + HALF_ROPE] = turned[0][span]
        pack[micro, :, RANK + HALF_ROPE : RANK + ROPE] = turned[1][span]
        pack[micro, :, RANK + ROPE :] = jnp.zeros((rows, ROPE), bf16)
    block = lambda k: packs.at[:, k * rows : (k + 1) * rows]
    for k in (1, 2, 3):
        sems.push(pack, block(k), k - 1, place.along(k))

    count = mat_ref.shape[0] // size
    held = None
    for t in range(count):
        fetch(t).wait()
        if t + 1 < count:
            fetch(t + 1).start()
        value = dot(ha, tiles[t % 2], 1, 1)
        if t < count - 2:
            q_ref[:, t * size : (t + 1) * size] = value.astype(bf16)
        elif held is None:
            held = value
        else:
            cosine, sine = cos_ref[...], sin_ref[...]
            q_ref[:, (t - 1) * size : t * size] = (held * cosine - value * sine).astype(bf16)
            q_ref[:, t * size : (t + 1) * size] = (value * cosine + held * sine).astype(bf16)

    for k in (1, 2, 3):
        sems.arrived(block(k), k - 1, place.along(4 - k))
    for micro in range(micros):
        for k in range(4):
            span = slice(k * rows, (k + 1) * rows)
            part = pack[micro] if k == 0 else packs[micro, span]
            lat_ref[micro, span] = part[:, :RANK]
            for ref, start in ((k1_ref, RANK), (k2_ref, RANK + HALF_ROPE)):
                lanes32 = part[:, start : start + HALF_ROPE]
                ref[micro, span] = jnp.concatenate([lanes32] * HEAD_GROUP, axis=1)
    sems.drain()


def front(x, again, kgain, kr, cosine, sine, mat, micros):
    toks, wide = x.shape
    length = 4 * (toks // micros)
    shape = jax.ShapeDtypeStruct
    vm, dma = pltpu.VMEM, pltpu.SemaphoreType.DMA
    size = HEADS * HALF_ROPE
    packed = RANK + 2 * ROPE
    vmem = pl.BlockSpec(memory_space=pltpu.VMEM)
    return pl.pallas_call(
        front_kernel,
        in_specs=[vmem] * 6 + [pl.BlockSpec(memory_space=HBM)],
        out_specs=[vmem] * 6,
        out_shape=[
            shape((toks, wide), bf16),
            shape((toks, RANK), f32),
            shape((toks, mat.shape[0]), bf16),
            shape((micros, length, RANK), bf16),
            shape((micros, length, GROUP_LANES), bf16),
            shape((micros, length, GROUP_LANES), bf16),
        ],
        scratch_shapes=[
            vm((2, size, wide), bf16),
            vm((micros, toks // micros, packed), bf16),
            vm((micros, length, packed), bf16),
            dma((3,)),
            dma((3,)),
            dma((2,)),
        ],
        compiler_params=pltpu.CompilerParams(
            collective_id=9, has_side_effects=True, vmem_limit_bytes=40 << 20
        ),
        name="front",
    )(x, again, kgain, kr, cosine, sine, mat)


def swap_kernel(count, axes, *refs):
    ins, outs, buffers = (refs[n * count : (n + 1) * count] for n in range(3))
    send, recv, local = refs[3 * count :]
    place = Place()
    sems = Sems(send, recv)
    greet([place.peer])

    def cut(i, core):
        if axes[i] is None:
            return ins[i]
        n = ins[i].shape[axes[i]] // 2
        if axes[i] == 0:
            return ins[i].at[rows16(core * n, n)]
        return ins[i].at[:, lanes(core * n, n)]

    for i in range(count):
        sems.push(cut(i, 1 - place.core), outs[i].at[1], sems.slot(), place.peer)
    kept = [
        Through(cut(i, place.core), buffers[i], outs[i].at[0], local.at[i]) for i in range(count)
    ]
    for copy in kept:
        copy.start()
    for copy in kept:
        copy.turn()
    for i in range(count):
        sems.arrived(outs[i].at[1], i, place.peer)
    sems.drain()
    for copy in kept:
        copy.wait()


def core_swap(arrays, axes, fast, ident):
    count = len(arrays)
    if not fast:
        reps = lax.axis_size("rep")
        core = lax.axis_index("rep") % 2
        res = []
        for a, axis in zip(arrays, axes):
            keep = give = a
            if axis is not None:
                n = a.shape[axis] // 2
                keep = lax.dynamic_slice_in_dim(a, core * n, n, axis)
                give = lax.dynamic_slice_in_dim(a, (1 - core) * n, n, axis)
            got = lax.ppermute(give, "rep", [(i, i + 1 - 2 * (i % 2)) for i in range(reps)])
            res.append(jnp.stack([keep, got]))
        return res
    shapes = [
        tuple(n // 2 if d == axis else n for d, n in enumerate(a.shape))
        for a, axis in zip(arrays, axes)
    ]
    return pl.pallas_call(
        functools.partial(swap_kernel, count, axes),
        in_specs=[pl.BlockSpec(memory_space=HBM)] * count,
        out_specs=[pl.BlockSpec(memory_space=HBM)] * count,
        out_shape=[jax.ShapeDtypeStruct((2,) + s, a.dtype) for s, a in zip(shapes, arrays)],
        scratch_shapes=[pltpu.VMEM(s, a.dtype) for s, a in zip(shapes, arrays)]
        + [
            pltpu.SemaphoreType.DMA((count,)),
            pltpu.SemaphoreType.DMA((count,)),
            pltpu.SemaphoreType.DMA((count,)),
        ],
        compiler_params=pltpu.CompilerParams(
            collective_id=ident, has_side_effects=True, vmem_limit_bytes=32 << 20
        ),
        name="core_swap",
    )(*arrays)


def add_rows(dst, terms):
    lead = dst.shape[:-2]
    rows = max(n for n in (16, 32, 48, 64, 80) if dst.shape[-2] % n == 0)
    steps = dst.shape[-2] // rows

    def body(step, carry):
        span = pl.ds(pl.multiple_of(step * rows, rows), rows)
        where = (slice(None),) * len(lead) + (span,)
        total = terms[0][where].astype(f32)
        for t in terms[1:]:
            total = total + t[where].astype(f32)
        dst[where] = total.astype(dst.dtype)
        return carry

    lax.fori_loop(0, steps, body, 0)


def reduce_anywhere(q, kr, kvb, out, sh, ex, gain):
    core = lax.axis_index("rep") % 2

    def whole(g, axis):
        wide = jnp.zeros(g.shape[:axis] + (g.shape[axis] * 2,) + g.shape[axis + 1 :], f32)
        return lax.dynamic_update_slice_in_dim(wide, g.astype(f32), core * g.shape[axis], axis)

    def total(g, axis, along):
        g = lax.psum_scatter(whole(g, axis), "shard", scatter_dimension=along, tiled=True)
        return lax.psum(g, "rep")

    return (
        total(q, 0, 1),
        total(kr, 0, 1),
        total(kvb, 1, 0),
        total(out, 1, 0),
        total(sh, 2, 1),
        lax.psum(whole(ex, 2), "rep"),
        lax.psum(lax.psum_scatter(gain, "shard", scatter_dimension=0, tiled=True), "rep")[0],
    )


class Unit:
    def __init__(self, job, name, u, axis, part, got1, got2, own=None, home=None, got3=None, last=None):
        self.job, self.name, self.u = job, name, u
        self.axis, self.other = axis, "y" if axis == "x" else "x"
        self.part, self.got1, self.got2, self.own = part, got1, got2, own
        self.home, self.got3, self.last = home, got3, last
        self.slots = [job.sems.slot() for _ in range(4)]

    def stage1(self):
        job = self.job
        place = job.place
        for n, chip in enumerate((self.axis, "xy")):
            job.sems.push(
                self.part(place.chips[chip]), self.got1.at[n], self.slots[n], place.across[self.axis]
            )

    def stage2(self):
        place = self.job.place
        if self.own is not None:
            ring, sem = self.own
            self.loads = [
                pltpu.make_async_copy(
                    self.part(place.chips["" if n == 0 else self.other]), ring.at[n], sem.at[n]
                )
                for n in (0, 1)
            ]
            for copy in self.loads:
                copy.start()
            self.mine = [ring.at[0], ring.at[1]]
        else:
            self.mine = [self.part(place.chips[""]), self.part(place.chips[self.other])]

    def stage3(self):
        sems, place = self.job.sems, self.job.place
        for n in (1, 0):
            if self.own is not None:
                self.loads[n].wait()
            sems.arrived(self.got1.at[n], self.slots[n], place.across[self.axis])
            add_rows(self.got1.at[n], [self.got1.at[n], self.mine[n]])
            if n == 1:
                sems.push(self.got1.at[1], self.got2, self.slots[2], place.across[self.other])

    def stage4(self):
        sems, place = self.job.sems, self.job.place
        sems.arrived(self.got2, self.slots[2], place.across[self.other])
        add_rows(self.got1.at[0], [self.got1.at[0], self.got2])
        if self.home:
            sems.push(self.got1.at[0], self.got3.at[self.home - 1], self.slots[3], place.along(self.home))

    def stage5(self):
        if self.last is None:
            return
        job = self.job
        place = job.place
        for unit in job.units:
            if unit.name == self.name and unit.home:
                got = unit.got3.at[unit.home - 1]
                job.sems.arrived(got, unit.slots[3], place.along(4 - unit.home))
        if self.got3 is not None:
            add_rows(self.got1.at[0], [self.got1.at[0]] + [self.got3.at[n] for n in range(3)])
        src, part, half, sem, by = self.last
        self.stay = pltpu.make_async_copy(src, part(place.core, place.chip), sem)
        self.stay.start()
        self.spread = PlaneGather(job.sems, place, part, half, by)
        self.spread.first(src)

    def stage6(self):
        if self.last is not None:
            self.spread.second()

    def stage7(self):
        if self.last is not None:
            self.stay.wait()
            self.spread.third()

    def stage8(self):
        if self.last is not None:
            self.spread.fourth()


class Pump:
    LAGS = (0, 4, 2, 3, 2, 1, 1, 1)

    def __init__(self, place, sems):
        self.place, self.sems = place, sems
        self.units = []
        self.at = [0] * 8

    def tick(self, flush=False):
        for n in range(8):
            ahead = len(self.units) if n == 0 else self.at[n - 1]
            if self.at[n] < ahead - (0 if flush else self.LAGS[n]):
                getattr(self.units[self.at[n]], "stage%d" % (n + 1))()
                self.at[n] += 1

    def ahead(self, count):
        for _ in range(min(count, len(self.units) - self.at[0])):
            self.units[self.at[0]].stage1()
            self.at[0] += 1

    def run(self, count):
        for _ in range(count):
            self.tick()

    def end(self):
        while self.at[-1] < len(self.units):
            before = list(self.at)
            self.tick()
            if self.at == before:
                self.tick(True)


BACK_IN = (
    "gsh",
    "gex",
    "gout",
    "q",
    "kvb",
    "kq",
    "kkr",
    "x",
    "mid",
    "lat",
    "k1",
    "k2",
    "seen",
    "do",
    "ha",
    "latent",
    "kgain",
    "again",
    "fgain",
    "cos",
    "sin",
    "rtr",
)
BACK_HBM = 9
BACK_OUT = (
    "oq",
    "okr",
    "okvb",
    "oout",
    "osh",
    "osd",
    "oex",
    "zsh",
    "ogain",
    "ograd",
)
BACK_SLOTS = 3 + 3 + 5 + 10 + 28 * 4 + 7 * 4
EARLY = 2


def back_kernel(scale, names, *refs):
    r = dict(zip(names, refs))
    place = Place()
    sems = Sems(r["send"], r["recv"])
    others = [place.peer]
    for axes in ("x", "y", "xy"):
        for flip in (place.core, 1 - place.core):
            others.append((place.chips[axes] * 2 + flip, place.z))
    greet(others + [place.along(k) for k in (1, 2, 3)])
    load = r["load"]
    pump = Pump(place, sems)
    core = place.core
    toks = r["ha"].shape[0]
    rows = toks // 2

    ff = r["gsh"].shape[1] // 4
    shared_slots = [sems.slot() for _ in range(3)]
    for k in (1, 2, 3):
        sems.push(
            r["gsh"].at[:EARLY, k * ff : (k + 1) * ff], r["zsh"].at[k - 1], shared_slots[k - 1], place.along(4 - k)
        )
    swap = {name: sems.slot() for name in ("ha", "kvb", "q", "kvd", "rtr")}
    sems.push(r["ha"], r["s_ha"], swap["ha"], place.peer)
    sems.push(r["rtr"], r["s_rtr"], swap["rtr"], place.peer)
    begin = [
        pltpu.make_async_copy(r["q"], r["qs"], load.at[0]),
        pltpu.make_async_copy(r["kvb"], r["kvbs"], load.at[1]),
    ]
    for copy in begin:
        copy.start()

    def out_split(o, by_rows):
        if by_rows:
            half = o.shape[0] // 2
            n = half // 4
            return (
                lambda c, chip: o.at[rows16(c * half + chip * n, n)],
                lambda c: o.at[rows16(c * half, half)],
            )
        half = o.shape[-1] // 2
        n = half // 4
        lead = (slice(None),) * (len(o.shape) - 1)
        return (
            lambda c, chip: o.at[(*lead, lanes(c * half + chip * n, n))],
            lambda c: o.at[(*lead, lanes(c * half, half))],
        )

    rings = 0

    def ring(shape_ref):
        nonlocal rings
        slot = rings % 4
        rings += 1
        return slot

    def add_matrices(name, source, count, out, by, ringed):
        for u in range(count):
            n = source.shape[-1] // 4
            own = None
            if ringed:
                slot = ring(None)
                own = (r["ring_" + name].at[slot], r["ringsem"].at[slot])
            last = None
            if u == count - 1:
                last = (r["got1_" + name].at[:, 0], *out_split(out, False), r["keep"].at[len(pump.units) % 8], by)
            pump.units.append(
                Unit(
                    pump,
                    name,
                    u,
                    "x" if u % 2 == 0 else "y",
                    lambda chip, u=u: source.at[u, :, lanes(chip * n, n)],
                    r["got1_" + name].at[u],
                    r["got2_" + name].at[u],
                    own=own,
                    last=last,
                )
            )

    def add_sharded(name, part_of, out, by_rows, by, ringed=None):
        for n, k in enumerate((1, 2, 3, 4)):
            u, s = k % 4, place.shard_at(k)
            own = None
            if ringed:
                slot = ring(None)
                own = (r["ring_" + ringed].at[slot], r["ringsem"].at[slot])
            last = None
            if k == 4:
                last = (r["got1_" + name].at[0, 0], *out_split(out, by_rows), r["keep"].at[len(pump.units) % 8], by)
            pump.units.append(
                Unit(
                    pump,
                    name,
                    u,
                    "x" if n % 2 == 0 else "y",
                    lambda chip, s=s, k=k: part_of(s, k, chip),
                    r["got1_" + name].at[u],
                    r["got2_" + name].at[u],
                    own=own,
                    home=k % 4,
                    got3=r["got3_" + name],
                    last=last,
                )
            )

    add_matrices("ex", r["gex"], r["gex"].shape[0], r["oex"], "x", True)
    block = r["gout"].shape[0] // 4
    n_out = r["gout"].shape[1] // 4
    add_sharded(
        "out",
        lambda s, k, chip: r["gout"].at[rows16(s * block, block), lanes(chip * n_out, n_out)],
        r["oout"],
        False,
        "y",
        "out",
    )
    n_sd = r["gsh"].shape[2] // 4
    add_sharded(
        "sd",
        lambda s, k, chip: r["gsh"].at[
            EARLY, (4 - k) % 4 * ff : ((4 - k) % 4 + 1) * ff, lanes(chip * n_sd, n_sd)
        ],
        r["osd"],
        False,
        "x",
        "ex",
    )
    pump.ahead(4)
    for copy in begin:
        copy.wait()

    qs, kvbs, kvg, acc, dlat, dkvb = (r[n] for n in ("qs", "kvbs", "kvg", "acc", "dlat", "dkvb"))
    n1 = HEADS * NOPE
    n2 = HEADS * (NOPE + HALF_ROPE)
    width = NOPE + VDIM
    lane = lax.broadcasted_iota(jnp.int32, (1, GROUP_LANES), 1)

    def attention_step(group, micro):
        span = slice(micro * rows, (micro + 1) * rows)
        at = group * GROUP_LANES
        lat, k1, k2 = r["lat"][micro], r["k1"][micro], r["k2"][micro]
        q1, q2 = qs[span, n1 + at : n1 + at + GROUP_LANES], qs[span, n2 + at : n2 + at + GROUP_LANES]
        dq1 = jnp.zeros(q1.shape, f32)
        dq2 = jnp.zeros(q2.shape, f32)
        dk1 = jnp.zeros(k1.shape, f32)
        dk2 = jnp.zeros(k2.shape, f32)
        for pair in (0, 1):
            cols = slice((group * 4 + pair * 2) * width, (group * 4 + pair * 2 + 2) * width)
            weight = kvbs[:, cols]
            kv = dot(lat, weight, 1, 0).astype(bf16)
            for n in (0, 1):
                head = pair * 2 + n
                here = slice((group * 4 + head) * NOPE, (group * 4 + head + 1) * NOPE)
                mine = (lane >= head * HALF_ROPE) & (lane < (head + 1) * HALF_ROPE)
                q_head = qs[span, here]
                k_head = kv[:, n * width : n * width + NOPE]
                v_head = kv[:, n * width + NOPE : (n + 1) * width]
                q1m = jnp.where(mine, q1, jnp.zeros_like(q1))
                q2m = jnp.where(mine, q2, jnp.zeros_like(q2))
                scores = dot(q_head, k_head, 1, 1) + dot(q1m, k1, 1, 1) + dot(q2m, k2, 1, 1)
                scores = jnp.where(r["seen"][...] > 0.0, scores * scale, masked_score)
                expo = jnp.exp(scores - jnp.max(scores, axis=-1, keepdims=True))
                probs = expo / jnp.sum(expo, axis=-1, keepdims=True)
                d_out = r["do"][micro, :, here]
                dprobs = dot(d_out, v_head, 1, 1)
                delta = jnp.sum(probs * dprobs, axis=-1, keepdims=True)
                ds = (probs * (dprobs - delta)).astype(bf16)
                qs[span, here] = (dot(ds, k_head, 1, 0) * scale).astype(bf16)
                dq1 = dq1 + jnp.where(mine, dot(ds, k1, 1, 0), 0.0)
                dq2 = dq2 + jnp.where(mine, dot(ds, k2, 1, 0), 0.0)
                dk1 = dk1 + dot(ds, q1m, 0, 0)
                dk2 = dk2 + dot(ds, q2m, 0, 0)
                kvg[:, n * width : n * width + NOPE] = (dot(ds, q_head, 0, 0) * scale).astype(bf16)
                kvg[:, n * width + NOPE : (n + 1) * width] = dot(
                    probs.astype(bf16), d_out, 0, 0
                ).astype(bf16)
            terms = kvg[...]
            if group == 0 and pair == 0:
                dlat[micro] = dot(terms, weight, 1, 1)
            else:
                dlat[micro] += dot(terms, weight, 1, 1)
            part = dot(lat, terms, 0, 0)
            hold = slice(pair * 2 * width, (pair + 1) * 2 * width)
            if micro == 0:
                acc[:, hold] = part
            else:
                dkvb[:, cols] = (acc[:, hold] + part).astype(bf16)
        dq1, dq2 = dq1 * scale, dq2 * scale
        cosine, sine = r["cos"][...], r["sin"][...]
        qs[span, n1 + at : n1 + at + GROUP_LANES] = (dq1 * cosine + dq2 * sine).astype(bf16)
        qs[span, n2 + at : n2 + at + GROUP_LANES] = (dq2 * cosine - dq1 * sine).astype(bf16)
        for ref, value in ((r["dk1"], dk1), (r["dk2"], dk2)):
            if group == 0:
                ref[micro] = value * scale
            else:
                ref[micro] += value * scale

    for group in range(HEADS // HEAD_GROUP):
        for micro in (0, 1):
            attention_step(group, micro)
            pump.run(1)

    pack, zs = r["pack"], r["zs"]
    fold = lambda t: sum(t[:, n * HALF_ROPE : (n + 1) * HALF_ROPE] for n in range(HEAD_GROUP))
    for micro in (0, 1):
        pack[micro, :, :RANK] = dlat[micro].astype(bf16)
        pack[micro, :, RANK : RANK + HALF_ROPE] = fold(r["dk1"][micro]).astype(bf16)
        pack[micro, :, RANK + HALF_ROPE : RANK + ROPE] = fold(r["dk2"][micro]).astype(bf16)
        pack[micro, :, RANK + ROPE :] = jnp.zeros((pack.shape[1], ROPE), bf16)
    z_slots = [sems.slot() for _ in range(3)]
    for k in (1, 2, 3):
        sems.push(pack.at[:, k * rows : (k + 1) * rows], zs.at[k - 1], z_slots[k - 1], place.along(4 - k))
    half_q, half_kvb = qs.shape[1] // 2, dkvb.shape[1] // 2
    sems.push(qs.at[:, lanes((1 - core) * half_q, half_q)], r["s_q"], swap["q"], place.peer)
    kvb_push = sems.push(
        dkvb.at[:, lanes((1 - core) * half_kvb, half_kvb)], r["s_kvb"], swap["kvb"], place.peer
    )
    pump.run(1)

    sems.arrived(r["s_kvb"], swap["kvb"], place.peer)
    add_rows(r["s_kvb"], [r["s_kvb"], dkvb.at[:, lanes(core * half_kvb, half_kvb)]])
    n_kvb, b_kvb = half_kvb // 4, dkvb.shape[0] // 4
    add_sharded(
        "kvb",
        lambda s, k, chip: r["s_kvb"].at[rows16(s * b_kvb, b_kvb), lanes(chip * n_kvb, n_kvb)],
        r["okvb"],
        False,
        "x",
    )
    sems.arrived(r["s_ha"], swap["ha"], place.peer)
    sems.arrived(r["s_q"], swap["q"], place.peer)
    gq, ha, s_ha = r["gq"], r["ha"], r["s_ha"]

    def q_tile(t, carry):
        own = qs[:, lanes(core * half_q + t * 128, 128)]
        got = r["s_q"][:, lanes(t * 128, 128)]
        gq[rows16(t * 128, 128)] = (dot(own, ha[...], 0, 0) + dot(got, s_ha[...], 0, 0)).astype(bf16)
        return carry

    for part in range(4):
        lax.fori_loop(part * 3, part * 3 + 3, q_tile, 0)
        pump.run(1)
    r_q, c_q = gq.shape[0] // 4, gq.shape[1] // 4
    add_sharded(
        "q",
        lambda s, k, chip: gq.at[rows16(chip * r_q, r_q), lanes(s * c_q, c_q)],
        r["oq"],
        True,
        "y",
    )
    pump.run(4)

    for k in (1, 2, 3):
        sems.arrived(zs.at[k - 1], z_slots[k - 1], place.along(k))
    kvd, gains = r["kvd"], r["gains"]
    kv_gain_grad = jnp.zeros((1, RANK), f32)
    for micro in (0, 1):
        span = slice(micro * rows, (micro + 1) * rows)
        total = pack[micro, :rows].astype(f32)
        for k in range(3):
            total = total + zs[k, micro].astype(f32)
        upstream, latent = total[:, :RANK], r["latent"][span]
        inv = rms_scale(latent)
        scaled = upstream * r["kgain"][...]
        inner = jnp.mean(scaled * latent, axis=-1, keepdims=True)
        kvd[span, :RANK] = (inv * scaled - latent * (inv * inv * inv) * inner).astype(bf16)
        kv_gain_grad = kv_gain_grad + jnp.sum(upstream * latent * inv, axis=0, keepdims=True)
        g1, g2 = total[:, RANK : RANK + HALF_ROPE], total[:, RANK + HALF_ROPE : RANK + ROPE]
        cosine, sine = r["cos"][:, :HALF_ROPE], r["sin"][:, :HALF_ROPE]
        kvd[span, RANK : RANK + HALF_ROPE] = (g1 * cosine + g2 * sine).astype(bf16)
        kvd[span, RANK + HALF_ROPE : RANK + ROPE] = (g2 * cosine - g1 * sine).astype(bf16)
        kvd[span, RANK + ROPE :] = jnp.zeros((rows, ROPE), bf16)
    sems.push(kvd, r["s_kvd"], swap["kvd"], place.peer)

    tile = 384
    tiles = [("kq", t * tile, tile) for t in range(qs.shape[1] // tile)]
    tiles += [("kkr", 0, tile), ("kkr", tile, r["kkr"].shape[0] - tile)]
    wide = ha.shape[1]
    half_w = wide // 2

    def fetch(t):
        name, start, n = tiles[t]
        return pltpu.make_async_copy(
            r[name].at[start : start + n],
            kvbs.at[:n, (t % 2) * wide : (t % 2 + 1) * wide],
            load.at[2 + t % 2],
        )

    fetch(0).start()
    for t, (name, start, n) in enumerate(tiles):
        fetch(t).wait()
        if t + 1 < len(tiles):
            fetch(t + 1).start()
        left = (qs if name == "kq" else kvd)[:, start : start + n]
        for half in (0, 1):
            base = (t % 2) * wide + half * half_w
            value = dot(left, kvbs[:n, base : base + half_w], 1, 0)
            where = slice(half * toks, (half + 1) * toks)
            if t == 0:
                acc[where] = value
            else:
                acc[where] += value
        if t % 2 == 1:
            pump.run(1)

    for k in (1, 2, 3):
        sems.arrived(r["zsh"].at[k - 1], shared_slots[k - 1], place.along(k))
    cols = r["gsh"].shape[2]
    for j in range(EARLY):
        copies = [pltpu.make_async_copy(r["gsh"].at[j, :ff], kvbs.at[:ff, :cols], load.at[6])]
        for k in range(3):
            copies.append(
                pltpu.make_async_copy(
                    r["zsh"].at[k, j], kvbs.at[:ff, (k + 1) * cols : (k + 2) * cols], load.at[7 + k]
                )
            )
        for copy in copies:
            copy.start()
        for copy in copies:
            copy.wait()
        add_rows(r["gshs"].at[j], [kvbs.at[:ff, k * cols : (k + 1) * cols] for k in range(4)])
    add_matrices("sh", r["gshs"], EARLY, r["osh"], "y", False)
    pump.run(2)

    sems.arrived(r["s_kvd"], swap["kvd"], place.peer)
    sems.arrived(r["s_rtr"], swap["rtr"], place.peer)
    sems.settle(kvb_push)
    half_kr = r["kkr"].shape[0] // 2
    r_kr, c_kr = half_kr // 4, wide // 4
    edges = sorted(set(list(range(0, 2 * half_kr + 1, 128)) + [half_kr]))
    for start, stop in zip(edges[:-1], edges[1:]):
        value = dot(kvd[:, start:stop], ha[...], 0, 0)
        value = value + dot(r["s_kvd"][:, start:stop], s_ha[...], 0, 0)
        n = start // half_kr
        if stop == 2 * half_kr:
            first = RANK + ROPE - start
            both = r["rtr"][...].astype(f32) + r["s_rtr"][...].astype(f32)
            value = jnp.concatenate([value[:first], both])
        dkvb[start - n * half_kr : stop - n * half_kr, n * wide : (n + 1) * wide] = value.astype(bf16)
    add_sharded(
        "kr",
        lambda s, k, chip: dkvb.at[rows16(chip * r_kr, r_kr), lanes(core * wide + s * c_kr, c_kr)],
        r["okr"],
        True,
        "x",
    )
    pump.run(2)

    again = r["again"][...]
    attn_gain_grad = jnp.zeros((1, wide), f32)
    step = 32
    for start in range(0, toks, step):
        fetched = [
            pltpu.make_async_copy(r[a].at[start : start + step], r[b], load.at[4 + n])
            for n, (a, b) in enumerate((("x", "xb"), ("mid", "mb")))
        ]
        for copy in fetched:
            copy.start()
        for copy in fetched:
            copy.wait()
        x = r["xb"][...].astype(f32)
        upstream = jnp.concatenate(
            [acc[start : start + step], acc[toks + start : toks + start + step]], axis=1
        )
        inv = rms_scale(x)
        scaled = upstream * again
        inner = jnp.mean(scaled * x, axis=-1, keepdims=True)
        part = inv * scaled - x * (inv * inv * inv) * inner
        r["ograd"][start : start + step] = (r["mb"][...] + part).astype(bf16)
        attn_gain_grad = attn_gain_grad + jnp.sum(upstream * x * inv, axis=0, keepdims=True)
        pump.run(1)
    n_a, n_k = wide // 4, RANK // 4
    gains[...] = jnp.zeros(gains.shape, f32)
    for s in range(4):
        gains[s, 0:1, :n_a] = attn_gain_grad[:, s * n_a : (s + 1) * n_a]
        gains[s, 0:1, n_a : 2 * n_a] = r["fgain"][:, s * n_a : (s + 1) * n_a]
        gains[s, 0:1, 2 * n_a :] = kv_gain_grad[:, s * n_k : (s + 1) * n_k]
    gain_slots = [sems.slot() for _ in range(3 + 7)]
    gz, gp, gs = r["gz"], r["gp"], r["gs"]
    for k in (1, 2, 3):
        sems.push(gains.at[place.shard_at(k)], gz.at[k - 1], gain_slots[k - 1], place.along(k))
    pump.run(2)

    for k in (1, 2, 3):
        sems.arrived(gz.at[k - 1], gain_slots[k - 1], place.along(4 - k))
    gs[...] = gains[place.z] + gz[0] + gz[1] + gz[2]
    for n, device in enumerate(others):
        sems.push(gs, gp.at[n], gain_slots[3 + n], device)
    pump.end()
    total = gs[...]
    for n, device in enumerate(others):
        sems.arrived(gp.at[n], gain_slots[3 + n], device)
        total = total + gp[n]
    r["ogain"][...] = total
    sems.drain()


def back_all(args, scale):
    shape = jax.ShapeDtypeStruct
    gsh, gex, gout, q, kvb, kq, kkr = (args[n] for n in BACK_IN[:7])
    toks, wide = args["ha"].shape
    micros, length, rank = args["lat"].shape
    fe, ff = gex.shape[1], gsh.shape[1] // 4
    rows = toks // micros
    n_a = wide // 4
    gain_shape = (8, 2 * n_a + rank // 4)
    outs = dict(
        oq=shape((q.shape[1], wide // 4), bf16),
        okr=shape((kkr.shape[0], wide // 4), bf16),
        okvb=shape((rank // 4, kvb.shape[1]), bf16),
        oout=shape((gout.shape[0] // 4, wide), bf16),
        osh=shape((EARLY, ff, wide), bf16),
        osd=shape((ff, wide), bf16),
        oex=shape((gex.shape[0], fe, wide), bf16),
        zsh=shape((3, EARLY, ff, wide // 2), bf16),
        ogain=shape(gain_shape, f32),
        ograd=shape((toks, wide), bf16),
    )
    vm = pltpu.VMEM
    parts = dict(
        out=(gout.shape[0] // 4, wide // 8),
        sd=(ff, wide // 8),
        kvb=(rank // 4, kvb.shape[1] // 8),
        q=(q.shape[1] // 8, wide // 4),
        kr=(kkr.shape[0] // 8, wide // 4),
    )
    scratch = dict(
        qs=vm(q.shape, bf16),
        kvbs=vm(kvb.shape, bf16),
        kvg=vm((length, 2 * (NOPE + VDIM)), bf16),
        acc=vm((2 * toks, wide // 2), f32),
        dlat=vm((micros, length, rank), f32),
        dk1=vm((micros, length, GROUP_LANES), f32),
        dk2=vm((micros, length, GROUP_LANES), f32),
        dkvb=vm(kvb.shape, bf16),
        pack=vm((micros, length, rank + 2 * ROPE), bf16),
        zs=vm((3, micros, rows, rank + 2 * ROPE), bf16),
        kvd=vm((toks, rank + 2 * ROPE), bf16),
        s_ha=vm((toks, wide), bf16),
        s_q=vm((toks, q.shape[1] // 2), bf16),
        s_kvb=vm((rank, kvb.shape[1] // 2), bf16),
        s_kvd=vm((toks, rank + 2 * ROPE), bf16),
        s_rtr=vm(args["rtr"].shape, bf16),
        gq=vm((q.shape[1] // 2, wide), bf16),
        gshs=vm((EARLY, ff, wide // 2), bf16),
        xb=vm((32, wide), bf16),
        mb=vm((32, wide), f32),
        gains=vm((4,) + gain_shape, f32),
        gz=vm((3,) + gain_shape, f32),
        gp=vm((7,) + gain_shape, f32),
        gs=vm(gain_shape, f32),
        ring_ex=vm((4, 2, fe, wide // 8), bf16),
        ring_out=vm((4, 2) + parts["out"], bf16),
        got1_ex=vm((gex.shape[0], 2, fe, wide // 8), bf16),
        got2_ex=vm((gex.shape[0], fe, wide // 8), bf16),
        got1_sh=vm((EARLY, 2, ff, wide // 8), bf16),
        got2_sh=vm((EARLY, ff, wide // 8), bf16),
    )
    for name, part in parts.items():
        scratch["got1_" + name] = vm((4, 2) + part, bf16)
        scratch["got2_" + name] = vm((4,) + part, bf16)
        scratch["got3_" + name] = vm((3,) + part, bf16)
    dma = pltpu.SemaphoreType.DMA
    scratch.update(
        send=dma((BACK_SLOTS,)), recv=dma((BACK_SLOTS,)), load=dma((10,)), keep=dma((8,)), ringsem=dma((4, 2))
    )
    names = (*BACK_IN, *BACK_OUT, *scratch)
    hbm, vmem = pl.BlockSpec(memory_space=HBM), pl.BlockSpec(memory_space=pltpu.VMEM)
    res = pl.pallas_call(
        functools.partial(back_kernel, scale, names),
        in_specs=[hbm] * BACK_HBM + [vmem] * (len(BACK_IN) - BACK_HBM),
        out_specs=[hbm if n not in ("ogain", "ograd") else vmem for n in BACK_OUT],
        out_shape=[outs[n] for n in BACK_OUT],
        scratch_shapes=list(scratch.values()),
        compiler_params=pltpu.CompilerParams(
            collective_id=1, has_side_effects=True, vmem_limit_bytes=61 << 20
        ),
        name="back_all",
    )(*(args[n] for n in BACK_IN))
    return dict(zip(BACK_OUT, res))


def head_split(weight):
    per_head = weight.reshape(HEADS, NOPE + ROPE, weight.shape[1])
    cuts = (0, NOPE, NOPE + HALF_ROPE, NOPE + ROPE)
    return jnp.concatenate(
        [per_head[:, a:b].reshape(-1, weight.shape[1]) for a, b in zip(cuts[:-1], cuts[1:])]
    )


def head_join(weight):
    cols = weight.shape[1]
    nope = weight[: HEADS * NOPE].reshape(HEADS, NOPE, cols)
    first = weight[HEADS * NOPE : HEADS * (NOPE + HALF_ROPE)].reshape(HEADS, HALF_ROPE, cols)
    second = weight[HEADS * (NOPE + HALF_ROPE) :].reshape(HEADS, HALF_ROPE, cols)
    return jnp.concatenate([nope, first, second], axis=1).reshape(-1, cols)


def shards(
    tokens,
    attn_gain,
    q_weight,
    kva_weight,
    kv_gain,
    kvb_weight,
    out_weight,
    ffn_gain,
    router_weight,
    shared_gate,
    shared_up,
    shared_down,
    expert_gate,
    expert_up,
    expert_down,
    expert_ids,
    cotangent,
):
    shard_count = lax.axis_size("shard")
    shard_index = lax.axis_index("shard")
    core = lax.axis_index("rep") % 2
    fast = lax.axis_size("rep") == 8 and shard_count == 4
    micros, rows, width = tokens.shape
    toks = micros * rows
    scale = (NOPE + ROPE) ** (-0.5)
    ga, gk = attn_gain.shape[0], kv_gain.shape[0]

    gain_pack = jnp.concatenate([attn_gain, ffn_gain, kv_gain]).astype(bf16)
    gain_pack = jnp.broadcast_to(gain_pack[None], (16, gain_pack.shape[0]))
    sh_own = jnp.stack([shared_gate, shared_up, shared_down]).astype(bf16)
    query_mat, kr_mat, kvb_mat, out_mat, sh_rest, gains = gather_weights(
        head_split(q_weight).astype(bf16),
        jnp.concatenate([kva_weight, router_weight]).astype(bf16),
        kvb_weight.astype(bf16),
        out_weight.astype(bf16),
        sh_own,
        gain_pack,
        fast,
    )
    gain_rows = gains[:, 0].astype(f32)
    attn_gain_f = gain_rows[:, :ga].reshape(-1)
    ffn_gain_f = gain_rows[:, ga : 2 * ga].reshape(-1)
    kv_gain_f = gain_rows[:, 2 * ga :].reshape(-1)
    kv_down_mat, router_mat = kr_mat[: RANK + ROPE], kr_mat[RANK + ROPE :]
    sh_mats = [sh_own, sh_rest] if fast else [sh_rest]

    def hidden(t, index):
        return jnp.concatenate([dot(t, m[index], 1, 1) for m in sh_mats], axis=1)

    def unhidden(t, index):
        at, total = 0, 0.0
        for m in sh_mats:
            total = total + dot(t[:, at : at + m.shape[1]], m[index], 1, 0)
            at += m.shape[1]
        return total


    x_in = tokens.reshape(toks, width).astype(f32)
    positions = (shard_index * rows + jnp.arange(rows, dtype=jnp.int32)).astype(f32)
    frequency = jnp.exp(
        -jnp.log(rope_base) * (2.0 * jnp.arange(HALF_ROPE, dtype=f32) / ROPE)
    )
    angles = positions[:, None] * frequency[None, :]
    cosine = jnp.tile(jnp.cos(angles), (micros, 1))
    sine = jnp.tile(jnp.sin(angles), (micros, 1))
    cos_all, sin_all = jnp.tile(cosine, (1, HEADS)), jnp.tile(sine, (1, HEADS))
    n1, n2 = HEADS * NOPE, HEADS * (NOPE + HALF_ROPE)
    by_micro = lambda t: t.reshape(micros, rows, t.shape[-1])
    row = lambda t: t.reshape(1, -1)
    if fast:
        h_attn, latent, q_all, lat_all, k1, k2 = front(
            tokens.reshape(toks, width),
            row(attn_gain_f),
            row(kv_gain_f),
            kr_mat,
            cos_all,
            sin_all,
            query_mat,
            micros,
        )
        length = lat_all.shape[1]
    else:
        inv_one = rms_scale(x_in)
        h_attn = (x_in * inv_one * attn_gain_f).astype(bf16)
        q_raw = dot(h_attn, query_mat, 1, 1)
        q_first, q_second = q_raw[:, n1:n2], q_raw[:, n2:]
        qn = by_micro(q_raw[:, :n1].astype(bf16))
        q1 = by_micro((q_first * cos_all - q_second * sin_all).astype(bf16))
        q2 = by_micro((q_second * cos_all + q_first * sin_all).astype(bf16))
        kv_down = dot(h_attn, kv_down_mat, 1, 1)
        latent = kv_down[:, :RANK]
        inv_kv = rms_scale(latent)
        latent_norm = (latent * inv_kv * kv_gain_f).astype(bf16)
        k_first, k_second = kv_down[:, RANK : RANK + HALF_ROPE], kv_down[:, RANK + HALF_ROPE :]
        latent_pack = jnp.concatenate(
            [
                latent_norm,
                (k_first * cosine - k_second * sine).astype(bf16),
                (k_second * cosine + k_first * sine).astype(bf16),
                jnp.zeros((toks, ROPE), bf16),
            ],
            axis=-1,
        )
        packs = z_all(by_micro(latent_pack), fast)
        length = packs.shape[1]
        lat_all = packs[..., :RANK]
        k1 = jnp.tile(packs[..., RANK : RANK + HALF_ROPE], (1, 1, HEAD_GROUP))
        k2 = jnp.tile(packs[..., RANK + HALF_ROPE : RANK + ROPE], (1, 1, HEAD_GROUP))
    key_shard = jnp.arange(length, dtype=jnp.int32) // rows
    if fast:
        key_shard = (shard_index - key_shard) % 4
    key_block = (key_shard * rows + jnp.arange(length, dtype=jnp.int32) % rows) // MASK_BLOCK
    seen = (key_block <= (shard_index * rows) // MASK_BLOCK).astype(f32).reshape(1, length)
    if fast:
        attended = attend_packed(seen, by_micro(q_all), lat_all, k1, k2, kvb_mat, scale)
    else:
        attended = attend(seen, qn, q1, q2, lat_all, k1, k2, kvb_mat, scale)
    attended = attended.reshape(toks, -1)

    x_mid = x_in + dot(attended, out_mat, 1, 0)
    inv_two = rms_scale(x_mid)
    h_ffn = (x_mid * inv_two * ffn_gain_f).astype(bf16)
    router_probs = jax.nn.softmax(dot(h_ffn, router_mat, 1, 1), axis=-1)
    grad_b = cotangent.reshape(toks, width)

    member = jnp.any(
        expert_ids[:, :, None, :] == jnp.arange(EXP_WIN, dtype=jnp.int32)[None, None, :, None], axis=-1
    ).astype(jnp.int32)
    placed = jnp.cumsum(member, axis=1) - 1
    hits = (member[:, :, :, None] == 1) & (
        placed[:, :, :, None] == jnp.arange(CAP, dtype=jnp.int32)
    )
    select = jnp.transpose(hits, (2, 0, 3, 1)).astype(f32)
    select_b = select.astype(bf16)
    h3, c3 = by_micro(h_ffn), by_micro(grad_b)
    gather_slots = lambda t: jnp.einsum(
        "emct,mtd->emcd", select_b, t, preferred_element_type=f32
    ).astype(bf16)
    flat = lambda t: t.reshape(EXP_WIN, micros * CAP, t.shape[-1])
    tall = lambda t: t.reshape(-1, t.shape[-1])
    picked_all = z_all(flat(gather_slots(c3)), fast)
    rows_all = z_all(flat(gather_slots(h3)), fast)

    gate_pre, up_pre = hidden(h_ffn, 0), hidden(h_ffn, 1)
    shared_hidden = (jax.nn.silu(gate_pre) * up_pre).astype(bf16)
    shared_hidden_grad = hidden(grad_b, 2)
    gate_grad_b, up_grad_b = swiglu_back(gate_pre, up_pre, shared_hidden_grad)
    sh_s, hf_s, cot_s = core_swap(
        [jnp.concatenate([gate_grad_b, up_grad_b, shared_hidden], axis=1), h_ffn, grad_b],
        (None, 1, 1),
        fast,
        7,
    )
    ff = shared_hidden.shape[1]
    sh_s, hf_s, cot_s = tall(sh_s), tall(hf_s), tall(cot_s)
    grad_sh = jnp.stack(
        [
            dot(sh_s[:, :ff], hf_s, 0, 0).astype(bf16),
            dot(sh_s[:, ff : 2 * ff], hf_s, 0, 0).astype(bf16),
            dot(sh_s[:, 2 * ff :], cot_s, 0, 0).astype(bf16),
        ]
    )
    picked_all = picked_all.astype(f32)
    slot_probs = jax.nn.softmax(
        jnp.einsum("end,xd->enx", rows_all, router_mat, preferred_element_type=f32), axis=-1
    )
    gates_all = jnp.stack([slot_probs[e, :, e] for e in range(EXP_WIN)])[..., None]
    dy_all = (gates_all * picked_all).astype(bf16)
    eg, eu, ed = expert_gate.astype(bf16), expert_up.astype(bf16), expert_down.astype(bf16)
    bdot = lambda a, b, ca, cb: lax.dot_general(
        a, b, (((ca,), (cb,)), ((0,), (0,))), preferred_element_type=f32
    )
    expert_pre = bdot(rows_all, eg, 2, 2)
    expert_upv = bdot(rows_all, eu, 2, 2)
    expert_hidden = (jax.nn.silu(expert_pre) * expert_upv).astype(bf16)
    expert_part = bdot(expert_hidden, ed, 2, 1)
    gate_part = jnp.sum(picked_all * expert_part, axis=-1, keepdims=True)
    gate_high = gate_part.astype(bf16)
    gate_low = (gate_part - gate_high.astype(f32)).astype(bf16)
    expert_hidden_grad = bdot(dy_all, ed, 2, 2)
    expert_gate_b, expert_up_b = swiglu_back(expert_pre, expert_upv, expert_hidden_grad)
    slot_part = (bdot(expert_gate_b, eg, 2, 1) + bdot(expert_up_b, eu, 2, 1)).astype(bf16)
    slot_part = jnp.concatenate(
        [slot_part, gate_high, gate_low, jnp.zeros(slot_part.shape[:2] + (126,), bf16)], axis=-1
    )
    slot_back = z_home(slot_part, fast)
    expert_back = z_home(expert_part.astype(bf16), fast)

    ex_s, row_s, dy_s = core_swap(
        [
            tall(jnp.concatenate([expert_gate_b, expert_up_b, expert_hidden], axis=-1)),
            tall(rows_all),
            tall(dy_all),
        ],
        (None, 1, 1),
        fast,
        8,
    )
    fe = expert_hidden.shape[-1]
    by_expert = lambda t: t.reshape(2, EXP_WIN, -1, t.shape[-1])
    ex_s, row_s, dy_s = by_expert(ex_s), by_expert(row_s), by_expert(dy_s)
    edot = lambda a, b: jnp.einsum("senf,send->efd", a, b, preferred_element_type=f32).astype(bf16)
    grad_ex = jnp.concatenate(
        [
            edot(ex_s[..., :fe], row_s),
            edot(ex_s[..., fe : 2 * fe], row_s),
            edot(ex_s[..., 2 * fe :], dy_s),
        ]
    )
    ffn_grad = unhidden(gate_grad_b, 0) + unhidden(up_grad_b, 1)
    back = lambda t: t.reshape(EXP_WIN, micros, CAP, t.shape[-1])
    slot_grad = back(slot_back[..., :width])
    gate_weight_grad = back(slot_back[..., width : width + 2]).sum(axis=-1)
    ffn_grad = ffn_grad + jnp.einsum(
        "emct,emcd->mtd", select, slot_grad, precision=highest
    ).reshape(toks, width)
    probs_grad = jnp.einsum("emct,emc->mte", select, gate_weight_grad, precision=highest)
    probs_grad = jnp.pad(
        probs_grad.reshape(toks, EXP_WIN), ((0, 0), (0, EXPERTS - EXP_WIN))
    )
    logit_grad = (
        router_probs * (probs_grad - jnp.sum(router_probs * probs_grad, axis=-1, keepdims=True))
    ).astype(bf16)
    ffn_grad = ffn_grad + dot(logit_grad, router_mat, 1, 0)
    mid_part, ffn_gain_grad = norm_back(x_mid, inv_two, ffn_gain_f, ffn_grad)
    mid_grad = grad_b.astype(f32) + mid_part
    attn_out_grad = mid_grad.astype(bf16)
    attended_grad = by_micro(dot(attn_out_grad, out_mat, 1, 1).astype(bf16))

    att_s, og_s = core_swap([attended, attn_out_grad], (None, 1), fast, 2)
    grad_out = dot(tall(att_s), tall(og_s), 0, 0).astype(bf16)
    expert_out = back(expert_back)
    slot_gates = jnp.einsum(
        "emct,mte->emc", select, by_micro(router_probs)[..., :EXP_WIN], precision=highest
    )
    routed = jnp.einsum("emct,emcd->mtd", select, slot_gates[..., None] * expert_out, precision=highest)
    layer_output = x_mid + unhidden(shared_hidden, 2) + routed.reshape(toks, width)
    layer_output = layer_output.astype(bf16)

    lane_rows = lambda t: t.reshape(shard_count, -1)
    if fast:
        group_tab = lambda t: jnp.tile(t[:rows], (1, HEAD_GROUP))
        res = back_all(
            dict(
                gsh=grad_sh,
                gex=grad_ex,
                gout=grad_out,
                q=q_all,
                kvb=kvb_mat,
                kq=query_mat,
                kkr=kr_mat,
                x=tokens.reshape(toks, width),
                mid=mid_grad,
                lat=lat_all,
                k1=k1,
                k2=k2,
                seen=seen,
                do=attended_grad,
                ha=h_attn,
                latent=latent,
                kgain=row(kv_gain_f),
                again=row(attn_gain_f),
                fgain=row(ffn_gain_grad),
                cos=group_tab(cosine),
                sin=group_tab(sine),
                rtr=dot(logit_grad, h_ffn, 0, 0).astype(bf16),
            ),
            scale,
        )
        gq, gkr, gkvb, gout = (res[n] for n in ("oq", "okr", "okvb", "oout"))
        gsh = (res["osh"][0], res["osh"][1], res["osd"])
        gex, gg = res["oex"], res["ogain"][0]
        input_grad = res["ograd"]
    else:
        dqn, dq1, dq2, dlat, dk1, dk2, dkvb = attend_back(
            seen, qn, q1, q2, lat_all, k1, k2, kvb_mat, attended_grad, scale
        )
        fold = lambda t: jnp.sum(t.reshape(micros, length, HEAD_GROUP, HALF_ROPE), axis=2)
        back_pack = jnp.concatenate(
            [dlat, fold(dk1), fold(dk2), jnp.zeros((micros, length, ROPE), f32)], axis=-1
        ).astype(bf16)
        own_back = z_home(back_pack, fast).reshape(toks, -1)
        latent_grad, kv_gain_grad = norm_back(latent, inv_kv, kv_gain_f, own_back[:, :RANK])
        g1, g2 = own_back[:, RANK : RANK + HALF_ROPE], own_back[:, RANK + HALF_ROPE : RANK + ROPE]
        kv_down_grad = jnp.concatenate(
            [latent_grad, g1 * cosine + g2 * sine, g2 * cosine - g1 * sine], axis=-1
        ).astype(bf16)
        dq1, dq2 = dq1.reshape(toks, -1), dq2.reshape(toks, -1)
        q_raw_grad = jnp.concatenate(
            [
                dqn.reshape(toks, -1),
                (dq1 * cos_all + dq2 * sin_all).astype(bf16),
                (dq2 * cos_all - dq1 * sin_all).astype(bf16),
            ],
            axis=-1,
        )
        attn_in_grad = dot(q_raw_grad, query_mat, 1, 0) + dot(kv_down_grad, kv_down_mat, 1, 0)
        x_part, attn_gain_grad = norm_back(x_in, inv_one, attn_gain_f, attn_in_grad)
        input_grad = (mid_grad + x_part).astype(bf16)

        kr_grad = jnp.concatenate(
            [dot(kv_down_grad, h_attn, 0, 0), dot(logit_grad, h_ffn, 0, 0)]
        ).astype(bf16)
        h_s, qg_s, krg_s, kvbg_s = core_swap(
            [h_attn, q_raw_grad, kr_grad, dkvb], (None, 1, 0, 1), fast, 6
        )
        grad_q = dot(tall(qg_s), tall(h_s), 0, 0).astype(bf16)
        grad_kr = (krg_s[0].astype(f32) + krg_s[1].astype(f32)).astype(bf16)
        grad_kvb = (kvbg_s[0].astype(f32) + kvbg_s[1].astype(f32)).astype(bf16)
        gain_grad = jnp.concatenate(
            [lane_rows(attn_gain_grad), lane_rows(ffn_gain_grad), lane_rows(kv_gain_grad)], axis=1
        )
        gain_len = gain_grad.shape[1]
        gain_grad = jnp.pad(gain_grad, ((0, 0), (0, 16 * 128 - gain_len))).reshape(-1, 16, 128)
        gq, gkr, gkvb, gout, gsh, gex, gg = reduce_anywhere(
            grad_q, grad_kr, grad_kvb, grad_out, grad_sh, grad_ex, gain_grad
        )
        gg = gg.reshape(-1)
    wide = lambda t: t.astype(f32)
    return (
        by_micro(layer_output),
        by_micro(input_grad),
        gg[:ga],
        wide(head_join(gq)),
        wide(gkr[: RANK + ROPE]),
        gg[2 * ga : 2 * ga + gk],
        wide(gkvb),
        wide(gout),
        gg[ga : 2 * ga],
        wide(gkr[RANK + ROPE :]),
        wide(gsh[0]),
        wide(gsh[1]),
        wide(gsh[2]),
        wide(gex[:2]),
        wide(gex[2:4]),
        wide(gex[4:]),
    )


def solution(mesh):
    token_spec = P(None, ("rep", "shard"), None)
    row_spec, col_spec, gain_spec = P("shard", None), P(None, "shard"), P("shard")
    expert_spec = P(None, "shard", None)
    weight_specs = (
        gain_spec,
        col_spec,
        col_spec,
        gain_spec,
        row_spec,
        row_spec,
        gain_spec,
        col_spec,
        row_spec,
        row_spec,
        row_spec,
        expert_spec,
        expert_spec,
        expert_spec,
    )
    return jax.shard_map(
        shards,
        mesh=mesh,
        in_specs=(token_spec,) + weight_specs + (token_spec, token_spec),
        out_specs=(token_spec, token_spec) + weight_specs,
        check_vma=False,
    )
```

```python
import functools

import jax
import jax.numpy as jnp
from jax import lax
from jax.experimental import pallas as pl
from jax.experimental.pallas import tpu as pltpu
from jax.sharding import PartitionSpec as P

HEADS = 16
NOPE = 128
ROPE = 64
VDIM = 128
RANK = 512
EXPERTS = 64
EXP_WIN = 2
MASK_BLOCK = 256
CAP = 16

epsilon = 1e-06
rope_base = 10000.0
masked_score = -1e30
highest = lax.Precision.HIGHEST
bf16 = jnp.bfloat16
f32 = jnp.float32
MESH = pl.DeviceIdType.MESH
HBM = pltpu.HBM
HALF_ROPE = ROPE // 2
HEAD_GROUP = 4
GROUP_LANES = HEAD_GROUP * HALF_ROPE


def dot(a, b, ca, cb):
    return lax.dot_general(a, b, (((ca,), (cb,)), ((), ())), preferred_element_type=f32)


def rms_scale(tensor):
    return lax.rsqrt(jnp.mean(tensor * tensor, axis=-1, keepdims=True) + epsilon)


def norm_back(tensor, inv_rms, gain_vec, gradient):
    scaled_grad = gradient * gain_vec
    inner_mean = jnp.mean(scaled_grad * tensor, axis=-1, keepdims=True)
    input_part = inv_rms * scaled_grad - tensor * (inv_rms * inv_rms * inv_rms) * inner_mean
    gain_part = jnp.sum(gradient * tensor * inv_rms, axis=0)
    return (input_part, gain_part)


def swiglu_back(gate_pre, up_pre, hidden_grad):
    sigmoid_gate = jax.nn.sigmoid(gate_pre)
    silu_gate = gate_pre * sigmoid_gate
    slope = sigmoid_gate * (1.0 + gate_pre * (1.0 - sigmoid_gate))
    return (
        (hidden_grad * up_pre * slope).astype(bf16),
        (hidden_grad * silu_gate).astype(bf16),
    )


def head_scores(qn, q1, q2, kv, k1, k2, seen, scale, head):
    lane = lax.broadcasted_iota(jnp.int32, (1, GROUP_LANES), 1)
    mine = (lane >= head * HALF_ROPE) & (lane < (head + 1) * HALF_ROPE)
    width = NOPE + VDIM
    q_head = qn[:, head * NOPE : (head + 1) * NOPE]
    k_head = kv[:, head * width : head * width + NOPE]
    v_head = kv[:, head * width + NOPE : (head + 1) * width]
    q1m = jnp.where(mine, q1, jnp.zeros_like(q1))
    q2m = jnp.where(mine, q2, jnp.zeros_like(q2))
    scores = dot(q_head, k_head, 1, 1) + dot(q1m, k1, 1, 1) + dot(q2m, k2, 1, 1)
    scores = jnp.where(seen > 0.0, scores * scale, masked_score)
    top = jnp.max(scores, axis=-1, keepdims=True)
    expo = jnp.exp(scores - top)
    probs = expo / jnp.sum(expo, axis=-1, keepdims=True)
    return probs, q_head, k_head, v_head, q1m, q2m, mine


def attend_kernel(scale, seen_ref, qn_ref, q1_ref, q2_ref, lat_ref, k1_ref, k2_ref, kvb_ref, out_ref):
    kv = dot(lat_ref[0], kvb_ref[...], 1, 0).astype(bf16)
    for head in range(HEAD_GROUP):
        probs, _, _, v_head, _, _, _ = head_scores(
            qn_ref[0], q1_ref[0], q2_ref[0], kv, k1_ref[0], k2_ref[0], seen_ref[...], scale, head
        )
        out_ref[0, :, head * VDIM : (head + 1) * VDIM] = dot(
            probs.astype(bf16), v_head, 1, 0
        ).astype(bf16)


def attend_back_kernel(
    scale,
    seen_ref,
    qn_ref,
    q1_ref,
    q2_ref,
    lat_ref,
    k1_ref,
    k2_ref,
    kvb_ref,
    do_ref,
    dqn_ref,
    dq1_ref,
    dq2_ref,
    dlat_ref,
    dk1_ref,
    dk2_ref,
    dkvb_ref,
    kvg_ref,
    acc_ref,
):
    group, micro = pl.program_id(0), pl.program_id(1)
    width = NOPE + VDIM

    @pl.when(group == 0)
    def _():
        dlat_ref[micro] = jnp.zeros(dlat_ref.shape[1:], f32)
        dk1_ref[micro] = jnp.zeros(dk1_ref.shape[1:], f32)
        dk2_ref[micro] = jnp.zeros(dk2_ref.shape[1:], f32)

    lat = lat_ref[0]
    kvb = kvb_ref[...]
    kv = dot(lat, kvb, 1, 0).astype(bf16)
    k1, k2 = k1_ref[0], k2_ref[0]
    dq1 = jnp.zeros(dq1_ref.shape[1:], f32)
    dq2 = jnp.zeros(dq2_ref.shape[1:], f32)
    dk1 = jnp.zeros(k1.shape, f32)
    dk2 = jnp.zeros(k2.shape, f32)
    for head in range(HEAD_GROUP):
        probs, q_head, k_head, v_head, q1m, q2m, mine = head_scores(
            qn_ref[0], q1_ref[0], q2_ref[0], kv, k1, k2, seen_ref[...], scale, head
        )
        d_out = do_ref[0, :, head * VDIM : (head + 1) * VDIM]
        dprobs = dot(d_out, v_head, 1, 1)
        delta = jnp.sum(probs * dprobs, axis=-1, keepdims=True)
        ds = (probs * (dprobs - delta)).astype(bf16)
        dqn_ref[0, :, head * NOPE : (head + 1) * NOPE] = (dot(ds, k_head, 1, 0) * scale).astype(bf16)
        dq1 = dq1 + jnp.where(mine, dot(ds, k1, 1, 0), 0.0)
        dq2 = dq2 + jnp.where(mine, dot(ds, k2, 1, 0), 0.0)
        dk1 = dk1 + dot(ds, q1m, 0, 0)
        dk2 = dk2 + dot(ds, q2m, 0, 0)
        kvg_ref[:, head * width : head * width + NOPE] = (dot(ds, q_head, 0, 0) * scale).astype(bf16)
        kvg_ref[:, head * width + NOPE : (head + 1) * width] = dot(
            probs.astype(bf16), d_out, 0, 0
        ).astype(bf16)
    dq1_ref[0] = dq1 * scale
    dq2_ref[0] = dq2 * scale
    dk1_ref[micro] += dk1 * scale
    dk2_ref[micro] += dk2 * scale
    kvg = kvg_ref[...]
    dlat_ref[micro] += dot(kvg, kvb, 1, 1)
    part = dot(lat, kvg, 0, 0)

    @pl.when(micro == 0)
    def _():
        acc_ref[...] = part

    @pl.when(micro > 0)
    def _():
        acc_ref[...] += part

    @pl.when(micro == pl.num_programs(1) - 1)
    def _():
        dkvb_ref[...] = acc_ref[...].astype(bf16)


def attention_specs(micros, rows, length):
    groups = HEADS // HEAD_GROUP
    wide = HEAD_GROUP * NOPE
    specs = [
        pl.BlockSpec((1, length), lambda g, m: (0, 0)),
        pl.BlockSpec((1, rows, wide), lambda g, m: (m, 0, g)),
        pl.BlockSpec((1, rows, GROUP_LANES), lambda g, m: (m, 0, g)),
        pl.BlockSpec((1, rows, GROUP_LANES), lambda g, m: (m, 0, g)),
        pl.BlockSpec((1, length, RANK), lambda g, m: (m, 0, 0)),
        pl.BlockSpec((1, length, GROUP_LANES), lambda g, m: (m, 0, 0)),
        pl.BlockSpec((1, length, GROUP_LANES), lambda g, m: (m, 0, 0)),
        pl.BlockSpec((RANK, HEAD_GROUP * (NOPE + VDIM)), lambda g, m: (0, g)),
    ]
    return (groups, micros), specs, pl.BlockSpec((1, rows, wide), lambda g, m: (m, 0, g))


def attend(seen, qn, q1, q2, lat, k1, k2, kvb, scale):
    micros, rows, _ = qn.shape
    length = lat.shape[1]
    grid, specs, out_spec = attention_specs(micros, rows, length)
    return pl.pallas_call(
        functools.partial(attend_kernel, scale),
        grid=grid,
        in_specs=specs,
        out_specs=out_spec,
        out_shape=jax.ShapeDtypeStruct(qn.shape, bf16),
        compiler_params=pltpu.CompilerParams(vmem_limit_bytes=48 << 20),
        name="attend",
    )(seen, qn, q1, q2, lat, k1, k2, kvb)


def attend_packed(seen, q, lat, k1, k2, kvb, scale):
    micros, rows, _ = q.shape
    length = lat.shape[1]
    grid, specs, out_spec = attention_specs(micros, rows, length)
    first = HEADS * NOPE // GROUP_LANES
    second = HEADS * (NOPE + HALF_ROPE) // GROUP_LANES
    specs[2] = pl.BlockSpec((1, rows, GROUP_LANES), lambda g, m: (m, 0, first + g))
    specs[3] = pl.BlockSpec((1, rows, GROUP_LANES), lambda g, m: (m, 0, second + g))
    return pl.pallas_call(
        functools.partial(attend_kernel, scale),
        grid=grid,
        in_specs=specs,
        out_specs=out_spec,
        out_shape=jax.ShapeDtypeStruct((micros, rows, HEADS * VDIM), bf16),
        compiler_params=pltpu.CompilerParams(vmem_limit_bytes=48 << 20),
        name="attend",
    )(seen, q, q, q, lat, k1, k2, kvb)


def attend_back(seen, qn, q1, q2, lat, k1, k2, kvb, d_out, scale):
    micros, rows, _ = qn.shape
    length = lat.shape[1]
    grid, specs, out_spec = attention_specs(micros, rows, length)
    whole = lambda g, m: (0, 0, 0)
    return pl.pallas_call(
        functools.partial(attend_back_kernel, scale),
        grid=grid,
        in_specs=specs + [out_spec],
        out_specs=[
            out_spec,
            pl.BlockSpec((1, rows, GROUP_LANES), lambda g, m: (m, 0, g)),
            pl.BlockSpec((1, rows, GROUP_LANES), lambda g, m: (m, 0, g)),
            pl.BlockSpec(lat.shape, whole),
            pl.BlockSpec(k1.shape, whole),
            pl.BlockSpec(k2.shape, whole),
            pl.BlockSpec((RANK, HEAD_GROUP * (NOPE + VDIM)), lambda g, m: (0, g)),
        ],
        out_shape=[
            jax.ShapeDtypeStruct(qn.shape, bf16),
            jax.ShapeDtypeStruct(q1.shape, f32),
            jax.ShapeDtypeStruct(q2.shape, f32),
            jax.ShapeDtypeStruct(lat.shape, f32),
            jax.ShapeDtypeStruct(k1.shape, f32),
            jax.ShapeDtypeStruct(k2.shape, f32),
            jax.ShapeDtypeStruct(kvb.shape, bf16),
        ],
        scratch_shapes=[
            pltpu.VMEM((length, HEAD_GROUP * (NOPE + VDIM)), bf16),
            pltpu.VMEM((RANK, HEAD_GROUP * (NOPE + VDIM)), f32),
        ],
        compiler_params=pltpu.CompilerParams(vmem_limit_bytes=48 << 20),
        name="attend_back",
    )(seen, qn, q1, q2, lat, k1, k2, kvb, d_out)


class Place:
    def __init__(self):
        self.r = lax.axis_index("rep")
        self.z = lax.axis_index("shard")
        self.core = self.r % 2
        self.chip = self.r // 2
        self.x = self.chip % 2
        self.y = self.chip // 2
        self.peer = (self.r + 1 - 2 * self.core, self.z)
        self.across = {
            "x": (self.r + 2 - 4 * self.x, self.z),
            "y": (self.r + 4 - 8 * self.y, self.z),
        }
        cx = self.chip + 1 - 2 * self.x
        cy = self.chip + 2 - 4 * self.y
        self.chips = {"": self.chip, "x": cx, "y": cy, "xy": cx + 2 - 4 * self.y}

    def along(self, step):
        return (self.r, (self.z + step) % 4)

    def shard_at(self, step):
        return (self.z + step) % 4


class Sems:
    def __init__(self, send, recv):
        self.send, self.recv = send, recv
        self.count = 0
        self.pending = []

    def slot(self):
        self.count += 1
        return self.count - 1

    def copy(self, src, dst, slot, device):
        return pltpu.make_async_remote_copy(
            src_ref=src,
            dst_ref=dst,
            send_sem=self.send.at[slot],
            recv_sem=self.recv.at[slot],
            device_id=device,
            device_id_type=MESH,
        )

    def push(self, src, dst, slot, device, when=None):
        under(when, lambda: self.copy(src, dst, slot, device).start())
        self.pending.append((lambda: self.copy(src, dst, slot, device).wait_send(), when))
        return self.pending[-1]

    def settle(self, entry):
        self.pending.remove(entry)
        under(entry[1], entry[0])

    def arrived(self, dst, slot, device, when=None):
        under(when, lambda: self.copy(dst, dst, slot, device).wait_recv())

    def drain(self):
        for wait, when in self.pending:
            under(when, wait)
        self.pending = []


def inside(z):
    return jnp.minimum(jnp.maximum(z, 0), 3)


def under(condition, act):
    if condition is None:
        act()
    else:
        pl.when(condition)(act)


def greet(devices):
    barrier = pltpu.get_barrier_semaphore()
    for device in devices:
        pl.semaphore_signal(barrier, inc=1, device_id=device, device_id_type=MESH)
    pl.semaphore_wait(barrier, len(devices))


def lanes(start, size):
    return pl.ds(pl.multiple_of(start, 128), size)


def rows16(start, size):
    return pl.ds(pl.multiple_of(start, 16), size)


class Through:
    def __init__(self, src, buffer, dst, sem):
        self.into = pltpu.make_async_copy(src, buffer, sem)
        self.out = pltpu.make_async_copy(buffer, dst, sem)

    def start(self):
        self.into.start()

    def turn(self):
        self.into.wait()
        self.out.start()

    def wait(self):
        self.out.wait()


class PlaneGather:
    def __init__(self, sems, place, part, half, by, when=None):
        self.sems, self.place, self.part, self.half, self.by = sems, place, part, half, by
        self.when = when
        self.slots = {k: sems.slot() for k in ("x", "y", "xy", "core")}

    def first(self, src=None):
        p = self.place
        mine = self.part(p.core, p.chip)
        for axis in ("x", "y"):
            self.push(mine if src is None else src, mine, self.slots[axis], p.across[axis])

    def push(self, src, dst, slot, device):
        self.sems.push(src, dst, slot, device, self.when)

    def arrived(self, dst, slot, device):
        self.sems.arrived(dst, slot, device, self.when)

    def second(self):
        p = self.place
        for axis in ("x", "y"):
            got = self.part(p.core, p.chips[axis])
            self.arrived(got, self.slots[axis], p.across[axis])
        via = self.by
        other = "y" if via == "x" else "x"
        got = self.part(p.core, p.chips[via])
        self.push(got, got, self.slots["xy"], p.across[other])

    def third(self):
        p = self.place
        got = self.part(p.core, p.chips["xy"])
        self.arrived(got, self.slots["xy"], p.across["y" if self.by == "x" else "x"])
        half = self.half(p.core)
        self.push(half, half, self.slots["core"], p.peer)

    def fourth(self):
        p = self.place
        self.arrived(self.half(1 - p.core), self.slots["core"], p.peer)


def weight_regions(place, refs, shard):
    q, kr, kvb, out = refs
    ds = q.shape[1] // 4
    cols = lanes(shard * ds, ds)

    def row_split(ref, n):
        half = ref.shape[0] // 2
        return (
            lambda core, chip: ref.at[rows16(core * half + chip * n, n), cols],
            lambda core: ref.at[rows16(core * half, half), cols],
        )

    def col_split(ref, full):
        rows = full // 4
        half = ref.shape[-1] // 2
        n = half // 4
        lead = (slice(None),) * (len(ref.shape) - 2)
        span = rows16(shard * rows, rows)
        return (
            lambda core, chip: ref.at[(*lead, span, lanes(core * half + chip * n, n))],
            lambda core: ref.at[(*lead, span, lanes(core * half, half))],
        )

    return [
        row_split(q, q.shape[0] // 8),
        row_split(kr, kr.shape[0] // 8),
        col_split(kvb, kvb.shape[0]),
        col_split(out, out.shape[0]),
    ]


def own_part(refs, place):
    q, kr, kvb, out, sh = refs
    res = []
    for ref in (q, kr):
        n = ref.shape[0] // 8
        res.append(ref.at[rows16(place.core * 4 * n + place.chip * n, n)])
    for ref in (kvb, out):
        n = ref.shape[-1] // 8
        res.append(ref.at[:, lanes(place.core * 4 * n + place.chip * n, n)])
    n = sh.shape[-1] // 8
    res.append(sh.at[:, :, lanes(place.r * n, n)])
    return res


ITEMS = 4
GATHER_ORDER = (1, 0, 2, 3)
GATHER_SEMS = 6 + ITEMS * 6 * 5
LAG = 6


class WeightGather:
    def __init__(self, place, sems, mine, outs):
        self.place, self.sems, self.mine, self.outs = place, sems, mine, outs
        z = place.z
        self.here = weight_regions(place, outs, z)
        self.slots = {}
        units = []
        for i in GATHER_ORDER:
            for d in (1, 2, 3):
                for s in (1, -1):
                    self.slots[i, d, s] = sems.slot()
                    exists = z >= d if s == 1 else z + d <= 3
                    part, half = weight_regions(place, outs, inside(z - s * d))[i]
                    by = "x" if (d + i) % 2 == 0 else "y"
                    units.append(
                        (i, d, s, exists, part, PlaneGather(sems, place, part, half, by, exists))
                    )
        for i in GATHER_ORDER[:2]:
            self.own(i)
        self.units = units

    def run(self, late):
        units = self.units
        for n in range(len(units) + 3 * LAG):
            if n == 3 * len(units) // 4:
                late()
            if n < len(units):
                if n % 6 == 0 and n // 6 + 2 < ITEMS:
                    self.own(GATHER_ORDER[n // 6 + 2])
                self.along(units[n])
            for lag, name in ((LAG, "second"), (2 * LAG, "third"), (3 * LAG, "fourth")):
                if 0 <= n - lag < len(units):
                    getattr(units[n - lag][5], name)()

    def onward(self, src, dst, i, d, s, exists=None):
        if d > 3:
            return
        z = self.place.z
        more = z < 3 if s == 1 else z > 0
        if exists is not None:
            more = more & exists
        device = (self.place.r, inside(z + s))
        self.sems.push(src, dst, self.slots[i, d, s], device, more)

    def own(self, i):
        for s in (1, -1):
            self.onward(self.mine[i], self.here[i][0](self.place.core, self.place.chip), i, 1, s)

    def along(self, unit):
        i, d, s, exists, part, spread = unit
        z = self.place.z
        got = part(self.place.core, self.place.chip)
        device = (self.place.r, inside(z - s))
        self.sems.arrived(got, self.slots[i, d, s], device, exists)
        self.onward(got, got, i, d + 1, s, exists)
        spread.first()


def gather_kernel(*refs):
    ins, shared, gain = refs[:ITEMS], refs[ITEMS], refs[ITEMS + 1]
    refs = refs[ITEMS + 2 :]
    outs, shared_out, gains = refs[:ITEMS], refs[ITEMS], refs[ITEMS + 1]
    refs = refs[ITEMS + 2 :]
    buffers, (gain_buffer, send, recv, local) = refs[:ITEMS], refs[ITEMS:]
    place = Place()
    sems = Sems(send, recv)
    greet([place.peer, place.across["x"], place.across["y"]] + [place.along(k) for k in (1, 2, 3)])
    mine = own_part((*ins, shared), place)
    ds = ins[0].shape[1]
    own = [
        outs[0].at[:, lanes(place.z * ds, ds)],
        outs[1].at[:, lanes(place.z * ds, ds)],
        outs[2].at[rows16(place.z * ins[2].shape[0], ins[2].shape[0])],
        outs[3].at[rows16(place.z * ins[3].shape[0], ins[3].shape[0])],
    ]
    kept = [Through(ins[i], buffers[i], own[i], local.at[i]) for i in range(ITEMS)]
    kept.append(Through(gain, gain_buffer, gains.at[place.z], local.at[ITEMS]))
    gain_slots = [sems.slot() for _ in range(3)]
    shared_slots = [sems.slot() for _ in range(3)]
    for k in (1, 2, 3):
        sems.push(gain, gains.at[place.z], gain_slots[k - 1], place.along(k))
    job = WeightGather(place, sems, mine, outs)
    for copy in kept:
        copy.start()
    for copy in kept:
        copy.turn()

    def late():
        for k in (1, 2, 3):
            sems.push(mine[ITEMS], shared_out.at[:, k - 1], shared_slots[k - 1], place.along(k))

    job.run(late)
    for k in (1, 2, 3):
        sems.arrived(gains.at[place.shard_at(4 - k)], gain_slots[k - 1], place.along(4 - k))
        sems.arrived(shared_out.at[:, k - 1], shared_slots[k - 1], place.along(4 - k))
    sems.drain()
    for copy in kept:
        copy.wait()


def gather_weights(q, kr, kvb, out, sh, gain, fast):
    if not fast:
        every = lambda w, axis: lax.all_gather(w, "shard", axis=axis, tiled=True)
        return (
            every(q, 1),
            every(kr, 1),
            every(kvb, 0),
            every(out, 0),
            every(sh, 1),
            lax.all_gather(gain, "shard", axis=0),
        )
    shape = jax.ShapeDtypeStruct
    *whole, rest, gains = pl.pallas_call(
        gather_kernel,
        in_specs=[pl.BlockSpec(memory_space=HBM)] * 6,
        out_specs=[pl.BlockSpec(memory_space=HBM)] * 6,
        out_shape=[
            shape((q.shape[0], q.shape[1] * 4), bf16),
            shape((kr.shape[0], kr.shape[1] * 4), bf16),
            shape((kvb.shape[0] * 4, kvb.shape[1]), bf16),
            shape((out.shape[0] * 4, out.shape[1]), bf16),
            shape((3, 3, sh.shape[1], sh.shape[2] // 8), bf16),
            shape((4,) + gain.shape, bf16),
        ],
        scratch_shapes=[pltpu.VMEM(w.shape, bf16) for w in (q, kr, kvb, out, gain)]
        + [
            pltpu.SemaphoreType.DMA((GATHER_SEMS,)),
            pltpu.SemaphoreType.DMA((GATHER_SEMS,)),
            pltpu.SemaphoreType.DMA((ITEMS + 1,)),
        ],
        compiler_params=pltpu.CompilerParams(
            collective_id=0, has_side_effects=True, vmem_limit_bytes=32 << 20
        ),
        name="gather_weights",
    )(q, kr, kvb, out, sh, gain)
    rest = lax.all_gather(rest, "rep", axis=3, tiled=True)
    return (*whole, rest.reshape(3, -1, sh.shape[2]), gains)


def along_z(tensor, step):
    return lax.ppermute(tensor, "shard", [(i, (i + step) % 4) for i in range(4)])


def over(tensor, mask):
    return lax.ppermute(tensor, "rep", [(i, i ^ mask) for i in range(8)])


def z_all(tensor, fast):
    if not fast:
        return lax.all_gather(tensor, "shard", axis=1, tiled=True)
    return jnp.concatenate([tensor] + [along_z(tensor, k) for k in (1, 2, 3)], axis=1)


def z_home(tensor, fast):
    if not fast:
        return lax.psum_scatter(tensor.astype(f32), "shard", scatter_dimension=1, tiled=True)
    rows = tensor.shape[1] // 4
    blocks = [lax.slice_in_dim(tensor, k * rows, (k + 1) * rows, axis=1) for k in range(4)]
    got = [along_z(blocks[k], -k).astype(f32) for k in (1, 2, 3)]
    return blocks[0].astype(f32) + got[0] + got[1] + got[2]


def front_kernel(
    x_ref,
    again_ref,
    kgain_ref,
    kr_ref,
    cos_ref,
    sin_ref,
    mat_ref,
    ha_ref,
    latent_ref,
    q_ref,
    lat_ref,
    k1_ref,
    k2_ref,
    tiles,
    pack,
    packs,
    send,
    recv,
    load,
):
    place = Place()
    sems = Sems(send, recv)
    size = tiles.shape[1]

    def fetch(t):
        return pltpu.make_async_copy(
            mat_ref.at[t * size : (t + 1) * size], tiles.at[t % 2], load.at[t % 2]
        )

    fetch(0).start()
    greet([place.along(k) for k in (1, 2, 3)])

    def normed(t, carry):
        span = pl.ds(pl.multiple_of(t * 32, 32), 32)
        x = x_ref[span].astype(f32)
        ha_ref[span] = (x * rms_scale(x) * again_ref[...]).astype(bf16)
        return carry

    lax.fori_loop(0, x_ref.shape[0] // 32, normed, 0)
    ha = ha_ref[...]
    kv_down = dot(ha, kr_ref[...], 1, 1)
    latent = kv_down[:, :RANK]
    latent_ref[...] = latent
    micros, rows, _ = pack.shape
    normal = (latent * rms_scale(latent) * kgain_ref[...]).astype(bf16)
    first = kv_down[:, RANK : RANK + HALF_ROPE]
    second = kv_down[:, RANK + HALF_ROPE : RANK + ROPE]
    cosine, sine = cos_ref[:, :HALF_ROPE], sin_ref[:, :HALF_ROPE]
    turned = (
        (first * cosine - second * sine).astype(bf16),
        (second * cosine + first * sine).astype(bf16),
    )
    for micro in range(micros):
        span = slice(micro * rows, (micro + 1) * rows)
        pack[micro, :, :RANK] = normal[span]
        pack[micro, :, RANK : RANK + HALF_ROPE] = turned[0][span]
        pack[micro, :, RANK + HALF_ROPE : RANK + ROPE] = turned[1][span]
        pack[micro, :, RANK + ROPE :] = jnp.zeros((rows, ROPE), bf16)
    block = lambda k: packs.at[:, k * rows : (k + 1) * rows]
    for k in (1, 2, 3):
        sems.push(pack, block(k), k - 1, place.along(k))

    count = mat_ref.shape[0] // size
    held = None
    for t in range(count):
        fetch(t).wait()
        if t + 1 < count:
            fetch(t + 1).start()
        value = dot(ha, tiles[t % 2], 1, 1)
        if t < count - 2:
            q_ref[:, t * size : (t + 1) * size] = value.astype(bf16)
        elif held is None:
            held = value
        else:
            cosine, sine = cos_ref[...], sin_ref[...]
            q_ref[:, (t - 1) * size : t * size] = (held * cosine - value * sine).astype(bf16)
            q_ref[:, t * size : (t + 1) * size] = (value * cosine + held * sine).astype(bf16)

    for k in (1, 2, 3):
        sems.arrived(block(k), k - 1, place.along(4 - k))
    for micro in range(micros):
        for k in range(4):
            span = slice(k * rows, (k + 1) * rows)
            part = pack[micro] if k == 0 else packs[micro, span]
            lat_ref[micro, span] = part[:, :RANK]
            for ref, start in ((k1_ref, RANK), (k2_ref, RANK + HALF_ROPE)):
                lanes32 = part[:, start : start + HALF_ROPE]
                ref[micro, span] = jnp.concatenate([lanes32] * HEAD_GROUP, axis=1)
    sems.drain()


def front(x, again, kgain, kr, cosine, sine, mat, micros):
    toks, wide = x.shape
    length = 4 * (toks // micros)
    shape = jax.ShapeDtypeStruct
    vm, dma = pltpu.VMEM, pltpu.SemaphoreType.DMA
    size = HEADS * HALF_ROPE
    packed = RANK + 2 * ROPE
    vmem = pl.BlockSpec(memory_space=pltpu.VMEM)
    return pl.pallas_call(
        front_kernel,
        in_specs=[vmem] * 6 + [pl.BlockSpec(memory_space=HBM)],
        out_specs=[vmem] * 6,
        out_shape=[
            shape((toks, wide), bf16),
            shape((toks, RANK), f32),
            shape((toks, mat.shape[0]), bf16),
            shape((micros, length, RANK), bf16),
            shape((micros, length, GROUP_LANES), bf16),
            shape((micros, length, GROUP_LANES), bf16),
        ],
        scratch_shapes=[
            vm((2, size, wide), bf16),
            vm((micros, toks // micros, packed), bf16),
            vm((micros, length, packed), bf16),
            dma((3,)),
            dma((3,)),
            dma((2,)),
        ],
        compiler_params=pltpu.CompilerParams(
            collective_id=9, has_side_effects=True, vmem_limit_bytes=40 << 20
        ),
        name="front",
    )(x, again, kgain, kr, cosine, sine, mat)


def swap_kernel(count, axes, *refs):
    ins, outs, buffers = (refs[n * count : (n + 1) * count] for n in range(3))
    send, recv, local = refs[3 * count :]
    place = Place()
    sems = Sems(send, recv)
    greet([place.peer])

    def cut(i, core):
        if axes[i] is None:
            return ins[i]
        n = ins[i].shape[axes[i]] // 2
        if axes[i] == 0:
            return ins[i].at[rows16(core * n, n)]
        return ins[i].at[:, lanes(core * n, n)]

    for i in range(count):
        sems.push(cut(i, 1 - place.core), outs[i].at[1], sems.slot(), place.peer)
    kept = [
        Through(cut(i, place.core), buffers[i], outs[i].at[0], local.at[i]) for i in range(count)
    ]
    for copy in kept:
        copy.start()
    for copy in kept:
        copy.turn()
    for i in range(count):
        sems.arrived(outs[i].at[1], i, place.peer)
    sems.drain()
    for copy in kept:
        copy.wait()


def core_swap(arrays, axes, fast, ident):
    count = len(arrays)
    if not fast:
        reps = lax.axis_size("rep")
        core = lax.axis_index("rep") % 2
        res = []
        for a, axis in zip(arrays, axes):
            keep = give = a
            if axis is not None:
                n = a.shape[axis] // 2
                keep = lax.dynamic_slice_in_dim(a, core * n, n, axis)
                give = lax.dynamic_slice_in_dim(a, (1 - core) * n, n, axis)
            got = lax.ppermute(give, "rep", [(i, i + 1 - 2 * (i % 2)) for i in range(reps)])
            res.append(jnp.stack([keep, got]))
        return res
    shapes = [
        tuple(n // 2 if d == axis else n for d, n in enumerate(a.shape))
        for a, axis in zip(arrays, axes)
    ]
    return pl.pallas_call(
        functools.partial(swap_kernel, count, axes),
        in_specs=[pl.BlockSpec(memory_space=HBM)] * count,
        out_specs=[pl.BlockSpec(memory_space=HBM)] * count,
        out_shape=[jax.ShapeDtypeStruct((2,) + s, a.dtype) for s, a in zip(shapes, arrays)],
        scratch_shapes=[pltpu.VMEM(s, a.dtype) for s, a in zip(shapes, arrays)]
        + [
            pltpu.SemaphoreType.DMA((count,)),
            pltpu.SemaphoreType.DMA((count,)),
            pltpu.SemaphoreType.DMA((count,)),
        ],
        compiler_params=pltpu.CompilerParams(
            collective_id=ident, has_side_effects=True, vmem_limit_bytes=32 << 20
        ),
        name="core_swap",
    )(*arrays)


def add_rows(dst, terms):
    lead = dst.shape[:-2]
    rows = max(n for n in (16, 32, 48, 64, 80) if dst.shape[-2] % n == 0)
    steps = dst.shape[-2] // rows

    def body(step, carry):
        span = pl.ds(pl.multiple_of(step * rows, rows), rows)
        where = (slice(None),) * len(lead) + (span,)
        total = terms[0][where].astype(f32)
        for t in terms[1:]:
            total = total + t[where].astype(f32)
        dst[where] = total.astype(dst.dtype)
        return carry

    lax.fori_loop(0, steps, body, 0)


def reduce_anywhere(q, kr, kvb, out, sh, ex, gain):
    core = lax.axis_index("rep") % 2

    def whole(g, axis):
        wide = jnp.zeros(g.shape[:axis] + (g.shape[axis] * 2,) + g.shape[axis + 1 :], f32)
        return lax.dynamic_update_slice_in_dim(wide, g.astype(f32), core * g.shape[axis], axis)

    def total(g, axis, along):
        g = lax.psum_scatter(whole(g, axis), "shard", scatter_dimension=along, tiled=True)
        return lax.psum(g, "rep")

    return (
        total(q, 0, 1),
        total(kr, 0, 1),
        total(kvb, 1, 0),
        total(out, 1, 0),
        total(sh, 2, 1),
        lax.psum(whole(ex, 2), "rep"),
        lax.psum(lax.psum_scatter(gain, "shard", scatter_dimension=0, tiled=True), "rep")[0],
    )


class Unit:
    def __init__(self, job, name, u, axis, part, got1, got2, own=None, home=None, got3=None, last=None):
        self.job, self.name, self.u = job, name, u
        self.axis, self.other = axis, "y" if axis == "x" else "x"
        self.part, self.got1, self.got2, self.own = part, got1, got2, own
        self.home, self.got3, self.last = home, got3, last
        self.slots = [job.sems.slot() for _ in range(4)]

    def stage1(self):
        job = self.job
        place = job.place
        for n, chip in enumerate((self.axis, "xy")):
            job.sems.push(
                self.part(place.chips[chip]), self.got1.at[n], self.slots[n], place.across[self.axis]
            )

    def stage2(self):
        place = self.job.place
        if self.own is not None:
            ring, sem = self.own
            self.loads = [
                pltpu.make_async_copy(
                    self.part(place.chips["" if n == 0 else self.other]), ring.at[n], sem.at[n]
                )
                for n in (0, 1)
            ]
            for copy in self.loads:
                copy.start()
            self.mine = [ring.at[0], ring.at[1]]
        else:
            self.mine = [self.part(place.chips[""]), self.part(place.chips[self.other])]

    def stage3(self):
        sems, place = self.job.sems, self.job.place
        for n in (1, 0):
            if self.own is not None:
                self.loads[n].wait()
            sems.arrived(self.got1.at[n], self.slots[n], place.across[self.axis])
            add_rows(self.got1.at[n], [self.got1.at[n], self.mine[n]])
            if n == 1:
                sems.push(self.got1.at[1], self.got2, self.slots[2], place.across[self.other])

    def stage4(self):
        sems, place = self.job.sems, self.job.place
        sems.arrived(self.got2, self.slots[2], place.across[self.other])
        add_rows(self.got1.at[0], [self.got1.at[0], self.got2])
        if self.home:
            sems.push(self.got1.at[0], self.got3.at[self.home - 1], self.slots[3], place.along(self.home))

    def stage5(self):
        if self.last is None:
            return
        job = self.job
        place = job.place
        for unit in job.units:
            if unit.name == self.name and unit.home:
                got = unit.got3.at[unit.home - 1]
                job.sems.arrived(got, unit.slots[3], place.along(4 - unit.home))
        if self.got3 is not None:
            add_rows(self.got1.at[0], [self.got1.at[0]] + [self.got3.at[n] for n in range(3)])
        src, part, half, sem, by = self.last
        self.stay = pltpu.make_async_copy(src, part(place.core, place.chip), sem)
        self.stay.start()
        self.spread = PlaneGather(job.sems, place, part, half, by)
        self.spread.first(src)

    def stage6(self):
        if self.last is not None:
            self.spread.second()

    def stage7(self):
        if self.last is not None:
            self.stay.wait()
            self.spread.third()

    def stage8(self):
        if self.last is not None:
            self.spread.fourth()


class Pump:
    LAGS = (0, 4, 2, 4, 3, 2, 2, 2)

    def __init__(self, place, sems):
        self.place, self.sems = place, sems
        self.units = []
        self.at = [0] * 8

    def tick(self, flush=False):
        for n in range(8):
            ahead = len(self.units) if n == 0 else self.at[n - 1]
            if self.at[n] < ahead - (0 if flush else self.LAGS[n]):
                getattr(self.units[self.at[n]], "stage%d" % (n + 1))()
                self.at[n] += 1

    def ahead(self, count):
        for _ in range(min(count, len(self.units) - self.at[0])):
            self.units[self.at[0]].stage1()
            self.at[0] += 1

    def run(self, count):
        for _ in range(count):
            self.tick()

    def end(self):
        while self.at[-1] < len(self.units):
            before = list(self.at)
            self.tick()
            if self.at == before:
                self.tick(True)


BACK_IN = (
    "gs0",
    "gs1",
    "gs2",
    "ge0",
    "ge1",
    "ge2",
    "gout",
    "q",
    "kvb",
    "kq",
    "kkr",
    "x",
    "mid",
    "lat",
    "k1",
    "k2",
    "seen",
    "do",
    "ha",
    "latent",
    "kgain",
    "again",
    "fgain",
    "cos",
    "sin",
    "rtr",
)
BACK_HBM = 13
BACK_OUT = (
    "oq",
    "okr",
    "okvb",
    "oout",
    "osh",
    "osd",
    "oex",
    "zsh",
    "ogain",
    "ograd",
)
BACK_SLOTS = 6 + 3 + 5 + 10 + 28 * 4 + 7 * 4
EARLY = 2


def back_kernel(scale, names, *refs):
    r = dict(zip(names, refs))
    place = Place()
    sems = Sems(r["send"], r["recv"])
    others = [place.peer]
    for axes in ("x", "y", "xy"):
        for flip in (place.core, 1 - place.core):
            others.append((place.chips[axes] * 2 + flip, place.z))
    greet(others + [place.along(k) for k in (1, 2, 3)])
    load = r["load"]
    pump = Pump(place, sems)
    core = place.core
    toks = r["ha"].shape[0]
    rows = toks // 2

    shared = [r["gs0"], r["gs1"], r["gs2"]]
    experts = [r["ge0"], r["ge1"], r["ge2"]]
    ff = shared[0].shape[0] // 4
    shared_slots = [[sems.slot() for _ in range(3)] for _ in range(EARLY)]
    for j in range(EARLY):
        for k in (1, 2, 3):
            sems.push(
                shared[j].at[k * ff : (k + 1) * ff],
                r["zsh"].at[k - 1, j],
                shared_slots[j][k - 1],
                place.along(4 - k),
            )
    swap = {name: sems.slot() for name in ("ha", "kvb", "q", "kvd", "rtr")}
    sems.push(r["ha"], r["s_ha"], swap["ha"], place.peer)
    sems.push(r["rtr"], r["s_rtr"], swap["rtr"], place.peer)
    begin = [
        pltpu.make_async_copy(r["q"], r["qs"], load.at[0]),
        pltpu.make_async_copy(r["kvb"], r["kvbs"], load.at[1]),
    ]
    for copy in begin:
        copy.start()

    def out_split(o, by_rows):
        if by_rows:
            half = o.shape[0] // 2
            n = half // 4
            return (
                lambda c, chip: o.at[rows16(c * half + chip * n, n)],
                lambda c: o.at[rows16(c * half, half)],
            )
        half = o.shape[-1] // 2
        n = half // 4
        lead = (slice(None),) * (len(o.shape) - 1)
        return (
            lambda c, chip: o.at[(*lead, lanes(c * half + chip * n, n))],
            lambda c: o.at[(*lead, lanes(c * half, half))],
        )

    rings = 0

    def ring(shape_ref):
        nonlocal rings
        slot = rings % 4
        rings += 1
        return slot

    def add_matrices(name, sources, out, by, ringed):
        count = len(sources)
        for u in range(count):
            n = sources[u].shape[-1] // 4
            own = None
            if ringed:
                slot = ring(None)
                own = (r["ring_" + name].at[slot], r["ringsem"].at[slot])
            last = None
            if u == count - 1:
                last = (r["got1_" + name].at[:, 0], *out_split(out, False), r["keep"].at[len(pump.units) % 8], by)
            pump.units.append(
                Unit(
                    pump,
                    name,
                    u,
                    "x" if u % 2 == 0 else "y",
                    lambda chip, u=u: sources[u].at[:, lanes(chip * n, n)],
                    r["got1_" + name].at[u],
                    r["got2_" + name].at[u],
                    own=own,
                    last=last,
                )
            )

    def add_sharded(name, part_of, out, by_rows, by, ringed=None):
        for n, k in enumerate((1, 2, 3, 4)):
            u, s = k % 4, place.shard_at(k)
            own = None
            if ringed:
                slot = ring(None)
                own = (r["ring_" + ringed].at[slot], r["ringsem"].at[slot])
            last = None
            if k == 4:
                last = (r["got1_" + name].at[0, 0], *out_split(out, by_rows), r["keep"].at[len(pump.units) % 8], by)
            pump.units.append(
                Unit(
                    pump,
                    name,
                    u,
                    "x" if n % 2 == 0 else "y",
                    lambda chip, s=s, k=k: part_of(s, k, chip),
                    r["got1_" + name].at[u],
                    r["got2_" + name].at[u],
                    own=own,
                    home=k % 4,
                    got3=r["got3_" + name],
                    last=last,
                )
            )

    add_matrices("ex", [t.at[e] for t in experts for e in range(EXP_WIN)], r["oex"], "x", True)
    block = r["gout"].shape[0] // 4
    n_out = r["gout"].shape[1] // 4
    add_sharded(
        "out",
        lambda s, k, chip: r["gout"].at[rows16(s * block, block), lanes(chip * n_out, n_out)],
        r["oout"],
        False,
        "y",
        "out",
    )
    n_sd = shared[EARLY].shape[1] // 4
    add_sharded(
        "sd",
        lambda s, k, chip: shared[EARLY].at[
            (4 - k) % 4 * ff : ((4 - k) % 4 + 1) * ff, lanes(chip * n_sd, n_sd)
        ],
        r["osd"],
        False,
        "x",
        "ex",
    )
    pump.ahead(4)
    for copy in begin:
        copy.wait()

    qs, kvbs, kvg, acc, dlat, dkvb = (r[n] for n in ("qs", "kvbs", "kvg", "acc", "dlat", "dkvb"))
    n1 = HEADS * NOPE
    n2 = HEADS * (NOPE + HALF_ROPE)
    width = NOPE + VDIM
    lane = lax.broadcasted_iota(jnp.int32, (1, GROUP_LANES), 1)

    def attention_step(group, micro):
        span = slice(micro * rows, (micro + 1) * rows)
        at = group * GROUP_LANES
        lat, k1, k2 = r["lat"][micro], r["k1"][micro], r["k2"][micro]
        q1, q2 = qs[span, n1 + at : n1 + at + GROUP_LANES], qs[span, n2 + at : n2 + at + GROUP_LANES]
        dq1 = jnp.zeros(q1.shape, f32)
        dq2 = jnp.zeros(q2.shape, f32)
        dk1 = jnp.zeros(k1.shape, f32)
        dk2 = jnp.zeros(k2.shape, f32)
        for pair in (0, 1):
            cols = slice((group * 4 + pair * 2) * width, (group * 4 + pair * 2 + 2) * width)
            weight = kvbs[:, cols]
            kv = dot(lat, weight, 1, 0).astype(bf16)
            for n in (0, 1):
                head = pair * 2 + n
                here = slice((group * 4 + head) * NOPE, (group * 4 + head + 1) * NOPE)
                mine = (lane >= head * HALF_ROPE) & (lane < (head + 1) * HALF_ROPE)
                q_head = qs[span, here]
                k_head = kv[:, n * width : n * width + NOPE]
                v_head = kv[:, n * width + NOPE : (n + 1) * width]
                q1m = jnp.where(mine, q1, jnp.zeros_like(q1))
                q2m = jnp.where(mine, q2, jnp.zeros_like(q2))
                scores = dot(q_head, k_head, 1, 1) + dot(q1m, k1, 1, 1) + dot(q2m, k2, 1, 1)
                scores = jnp.where(r["seen"][...] > 0.0, scores * scale, masked_score)
                expo = jnp.exp(scores - jnp.max(scores, axis=-1, keepdims=True))
                probs = expo / jnp.sum(expo, axis=-1, keepdims=True)
                d_out = r["do"][micro, :, here]
                dprobs = dot(d_out, v_head, 1, 1)
                delta = jnp.sum(probs * dprobs, axis=-1, keepdims=True)
                ds = (probs * (dprobs - delta)).astype(bf16)
                qs[span, here] = (dot(ds, k_head, 1, 0) * scale).astype(bf16)
                dq1 = dq1 + jnp.where(mine, dot(ds, k1, 1, 0), 0.0)
                dq2 = dq2 + jnp.where(mine, dot(ds, k2, 1, 0), 0.0)
                dk1 = dk1 + dot(ds, q1m, 0, 0)
                dk2 = dk2 + dot(ds, q2m, 0, 0)
                kvg[:, n * width : n * width + NOPE] = (dot(ds, q_head, 0, 0) * scale).astype(bf16)
                kvg[:, n * width + NOPE : (n + 1) * width] = dot(
                    probs.astype(bf16), d_out, 0, 0
                ).astype(bf16)
            terms = kvg[...]
            if group == 0 and pair == 0:
                dlat[micro] = dot(terms, weight, 1, 1)
            else:
                dlat[micro] += dot(terms, weight, 1, 1)
            part = dot(lat, terms, 0, 0)
            hold = slice(pair * 2 * width, (pair + 1) * 2 * width)
            if micro == 0:
                acc[:, hold] = part
            else:
                dkvb[:, cols] = (acc[:, hold] + part).astype(bf16)
        dq1, dq2 = dq1 * scale, dq2 * scale
        cosine, sine = r["cos"][...], r["sin"][...]
        qs[span, n1 + at : n1 + at + GROUP_LANES] = (dq1 * cosine + dq2 * sine).astype(bf16)
        qs[span, n2 + at : n2 + at + GROUP_LANES] = (dq2 * cosine - dq1 * sine).astype(bf16)
        for ref, value in ((r["dk1"], dk1), (r["dk2"], dk2)):
            if group == 0:
                ref[micro] = value * scale
            else:
                ref[micro] += value * scale

    for group in range(HEADS // HEAD_GROUP):
        for micro in (0, 1):
            attention_step(group, micro)
            pump.run(1)

    pack, zs = r["pack"], r["zs"]
    fold = lambda t: sum(t[:, n * HALF_ROPE : (n + 1) * HALF_ROPE] for n in range(HEAD_GROUP))
    for micro in (0, 1):
        pack[micro, :, :RANK] = dlat[micro].astype(bf16)
        pack[micro, :, RANK : RANK + HALF_ROPE] = fold(r["dk1"][micro]).astype(bf16)
        pack[micro, :, RANK + HALF_ROPE : RANK + ROPE] = fold(r["dk2"][micro]).astype(bf16)
        pack[micro, :, RANK + ROPE :] = jnp.zeros((pack.shape[1], ROPE), bf16)
    z_slots = [sems.slot() for _ in range(3)]
    for k in (1, 2, 3):
        sems.push(pack.at[:, k * rows : (k + 1) * rows], zs.at[k - 1], z_slots[k - 1], place.along(4 - k))
    half_q, half_kvb = qs.shape[1] // 2, dkvb.shape[1] // 2
    sems.push(qs.at[:, lanes((1 - core) * half_q, half_q)], r["s_q"], swap["q"], place.peer)
    kvb_push = sems.push(
        dkvb.at[:, lanes((1 - core) * half_kvb, half_kvb)], r["s_kvb"], swap["kvb"], place.peer
    )
    pump.run(1)

    sems.arrived(r["s_kvb"], swap["kvb"], place.peer)
    add_rows(r["s_kvb"], [r["s_kvb"], dkvb.at[:, lanes(core * half_kvb, half_kvb)]])
    n_kvb, b_kvb = half_kvb // 4, dkvb.shape[0] // 4
    add_sharded(
        "kvb",
        lambda s, k, chip: r["s_kvb"].at[rows16(s * b_kvb, b_kvb), lanes(chip * n_kvb, n_kvb)],
        r["okvb"],
        False,
        "x",
    )
    sems.arrived(r["s_ha"], swap["ha"], place.peer)
    sems.arrived(r["s_q"], swap["q"], place.peer)
    gq, ha, s_ha = r["gq"], r["ha"], r["s_ha"]

    def q_tile(t, carry):
        own = qs[:, lanes(core * half_q + t * 128, 128)]
        got = r["s_q"][:, lanes(t * 128, 128)]
        gq[rows16(t * 128, 128)] = (dot(own, ha[...], 0, 0) + dot(got, s_ha[...], 0, 0)).astype(bf16)
        return carry

    for part in range(4):
        lax.fori_loop(part * 3, part * 3 + 3, q_tile, 0)
        pump.run(1)
    r_q, c_q = gq.shape[0] // 4, gq.shape[1] // 4
    add_sharded(
        "q",
        lambda s, k, chip: gq.at[rows16(chip * r_q, r_q), lanes(s * c_q, c_q)],
        r["oq"],
        True,
        "y",
    )
    pump.run(4)

    for k in (1, 2, 3):
        sems.arrived(zs.at[k - 1], z_slots[k - 1], place.along(k))
    kvd, gains = r["kvd"], r["gains"]
    kv_gain_grad = jnp.zeros((1, RANK), f32)
    for micro in (0, 1):
        span = slice(micro * rows, (micro + 1) * rows)
        total = pack[micro, :rows].astype(f32)
        for k in range(3):
            total = total + zs[k, micro].astype(f32)
        upstream, latent = total[:, :RANK], r["latent"][span]
        inv = rms_scale(latent)
        scaled = upstream * r["kgain"][...]
        inner = jnp.mean(scaled * latent, axis=-1, keepdims=True)
        kvd[span, :RANK] = (inv * scaled - latent * (inv * inv * inv) * inner).astype(bf16)
        kv_gain_grad = kv_gain_grad + jnp.sum(upstream * latent * inv, axis=0, keepdims=True)
        g1, g2 = total[:, RANK : RANK + HALF_ROPE], total[:, RANK + HALF_ROPE : RANK + ROPE]
        cosine, sine = r["cos"][:, :HALF_ROPE], r["sin"][:, :HALF_ROPE]
        kvd[span, RANK : RANK + HALF_ROPE] = (g1 * cosine + g2 * sine).astype(bf16)
        kvd[span, RANK + HALF_ROPE : RANK + ROPE] = (g2 * cosine - g1 * sine).astype(bf16)
        kvd[span, RANK + ROPE :] = jnp.zeros((rows, ROPE), bf16)
    sems.push(kvd, r["s_kvd"], swap["kvd"], place.peer)

    tile = 384
    tiles = [("kq", t * tile, tile) for t in range(qs.shape[1] // tile)]
    tiles += [("kkr", 0, tile), ("kkr", tile, r["kkr"].shape[0] - tile)]
    wide = ha.shape[1]
    half_w = wide // 2

    def fetch(t):
        name, start, n = tiles[t]
        return pltpu.make_async_copy(
            r[name].at[start : start + n],
            kvbs.at[:n, (t % 2) * wide : (t % 2 + 1) * wide],
            load.at[2 + t % 2],
        )

    fetch(0).start()
    for t, (name, start, n) in enumerate(tiles):
        fetch(t).wait()
        if t + 1 < len(tiles):
            fetch(t + 1).start()
        left = (qs if name == "kq" else kvd)[:, start : start + n]
        for half in (0, 1):
            base = (t % 2) * wide + half * half_w
            value = dot(left, kvbs[:n, base : base + half_w], 1, 0)
            where = slice(half * toks, (half + 1) * toks)
            if t == 0:
                acc[where] = value
            else:
                acc[where] += value
        if t % 2 == 1:
            pump.run(1)

    cols = shared[0].shape[1]
    for j in range(EARLY):
        for k in (1, 2, 3):
            sems.arrived(r["zsh"].at[k - 1, j], shared_slots[j][k - 1], place.along(k))
        copies = [pltpu.make_async_copy(shared[j].at[:ff], kvbs.at[:ff, :cols], load.at[6])]
        for k in range(3):
            copies.append(
                pltpu.make_async_copy(
                    r["zsh"].at[k, j], kvbs.at[:ff, (k + 1) * cols : (k + 2) * cols], load.at[7 + k]
                )
            )
        for copy in copies:
            copy.start()
        for copy in copies:
            copy.wait()
        add_rows(r["gshs"].at[j], [kvbs.at[:ff, k * cols : (k + 1) * cols] for k in range(4)])
    add_matrices("sh", [r["gshs"].at[j] for j in range(EARLY)], r["osh"], "y", False)
    pump.run(2)

    sems.arrived(r["s_kvd"], swap["kvd"], place.peer)
    sems.arrived(r["s_rtr"], swap["rtr"], place.peer)
    sems.settle(kvb_push)
    half_kr = r["kkr"].shape[0] // 2
    r_kr, c_kr = half_kr // 4, wide // 4
    edges = sorted(set(list(range(0, 2 * half_kr + 1, 128)) + [half_kr]))
    for start, stop in zip(edges[:-1], edges[1:]):
        value = dot(kvd[:, start:stop], ha[...], 0, 0)
        value = value + dot(r["s_kvd"][:, start:stop], s_ha[...], 0, 0)
        n = start // half_kr
        if stop == 2 * half_kr:
            first = RANK + ROPE - start
            both = r["rtr"][...].astype(f32) + r["s_rtr"][...].astype(f32)
            value = jnp.concatenate([value[:first], both])
        dkvb[start - n * half_kr : stop - n * half_kr, n * wide : (n + 1) * wide] = value.astype(bf16)
    add_sharded(
        "kr",
        lambda s, k, chip: dkvb.at[rows16(chip * r_kr, r_kr), lanes(core * wide + s * c_kr, c_kr)],
        r["okr"],
        True,
        "x",
    )
    pump.run(2)

    again = r["again"][...]
    attn_gain_grad = jnp.zeros((1, wide), f32)
    step = 32
    for start in range(0, toks, step):
        fetched = [
            pltpu.make_async_copy(r[a].at[start : start + step], r[b], load.at[4 + n])
            for n, (a, b) in enumerate((("x", "xb"), ("mid", "mb")))
        ]
        for copy in fetched:
            copy.start()
        for copy in fetched:
            copy.wait()
        x = r["xb"][...].astype(f32)
        upstream = jnp.concatenate(
            [acc[start : start + step], acc[toks + start : toks + start + step]], axis=1
        )
        inv = rms_scale(x)
        scaled = upstream * again
        inner = jnp.mean(scaled * x, axis=-1, keepdims=True)
        part = inv * scaled - x * (inv * inv * inv) * inner
        r["ograd"][start : start + step] = (r["mb"][...] + part).astype(bf16)
        attn_gain_grad = attn_gain_grad + jnp.sum(upstream * x * inv, axis=0, keepdims=True)
        pump.run(1)
    n_a, n_k = wide // 4, RANK // 4
    gains[...] = jnp.zeros(gains.shape, f32)
    for s in range(4):
        gains[s, 0:1, :n_a] = attn_gain_grad[:, s * n_a : (s + 1) * n_a]
        gains[s, 0:1, n_a : 2 * n_a] = r["fgain"][:, s * n_a : (s + 1) * n_a]
        gains[s, 0:1, 2 * n_a :] = kv_gain_grad[:, s * n_k : (s + 1) * n_k]
    gain_slots = [sems.slot() for _ in range(3 + 7)]
    gz, gp, gs = r["gz"], r["gp"], r["gs"]
    for k in (1, 2, 3):
        sems.push(gains.at[place.shard_at(k)], gz.at[k - 1], gain_slots[k - 1], place.along(k))
    pump.run(2)

    for k in (1, 2, 3):
        sems.arrived(gz.at[k - 1], gain_slots[k - 1], place.along(4 - k))
    gs[...] = gains[place.z] + gz[0] + gz[1] + gz[2]
    for n, device in enumerate(others):
        sems.push(gs, gp.at[n], gain_slots[3 + n], device)
    pump.end()
    total = gs[...]
    for n, device in enumerate(others):
        sems.arrived(gp.at[n], gain_slots[3 + n], device)
        total = total + gp[n]
    r["ogain"][...] = total
    sems.drain()


def back_all(args, scale):
    shape = jax.ShapeDtypeStruct
    gout, q, kvb, kq, kkr = (args[n] for n in ("gout", "q", "kvb", "kq", "kkr"))
    toks, wide = args["ha"].shape
    micros, length, rank = args["lat"].shape
    fe, ff = args["ge0"].shape[1], args["gs0"].shape[0] // 4
    mats = 3 * EXP_WIN
    rows = toks // micros
    n_a = wide // 4
    gain_shape = (8, 2 * n_a + rank // 4)
    outs = dict(
        oq=shape((q.shape[1], wide // 4), bf16),
        okr=shape((kkr.shape[0], wide // 4), bf16),
        okvb=shape((rank // 4, kvb.shape[1]), bf16),
        oout=shape((gout.shape[0] // 4, wide), bf16),
        osh=shape((EARLY, ff, wide), bf16),
        osd=shape((ff, wide), bf16),
        oex=shape((mats, fe, wide), bf16),
        zsh=shape((3, EARLY, ff, wide // 2), bf16),
        ogain=shape(gain_shape, f32),
        ograd=shape((toks, wide), bf16),
    )
    vm = pltpu.VMEM
    parts = dict(
        out=(gout.shape[0] // 4, wide // 8),
        sd=(ff, wide // 8),
        kvb=(rank // 4, kvb.shape[1] // 8),
        q=(q.shape[1] // 8, wide // 4),
        kr=(kkr.shape[0] // 8, wide // 4),
    )
    scratch = dict(
        qs=vm(q.shape, bf16),
        kvbs=vm(kvb.shape, bf16),
        kvg=vm((length, 2 * (NOPE + VDIM)), bf16),
        acc=vm((2 * toks, wide // 2), f32),
        dlat=vm((micros, length, rank), f32),
        dk1=vm((micros, length, GROUP_LANES), f32),
        dk2=vm((micros, length, GROUP_LANES), f32),
        dkvb=vm(kvb.shape, bf16),
        pack=vm((micros, length, rank + 2 * ROPE), bf16),
        zs=vm((3, micros, rows, rank + 2 * ROPE), bf16),
        kvd=vm((toks, rank + 2 * ROPE), bf16),
        s_ha=vm((toks, wide), bf16),
        s_q=vm((toks, q.shape[1] // 2), bf16),
        s_kvb=vm((rank, kvb.shape[1] // 2), bf16),
        s_kvd=vm((toks, rank + 2 * ROPE), bf16),
        s_rtr=vm(args["rtr"].shape, bf16),
        gq=vm((q.shape[1] // 2, wide), bf16),
        gshs=vm((EARLY, ff, wide // 2), bf16),
        xb=vm((32, wide), bf16),
        mb=vm((32, wide), f32),
        gains=vm((4,) + gain_shape, f32),
        gz=vm((3,) + gain_shape, f32),
        gp=vm((7,) + gain_shape, f32),
        gs=vm(gain_shape, f32),
        ring_ex=vm((4, 2, fe, wide // 8), bf16),
        ring_out=vm((4, 2) + parts["out"], bf16),
        got1_ex=vm((mats, 2, fe, wide // 8), bf16),
        got2_ex=vm((mats, fe, wide // 8), bf16),
        got1_sh=vm((EARLY, 2, ff, wide // 8), bf16),
        got2_sh=vm((EARLY, ff, wide // 8), bf16),
    )
    for name, part in parts.items():
        scratch["got1_" + name] = vm((4, 2) + part, bf16)
        scratch["got2_" + name] = vm((4,) + part, bf16)
        scratch["got3_" + name] = vm((3,) + part, bf16)
    dma = pltpu.SemaphoreType.DMA
    scratch.update(
        send=dma((BACK_SLOTS,)), recv=dma((BACK_SLOTS,)), load=dma((10,)), keep=dma((8,)), ringsem=dma((4, 2))
    )
    names = (*BACK_IN, *BACK_OUT, *scratch)
    hbm, vmem = pl.BlockSpec(memory_space=HBM), pl.BlockSpec(memory_space=pltpu.VMEM)
    res = pl.pallas_call(
        functools.partial(back_kernel, scale, names),
        in_specs=[hbm] * BACK_HBM + [vmem] * (len(BACK_IN) - BACK_HBM),
        out_specs=[hbm if n not in ("ogain", "ograd") else vmem for n in BACK_OUT],
        out_shape=[outs[n] for n in BACK_OUT],
        scratch_shapes=list(scratch.values()),
        compiler_params=pltpu.CompilerParams(
            collective_id=1, has_side_effects=True, vmem_limit_bytes=61 << 20
        ),
        name="back_all",
    )(*(args[n] for n in BACK_IN))
    return dict(zip(BACK_OUT, res))


def head_split(weight):
    per_head = weight.reshape(HEADS, NOPE + ROPE, weight.shape[1])
    cuts = (0, NOPE, NOPE + HALF_ROPE, NOPE + ROPE)
    return jnp.concatenate(
        [per_head[:, a:b].reshape(-1, weight.shape[1]) for a, b in zip(cuts[:-1], cuts[1:])]
    )


def head_join(weight):
    cols = weight.shape[1]
    nope = weight[: HEADS * NOPE].reshape(HEADS, NOPE, cols)
    first = weight[HEADS * NOPE : HEADS * (NOPE + HALF_ROPE)].reshape(HEADS, HALF_ROPE, cols)
    second = weight[HEADS * (NOPE + HALF_ROPE) :].reshape(HEADS, HALF_ROPE, cols)
    return jnp.concatenate([nope, first, second], axis=1).reshape(-1, cols)


def shards(
    tokens,
    attn_gain,
    q_weight,
    kva_weight,
    kv_gain,
    kvb_weight,
    out_weight,
    ffn_gain,
    router_weight,
    shared_gate,
    shared_up,
    shared_down,
    expert_gate,
    expert_up,
    expert_down,
    expert_ids,
    cotangent,
):
    shard_count = lax.axis_size("shard")
    shard_index = lax.axis_index("shard")
    core = lax.axis_index("rep") % 2
    fast = lax.axis_size("rep") == 8 and shard_count == 4
    micros, rows, width = tokens.shape
    toks = micros * rows
    scale = (NOPE + ROPE) ** (-0.5)
    ga, gk = attn_gain.shape[0], kv_gain.shape[0]

    gain_pack = jnp.concatenate([attn_gain, ffn_gain, kv_gain]).astype(bf16)
    gain_pack = jnp.broadcast_to(gain_pack[None], (16, gain_pack.shape[0]))
    sh_own = jnp.stack([shared_gate, shared_up, shared_down]).astype(bf16)
    query_mat, kr_mat, kvb_mat, out_mat, sh_rest, gains = gather_weights(
        head_split(q_weight).astype(bf16),
        jnp.concatenate([kva_weight, router_weight]).astype(bf16),
        kvb_weight.astype(bf16),
        out_weight.astype(bf16),
        sh_own,
        gain_pack,
        fast,
    )
    gain_rows = gains[:, 0].astype(f32)
    attn_gain_f = gain_rows[:, :ga].reshape(-1)
    ffn_gain_f = gain_rows[:, ga : 2 * ga].reshape(-1)
    kv_gain_f = gain_rows[:, 2 * ga :].reshape(-1)
    kv_down_mat, router_mat = kr_mat[: RANK + ROPE], kr_mat[RANK + ROPE :]
    sh_mats = [sh_own, sh_rest] if fast else [sh_rest]

    def hidden(t, index):
        return jnp.concatenate([dot(t, m[index], 1, 1) for m in sh_mats], axis=1)

    def unhidden(t, index):
        at, total = 0, 0.0
        for m in sh_mats:
            total = total + dot(t[:, at : at + m.shape[1]], m[index], 1, 0)
            at += m.shape[1]
        return total


    x_in = tokens.reshape(toks, width).astype(f32)
    positions = (shard_index * rows + jnp.arange(rows, dtype=jnp.int32)).astype(f32)
    frequency = jnp.exp(
        -jnp.log(rope_base) * (2.0 * jnp.arange(HALF_ROPE, dtype=f32) / ROPE)
    )
    angles = positions[:, None] * frequency[None, :]
    cosine = jnp.tile(jnp.cos(angles), (micros, 1))
    sine = jnp.tile(jnp.sin(angles), (micros, 1))
    cos_all, sin_all = jnp.tile(cosine, (1, HEADS)), jnp.tile(sine, (1, HEADS))
    n1, n2 = HEADS * NOPE, HEADS * (NOPE + HALF_ROPE)
    by_micro = lambda t: t.reshape(micros, rows, t.shape[-1])
    row = lambda t: t.reshape(1, -1)
    if fast:
        h_attn, latent, q_all, lat_all, k1, k2 = front(
            tokens.reshape(toks, width),
            row(attn_gain_f),
            row(kv_gain_f),
            kr_mat,
            cos_all,
            sin_all,
            query_mat,
            micros,
        )
        length = lat_all.shape[1]
    else:
        inv_one = rms_scale(x_in)
        h_attn = (x_in * inv_one * attn_gain_f).astype(bf16)
        q_raw = dot(h_attn, query_mat, 1, 1)
        q_first, q_second = q_raw[:, n1:n2], q_raw[:, n2:]
        qn = by_micro(q_raw[:, :n1].astype(bf16))
        q1 = by_micro((q_first * cos_all - q_second * sin_all).astype(bf16))
        q2 = by_micro((q_second * cos_all + q_first * sin_all).astype(bf16))
        kv_down = dot(h_attn, kv_down_mat, 1, 1)
        latent = kv_down[:, :RANK]
        inv_kv = rms_scale(latent)
        latent_norm = (latent * inv_kv * kv_gain_f).astype(bf16)
        k_first, k_second = kv_down[:, RANK : RANK + HALF_ROPE], kv_down[:, RANK + HALF_ROPE :]
        latent_pack = jnp.concatenate(
            [
                latent_norm,
                (k_first * cosine - k_second * sine).astype(bf16),
                (k_second * cosine + k_first * sine).astype(bf16),
                jnp.zeros((toks, ROPE), bf16),
            ],
            axis=-1,
        )
        packs = z_all(by_micro(latent_pack), fast)
        length = packs.shape[1]
        lat_all = packs[..., :RANK]
        k1 = jnp.tile(packs[..., RANK : RANK + HALF_ROPE], (1, 1, HEAD_GROUP))
        k2 = jnp.tile(packs[..., RANK + HALF_ROPE : RANK + ROPE], (1, 1, HEAD_GROUP))
    key_shard = jnp.arange(length, dtype=jnp.int32) // rows
    if fast:
        key_shard = (shard_index - key_shard) % 4
    key_block = (key_shard * rows + jnp.arange(length, dtype=jnp.int32) % rows) // MASK_BLOCK
    seen = (key_block <= (shard_index * rows) // MASK_BLOCK).astype(f32).reshape(1, length)
    if fast:
        attended = attend_packed(seen, by_micro(q_all), lat_all, k1, k2, kvb_mat, scale)
    else:
        attended = attend(seen, qn, q1, q2, lat_all, k1, k2, kvb_mat, scale)
    attended = attended.reshape(toks, -1)

    x_mid = x_in + dot(attended, out_mat, 1, 0)
    inv_two = rms_scale(x_mid)
    h_ffn = (x_mid * inv_two * ffn_gain_f).astype(bf16)
    router_probs = jax.nn.softmax(dot(h_ffn, router_mat, 1, 1), axis=-1)
    grad_b = cotangent.reshape(toks, width)

    member = jnp.any(
        expert_ids[:, :, None, :] == jnp.arange(EXP_WIN, dtype=jnp.int32)[None, None, :, None], axis=-1
    ).astype(jnp.int32)
    placed = jnp.cumsum(member, axis=1) - 1
    hits = (member[:, :, :, None] == 1) & (
        placed[:, :, :, None] == jnp.arange(CAP, dtype=jnp.int32)
    )
    select = jnp.transpose(hits, (2, 0, 3, 1)).astype(f32)
    select_b = select.astype(bf16)
    h3, c3 = by_micro(h_ffn), by_micro(grad_b)
    gather_slots = lambda t: jnp.einsum(
        "emct,mtd->emcd", select_b, t, preferred_element_type=f32
    ).astype(bf16)
    flat = lambda t: t.reshape(EXP_WIN, micros * CAP, t.shape[-1])
    tall = lambda t: t.reshape(-1, t.shape[-1])
    picked_all = z_all(flat(gather_slots(c3)), fast)
    rows_all = z_all(flat(gather_slots(h3)), fast)

    gate_pre, up_pre = hidden(h_ffn, 0), hidden(h_ffn, 1)
    shared_hidden = (jax.nn.silu(gate_pre) * up_pre).astype(bf16)
    shared_hidden_grad = hidden(grad_b, 2)
    gate_grad_b, up_grad_b = swiglu_back(gate_pre, up_pre, shared_hidden_grad)
    hf_s, cot_s, *sh_s = core_swap(
        [h_ffn, grad_b, gate_grad_b, up_grad_b, shared_hidden],
        (1, 1, None, None, None),
        fast,
        7,
    )
    grad_sh = [
        dot(tall(a), tall(b), 0, 0).astype(bf16) for a, b in zip(sh_s, (hf_s, hf_s, cot_s))
    ]

    picked_all = picked_all.astype(f32)
    slot_probs = jax.nn.softmax(
        jnp.einsum("end,xd->enx", rows_all, router_mat, preferred_element_type=f32), axis=-1
    )
    gates_all = jnp.stack([slot_probs[e, :, e] for e in range(EXP_WIN)])[..., None]
    dy_all = (gates_all * picked_all).astype(bf16)
    eg, eu, ed = expert_gate.astype(bf16), expert_up.astype(bf16), expert_down.astype(bf16)
    bdot = lambda a, b, ca, cb: lax.dot_general(
        a, b, (((ca,), (cb,)), ((0,), (0,))), preferred_element_type=f32
    )
    expert_pre = bdot(rows_all, eg, 2, 2)
    expert_upv = bdot(rows_all, eu, 2, 2)
    expert_hidden = (jax.nn.silu(expert_pre) * expert_upv).astype(bf16)
    expert_part = bdot(expert_hidden, ed, 2, 1)
    gate_part = jnp.sum(picked_all * expert_part, axis=-1, keepdims=True)
    gate_high = gate_part.astype(bf16)
    gate_low = (gate_part - gate_high.astype(f32)).astype(bf16)
    expert_hidden_grad = bdot(dy_all, ed, 2, 2)
    expert_gate_b, expert_up_b = swiglu_back(expert_pre, expert_upv, expert_hidden_grad)
    slot_part = (bdot(expert_gate_b, eg, 2, 1) + bdot(expert_up_b, eu, 2, 1)).astype(bf16)
    slot_part = jnp.concatenate(
        [slot_part, gate_high, gate_low, jnp.zeros(slot_part.shape[:2] + (126,), bf16)], axis=-1
    )
    slot_back = z_home(slot_part, fast)
    expert_back = z_home(expert_part.astype(bf16), fast)

    row_s, dy_s, *ex_s = core_swap(
        [tall(t) for t in (rows_all, dy_all, expert_gate_b, expert_up_b, expert_hidden)],
        (1, 1, None, None, None),
        fast,
        8,
    )
    by_expert = lambda t: t.reshape(2, EXP_WIN, -1, t.shape[-1])
    edot = lambda a, b: jnp.einsum(
        "senf,send->efd", by_expert(a), by_expert(b), preferred_element_type=f32
    ).astype(bf16)
    grad_ex = [edot(a, b) for a, b in zip(ex_s, (row_s, row_s, dy_s))]

    ffn_grad = unhidden(gate_grad_b, 0) + unhidden(up_grad_b, 1)
    back = lambda t: t.reshape(EXP_WIN, micros, CAP, t.shape[-1])
    slot_grad = back(slot_back[..., :width])
    gate_weight_grad = back(slot_back[..., width : width + 2]).sum(axis=-1)
    ffn_grad = ffn_grad + jnp.einsum(
        "emct,emcd->mtd", select, slot_grad, precision=highest
    ).reshape(toks, width)
    probs_grad = jnp.einsum("emct,emc->mte", select, gate_weight_grad, precision=highest)
    probs_grad = jnp.pad(
        probs_grad.reshape(toks, EXP_WIN), ((0, 0), (0, EXPERTS - EXP_WIN))
    )
    logit_grad = (
        router_probs * (probs_grad - jnp.sum(router_probs * probs_grad, axis=-1, keepdims=True))
    ).astype(bf16)
    ffn_grad = ffn_grad + dot(logit_grad, router_mat, 1, 0)
    mid_part, ffn_gain_grad = norm_back(x_mid, inv_two, ffn_gain_f, ffn_grad)
    mid_grad = grad_b.astype(f32) + mid_part
    attn_out_grad = mid_grad.astype(bf16)
    attended_grad = by_micro(dot(attn_out_grad, out_mat, 1, 1).astype(bf16))

    att_s, og_s = core_swap([attended, attn_out_grad], (None, 1), fast, 2)
    grad_out = dot(tall(att_s), tall(og_s), 0, 0).astype(bf16)

    expert_out = back(expert_back)
    slot_gates = jnp.einsum(
        "emct,mte->emc", select, by_micro(router_probs)[..., :EXP_WIN], precision=highest
    )
    routed = jnp.einsum("emct,emcd->mtd", select, slot_gates[..., None] * expert_out, precision=highest)
    layer_output = x_mid + unhidden(shared_hidden, 2) + routed.reshape(toks, width)
    layer_output = layer_output.astype(bf16)

    lane_rows = lambda t: t.reshape(shard_count, -1)
    if fast:
        group_tab = lambda t: jnp.tile(t[:rows], (1, HEAD_GROUP))
        res = back_all(
            dict(
                gs0=grad_sh[0],
                gs1=grad_sh[1],
                gs2=grad_sh[2],
                ge0=grad_ex[0],
                ge1=grad_ex[1],
                ge2=grad_ex[2],
                gout=grad_out,
                q=q_all,
                kvb=kvb_mat,
                kq=query_mat,
                kkr=kr_mat,
                x=tokens.reshape(toks, width),
                mid=mid_grad,
                lat=lat_all,
                k1=k1,
                k2=k2,
                seen=seen,
                do=attended_grad,
                ha=h_attn,
                latent=latent,
                kgain=row(kv_gain_f),
                again=row(attn_gain_f),
                fgain=row(ffn_gain_grad),
                cos=group_tab(cosine),
                sin=group_tab(sine),
                rtr=dot(logit_grad, h_ffn, 0, 0).astype(bf16),
            ),
            scale,
        )
        gq, gkr, gkvb, gout = (res[n] for n in ("oq", "okr", "okvb", "oout"))
        gsh = (res["osh"][0], res["osh"][1], res["osd"])
        gex, gg = res["oex"], res["ogain"][0]
        input_grad = res["ograd"]
    else:
        dqn, dq1, dq2, dlat, dk1, dk2, dkvb = attend_back(
            seen, qn, q1, q2, lat_all, k1, k2, kvb_mat, attended_grad, scale
        )
        fold = lambda t: jnp.sum(t.reshape(micros, length, HEAD_GROUP, HALF_ROPE), axis=2)
        back_pack = jnp.concatenate(
            [dlat, fold(dk1), fold(dk2), jnp.zeros((micros, length, ROPE), f32)], axis=-1
        ).astype(bf16)
        own_back = z_home(back_pack, fast).reshape(toks, -1)
        latent_grad, kv_gain_grad = norm_back(latent, inv_kv, kv_gain_f, own_back[:, :RANK])
        g1, g2 = own_back[:, RANK : RANK + HALF_ROPE], own_back[:, RANK + HALF_ROPE : RANK + ROPE]
        kv_down_grad = jnp.concatenate(
            [latent_grad, g1 * cosine + g2 * sine, g2 * cosine - g1 * sine], axis=-1
        ).astype(bf16)
        dq1, dq2 = dq1.reshape(toks, -1), dq2.reshape(toks, -1)
        q_raw_grad = jnp.concatenate(
            [
                dqn.reshape(toks, -1),
                (dq1 * cos_all + dq2 * sin_all).astype(bf16),
                (dq2 * cos_all - dq1 * sin_all).astype(bf16),
            ],
            axis=-1,
        )
        attn_in_grad = dot(q_raw_grad, query_mat, 1, 0) + dot(kv_down_grad, kv_down_mat, 1, 0)
        x_part, attn_gain_grad = norm_back(x_in, inv_one, attn_gain_f, attn_in_grad)
        input_grad = (mid_grad + x_part).astype(bf16)

        kr_grad = jnp.concatenate(
            [dot(kv_down_grad, h_attn, 0, 0), dot(logit_grad, h_ffn, 0, 0)]
        ).astype(bf16)
        h_s, qg_s, krg_s, kvbg_s = core_swap(
            [h_attn, q_raw_grad, kr_grad, dkvb], (None, 1, 0, 1), fast, 6
        )
        grad_q = dot(tall(qg_s), tall(h_s), 0, 0).astype(bf16)
        grad_kr = (krg_s[0].astype(f32) + krg_s[1].astype(f32)).astype(bf16)
        grad_kvb = (kvbg_s[0].astype(f32) + kvbg_s[1].astype(f32)).astype(bf16)
        gain_grad = jnp.concatenate(
            [lane_rows(attn_gain_grad), lane_rows(ffn_gain_grad), lane_rows(kv_gain_grad)], axis=1
        )
        gain_len = gain_grad.shape[1]
        gain_grad = jnp.pad(gain_grad, ((0, 0), (0, 16 * 128 - gain_len))).reshape(-1, 16, 128)
        gq, gkr, gkvb, gout, gsh, gex, gg = reduce_anywhere(
            grad_q, grad_kr, grad_kvb, grad_out, jnp.stack(grad_sh), jnp.concatenate(grad_ex), gain_grad
        )
        gg = gg.reshape(-1)
    wide = lambda t: t.astype(f32)
    return (
        by_micro(layer_output),
        by_micro(input_grad),
        gg[:ga],
        wide(head_join(gq)),
        wide(gkr[: RANK + ROPE]),
        gg[2 * ga : 2 * ga + gk],
        wide(gkvb),
        wide(gout),
        gg[ga : 2 * ga],
        wide(gkr[RANK + ROPE :]),
        wide(gsh[0]),
        wide(gsh[1]),
        wide(gsh[2]),
        wide(gex[:2]),
        wide(gex[2:4]),
        wide(gex[4:]),
    )


def solution(mesh):
    token_spec = P(None, ("rep", "shard"), None)
    row_spec, col_spec, gain_spec = P("shard", None), P(None, "shard"), P("shard")
    expert_spec = P(None, "shard", None)
    weight_specs = (
        gain_spec,
        col_spec,
        col_spec,
        gain_spec,
        row_spec,
        row_spec,
        gain_spec,
        col_spec,
        row_spec,
        row_spec,
        row_spec,
        expert_spec,
        expert_spec,
        expert_spec,
    )
    return jax.shard_map(
        shards,
        mesh=mesh,
        in_specs=(token_spec,) + weight_specs + (token_spec, token_spec),
        out_specs=(token_spec, token_spec) + weight_specs,
        check_vma=False,
    )
```

```python
import functools

import jax
import jax.numpy as jnp
from jax import lax
from jax.experimental import pallas as pl
from jax.experimental.pallas import tpu as pltpu
from jax.sharding import PartitionSpec as P

HEADS = 16
NOPE = 128
ROPE = 64
VDIM = 128
RANK = 512
EXPERTS = 64
EXP_WIN = 2
MASK_BLOCK = 256
CAP = 16

epsilon = 1e-06
rope_base = 10000.0
masked_score = -1e30
highest = lax.Precision.HIGHEST
bf16 = jnp.bfloat16
f32 = jnp.float32
MESH = pl.DeviceIdType.MESH
HBM = pltpu.HBM
HALF_ROPE = ROPE // 2
HEAD_GROUP = 4
GROUP_LANES = HEAD_GROUP * HALF_ROPE


def dot(a, b, ca, cb):
    return lax.dot_general(a, b, (((ca,), (cb,)), ((), ())), preferred_element_type=f32)


def rms_scale(tensor):
    return lax.rsqrt(jnp.mean(tensor * tensor, axis=-1, keepdims=True) + epsilon)


def norm_back(tensor, inv_rms, gain_vec, gradient):
    scaled_grad = gradient * gain_vec
    inner_mean = jnp.mean(scaled_grad * tensor, axis=-1, keepdims=True)
    input_part = inv_rms * scaled_grad - tensor * (inv_rms * inv_rms * inv_rms) * inner_mean
    gain_part = jnp.sum(gradient * tensor * inv_rms, axis=0)
    return (input_part, gain_part)


def swiglu_back(gate_pre, up_pre, hidden_grad):
    sigmoid_gate = jax.nn.sigmoid(gate_pre)
    silu_gate = gate_pre * sigmoid_gate
    slope = sigmoid_gate * (1.0 + gate_pre * (1.0 - sigmoid_gate))
    return (
        (hidden_grad * up_pre * slope).astype(bf16),
        (hidden_grad * silu_gate).astype(bf16),
    )


def head_scores(qn, q1, q2, kv, k1, k2, seen, scale, head):
    lane = lax.broadcasted_iota(jnp.int32, (1, GROUP_LANES), 1)
    mine = (lane >= head * HALF_ROPE) & (lane < (head + 1) * HALF_ROPE)
    width = NOPE + VDIM
    q_head = qn[:, head * NOPE : (head + 1) * NOPE]
    k_head = kv[:, head * width : head * width + NOPE]
    v_head = kv[:, head * width + NOPE : (head + 1) * width]
    q1m = jnp.where(mine, q1, jnp.zeros_like(q1))
    q2m = jnp.where(mine, q2, jnp.zeros_like(q2))
    scores = dot(q_head, k_head, 1, 1) + dot(q1m, k1, 1, 1) + dot(q2m, k2, 1, 1)
    scores = jnp.where(seen > 0.0, scores * scale, masked_score)
    top = jnp.max(scores, axis=-1, keepdims=True)
    expo = jnp.exp(scores - top)
    probs = expo / jnp.sum(expo, axis=-1, keepdims=True)
    return probs, q_head, k_head, v_head, q1m, q2m, mine


def attend_kernel(scale, seen_ref, qn_ref, q1_ref, q2_ref, lat_ref, k1_ref, k2_ref, kvb_ref, out_ref):
    kv = dot(lat_ref[0], kvb_ref[...], 1, 0).astype(bf16)
    for head in range(HEAD_GROUP):
        probs, _, _, v_head, _, _, _ = head_scores(
            qn_ref[0], q1_ref[0], q2_ref[0], kv, k1_ref[0], k2_ref[0], seen_ref[...], scale, head
        )
        out_ref[0, :, head * VDIM : (head + 1) * VDIM] = dot(
            probs.astype(bf16), v_head, 1, 0
        ).astype(bf16)


def attend_back_kernel(
    scale,
    seen_ref,
    qn_ref,
    q1_ref,
    q2_ref,
    lat_ref,
    k1_ref,
    k2_ref,
    kvb_ref,
    do_ref,
    dqn_ref,
    dq1_ref,
    dq2_ref,
    dlat_ref,
    dk1_ref,
    dk2_ref,
    dkvb_ref,
    kvg_ref,
    acc_ref,
):
    group, micro = pl.program_id(0), pl.program_id(1)
    width = NOPE + VDIM

    @pl.when(group == 0)
    def _():
        dlat_ref[micro] = jnp.zeros(dlat_ref.shape[1:], f32)
        dk1_ref[micro] = jnp.zeros(dk1_ref.shape[1:], f32)
        dk2_ref[micro] = jnp.zeros(dk2_ref.shape[1:], f32)

    lat = lat_ref[0]
    kvb = kvb_ref[...]
    kv = dot(lat, kvb, 1, 0).astype(bf16)
    k1, k2 = k1_ref[0], k2_ref[0]
    dq1 = jnp.zeros(dq1_ref.shape[1:], f32)
    dq2 = jnp.zeros(dq2_ref.shape[1:], f32)
    dk1 = jnp.zeros(k1.shape, f32)
    dk2 = jnp.zeros(k2.shape, f32)
    for head in range(HEAD_GROUP):
        probs, q_head, k_head, v_head, q1m, q2m, mine = head_scores(
            qn_ref[0], q1_ref[0], q2_ref[0], kv, k1, k2, seen_ref[...], scale, head
        )
        d_out = do_ref[0, :, head * VDIM : (head + 1) * VDIM]
        dprobs = dot(d_out, v_head, 1, 1)
        delta = jnp.sum(probs * dprobs, axis=-1, keepdims=True)
        ds = (probs * (dprobs - delta)).astype(bf16)
        dqn_ref[0, :, head * NOPE : (head + 1) * NOPE] = (dot(ds, k_head, 1, 0) * scale).astype(bf16)
        dq1 = dq1 + jnp.where(mine, dot(ds, k1, 1, 0), 0.0)
        dq2 = dq2 + jnp.where(mine, dot(ds, k2, 1, 0), 0.0)
        dk1 = dk1 + dot(ds, q1m, 0, 0)
        dk2 = dk2 + dot(ds, q2m, 0, 0)
        kvg_ref[:, head * width : head * width + NOPE] = (dot(ds, q_head, 0, 0) * scale).astype(bf16)
        kvg_ref[:, head * width + NOPE : (head + 1) * width] = dot(
            probs.astype(bf16), d_out, 0, 0
        ).astype(bf16)
    dq1_ref[0] = dq1 * scale
    dq2_ref[0] = dq2 * scale
    dk1_ref[micro] += dk1 * scale
    dk2_ref[micro] += dk2 * scale
    kvg = kvg_ref[...]
    dlat_ref[micro] += dot(kvg, kvb, 1, 1)
    part = dot(lat, kvg, 0, 0)

    @pl.when(micro == 0)
    def _():
        acc_ref[...] = part

    @pl.when(micro > 0)
    def _():
        acc_ref[...] += part

    @pl.when(micro == pl.num_programs(1) - 1)
    def _():
        dkvb_ref[...] = acc_ref[...].astype(bf16)


def attention_specs(micros, rows, length):
    groups = HEADS // HEAD_GROUP
    wide = HEAD_GROUP * NOPE
    specs = [
        pl.BlockSpec((1, length), lambda g, m: (0, 0)),
        pl.BlockSpec((1, rows, wide), lambda g, m: (m, 0, g)),
        pl.BlockSpec((1, rows, GROUP_LANES), lambda g, m: (m, 0, g)),
        pl.BlockSpec((1, rows, GROUP_LANES), lambda g, m: (m, 0, g)),
        pl.BlockSpec((1, length, RANK), lambda g, m: (m, 0, 0)),
        pl.BlockSpec((1, length, GROUP_LANES), lambda g, m: (m, 0, 0)),
        pl.BlockSpec((1, length, GROUP_LANES), lambda g, m: (m, 0, 0)),
        pl.BlockSpec((RANK, HEAD_GROUP * (NOPE + VDIM)), lambda g, m: (0, g)),
    ]
    return (groups, micros), specs, pl.BlockSpec((1, rows, wide), lambda g, m: (m, 0, g))


def attend(seen, qn, q1, q2, lat, k1, k2, kvb, scale):
    micros, rows, _ = qn.shape
    length = lat.shape[1]
    grid, specs, out_spec = attention_specs(micros, rows, length)
    return pl.pallas_call(
        functools.partial(attend_kernel, scale),
        grid=grid,
        in_specs=specs,
        out_specs=out_spec,
        out_shape=jax.ShapeDtypeStruct(qn.shape, bf16),
        compiler_params=pltpu.CompilerParams(vmem_limit_bytes=48 << 20),
        name="attend",
    )(seen, qn, q1, q2, lat, k1, k2, kvb)


def attend_packed(seen, q, lat, k1, k2, kvb, scale):
    micros, rows, _ = q.shape
    length = lat.shape[1]
    grid, specs, out_spec = attention_specs(micros, rows, length)
    first = HEADS * NOPE // GROUP_LANES
    second = HEADS * (NOPE + HALF_ROPE) // GROUP_LANES
    specs[2] = pl.BlockSpec((1, rows, GROUP_LANES), lambda g, m: (m, 0, first + g))
    specs[3] = pl.BlockSpec((1, rows, GROUP_LANES), lambda g, m: (m, 0, second + g))
    return pl.pallas_call(
        functools.partial(attend_kernel, scale),
        grid=grid,
        in_specs=specs,
        out_specs=out_spec,
        out_shape=jax.ShapeDtypeStruct((micros, rows, HEADS * VDIM), bf16),
        compiler_params=pltpu.CompilerParams(vmem_limit_bytes=48 << 20),
        name="attend",
    )(seen, q, q, q, lat, k1, k2, kvb)


def attend_back(seen, qn, q1, q2, lat, k1, k2, kvb, d_out, scale):
    micros, rows, _ = qn.shape
    length = lat.shape[1]
    grid, specs, out_spec = attention_specs(micros, rows, length)
    whole = lambda g, m: (0, 0, 0)
    return pl.pallas_call(
        functools.partial(attend_back_kernel, scale),
        grid=grid,
        in_specs=specs + [out_spec],
        out_specs=[
            out_spec,
            pl.BlockSpec((1, rows, GROUP_LANES), lambda g, m: (m, 0, g)),
            pl.BlockSpec((1, rows, GROUP_LANES), lambda g, m: (m, 0, g)),
            pl.BlockSpec(lat.shape, whole),
            pl.BlockSpec(k1.shape, whole),
            pl.BlockSpec(k2.shape, whole),
            pl.BlockSpec((RANK, HEAD_GROUP * (NOPE + VDIM)), lambda g, m: (0, g)),
        ],
        out_shape=[
            jax.ShapeDtypeStruct(qn.shape, bf16),
            jax.ShapeDtypeStruct(q1.shape, f32),
            jax.ShapeDtypeStruct(q2.shape, f32),
            jax.ShapeDtypeStruct(lat.shape, f32),
            jax.ShapeDtypeStruct(k1.shape, f32),
            jax.ShapeDtypeStruct(k2.shape, f32),
            jax.ShapeDtypeStruct(kvb.shape, bf16),
        ],
        scratch_shapes=[
            pltpu.VMEM((length, HEAD_GROUP * (NOPE + VDIM)), bf16),
            pltpu.VMEM((RANK, HEAD_GROUP * (NOPE + VDIM)), f32),
        ],
        compiler_params=pltpu.CompilerParams(vmem_limit_bytes=48 << 20),
        name="attend_back",
    )(seen, qn, q1, q2, lat, k1, k2, kvb, d_out)


class Place:
    def __init__(self):
        self.r = lax.axis_index("rep")
        self.z = lax.axis_index("shard")
        self.core = self.r % 2
        self.chip = self.r // 2
        self.x = self.chip % 2
        self.y = self.chip // 2
        self.peer = (self.r + 1 - 2 * self.core, self.z)
        self.across = {
            "x": (self.r + 2 - 4 * self.x, self.z),
            "y": (self.r + 4 - 8 * self.y, self.z),
        }
        cx = self.chip + 1 - 2 * self.x
        cy = self.chip + 2 - 4 * self.y
        self.chips = {"": self.chip, "x": cx, "y": cy, "xy": cx + 2 - 4 * self.y}

    def along(self, step):
        return (self.r, (self.z + step) % 4)

    def shard_at(self, step):
        return (self.z + step) % 4


class Sems:
    def __init__(self, send, recv):
        self.send, self.recv = send, recv
        self.count = 0
        self.pending = []

    def slot(self):
        self.count += 1
        return self.count - 1

    def copy(self, src, dst, slot, device):
        return pltpu.make_async_remote_copy(
            src_ref=src,
            dst_ref=dst,
            send_sem=self.send.at[slot],
            recv_sem=self.recv.at[slot],
            device_id=device,
            device_id_type=MESH,
        )

    def push(self, src, dst, slot, device, when=None):
        under(when, lambda: self.copy(src, dst, slot, device).start())
        self.pending.append((lambda: self.copy(src, dst, slot, device).wait_send(), when))
        return self.pending[-1]

    def settle(self, entry):
        self.pending.remove(entry)
        under(entry[1], entry[0])

    def arrived(self, dst, slot, device, when=None):
        under(when, lambda: self.copy(dst, dst, slot, device).wait_recv())

    def drain(self):
        for wait, when in self.pending:
            under(when, wait)
        self.pending = []


def inside(z):
    return jnp.minimum(jnp.maximum(z, 0), 3)


def under(condition, act):
    if condition is None:
        act()
    else:
        pl.when(condition)(act)


def greet(devices):
    barrier = pltpu.get_barrier_semaphore()
    for device in devices:
        pl.semaphore_signal(barrier, inc=1, device_id=device, device_id_type=MESH)
    pl.semaphore_wait(barrier, len(devices))


def lanes(start, size):
    return pl.ds(pl.multiple_of(start, 128), size)


def rows16(start, size):
    return pl.ds(pl.multiple_of(start, 16), size)


class Through:
    def __init__(self, src, buffer, dst, sem):
        self.into = pltpu.make_async_copy(src, buffer, sem)
        self.out = pltpu.make_async_copy(buffer, dst, sem)

    def start(self):
        self.into.start()

    def turn(self):
        self.into.wait()
        self.out.start()

    def wait(self):
        self.out.wait()


class PlaneGather:
    def __init__(self, sems, place, part, half, by, when=None):
        self.sems, self.place, self.part, self.half, self.by = sems, place, part, half, by
        self.when = when
        self.slots = {k: sems.slot() for k in ("x", "y", "xy", "core")}

    def first(self, src=None):
        p = self.place
        mine = self.part(p.core, p.chip)
        for axis in ("x", "y"):
            self.push(mine if src is None else src, mine, self.slots[axis], p.across[axis])

    def push(self, src, dst, slot, device):
        self.sems.push(src, dst, slot, device, self.when)

    def arrived(self, dst, slot, device):
        self.sems.arrived(dst, slot, device, self.when)

    def second(self):
        p = self.place
        for axis in ("x", "y"):
            got = self.part(p.core, p.chips[axis])
            self.arrived(got, self.slots[axis], p.across[axis])
        via = self.by
        other = "y" if via == "x" else "x"
        got = self.part(p.core, p.chips[via])
        self.push(got, got, self.slots["xy"], p.across[other])

    def third(self):
        p = self.place
        got = self.part(p.core, p.chips["xy"])
        self.arrived(got, self.slots["xy"], p.across["y" if self.by == "x" else "x"])
        half = self.half(p.core)
        self.push(half, half, self.slots["core"], p.peer)

    def fourth(self):
        p = self.place
        self.arrived(self.half(1 - p.core), self.slots["core"], p.peer)


def weight_regions(place, refs, shard):
    q, kr, kvb, out = refs
    ds = q.shape[1] // 4
    cols = lanes(shard * ds, ds)

    def row_split(ref, n):
        half = ref.shape[0] // 2
        return (
            lambda core, chip: ref.at[rows16(core * half + chip * n, n), cols],
            lambda core: ref.at[rows16(core * half, half), cols],
        )

    def col_split(ref, full):
        rows = full // 4
        half = ref.shape[-1] // 2
        n = half // 4
        lead = (slice(None),) * (len(ref.shape) - 2)
        span = rows16(shard * rows, rows)
        return (
            lambda core, chip: ref.at[(*lead, span, lanes(core * half + chip * n, n))],
            lambda core: ref.at[(*lead, span, lanes(core * half, half))],
        )

    return [
        row_split(q, q.shape[0] // 8),
        row_split(kr, kr.shape[0] // 8),
        col_split(kvb, kvb.shape[0]),
        col_split(out, out.shape[0]),
    ]


def own_part(refs, place):
    q, kr, kvb, out, sh = refs
    res = []
    for ref in (q, kr):
        n = ref.shape[0] // 8
        res.append(ref.at[rows16(place.core * 4 * n + place.chip * n, n)])
    for ref in (kvb, out):
        n = ref.shape[-1] // 8
        res.append(ref.at[:, lanes(place.core * 4 * n + place.chip * n, n)])
    n = sh.shape[-1] // 8
    res.append(sh.at[:, :, lanes(place.r * n, n)])
    return res


ITEMS = 4
GATHER_ORDER = (1, 0, 2, 3)
GATHER_SEMS = 6 + ITEMS * 6 * 5
LAG = 8


class WeightGather:
    def __init__(self, place, sems, mine, outs):
        self.place, self.sems, self.mine, self.outs = place, sems, mine, outs
        z = place.z
        self.here = weight_regions(place, outs, z)
        self.slots = {}
        units = []
        for i in GATHER_ORDER:
            for d in (1, 2, 3):
                for s in (1, -1):
                    self.slots[i, d, s] = sems.slot()
                    exists = z >= d if s == 1 else z + d <= 3
                    part, half = weight_regions(place, outs, inside(z - s * d))[i]
                    by = "x" if (d + i) % 2 == 0 else "y"
                    units.append(
                        (i, d, s, exists, part, PlaneGather(sems, place, part, half, by, exists))
                    )
        for i in GATHER_ORDER[:2]:
            self.own(i)
        self.units = units

    def run(self, late):
        units = self.units
        for n in range(len(units) + 3 * LAG):
            if n == len(units):
                late()
            if n < len(units):
                if n % 6 == 0 and n // 6 + 2 < ITEMS:
                    self.own(GATHER_ORDER[n // 6 + 2])
                self.along(units[n])
            for lag, name in ((LAG, "second"), (2 * LAG, "third"), (3 * LAG, "fourth")):
                if 0 <= n - lag < len(units):
                    getattr(units[n - lag][5], name)()

    def onward(self, src, dst, i, d, s, exists=None):
        if d > 3:
            return
        z = self.place.z
        more = z < 3 if s == 1 else z > 0
        if exists is not None:
            more = more & exists
        device = (self.place.r, inside(z + s))
        self.sems.push(src, dst, self.slots[i, d, s], device, more)

    def own(self, i):
        for s in (1, -1):
            self.onward(self.mine[i], self.here[i][0](self.place.core, self.place.chip), i, 1, s)

    def along(self, unit):
        i, d, s, exists, part, spread = unit
        z = self.place.z
        got = part(self.place.core, self.place.chip)
        device = (self.place.r, inside(z - s))
        self.sems.arrived(got, self.slots[i, d, s], device, exists)
        self.onward(got, got, i, d + 1, s, exists)
        spread.first()


def gather_kernel(*refs):
    ins, shared, gain = refs[:ITEMS], refs[ITEMS], refs[ITEMS + 1]
    refs = refs[ITEMS + 2 :]
    outs, shared_out, gains = refs[:ITEMS], refs[ITEMS], refs[ITEMS + 1]
    refs = refs[ITEMS + 2 :]
    buffers, (gain_buffer, send, recv, local) = refs[:ITEMS], refs[ITEMS:]
    place = Place()
    sems = Sems(send, recv)
    greet([place.peer, place.across["x"], place.across["y"]] + [place.along(k) for k in (1, 2, 3)])
    mine = own_part((*ins, shared), place)
    ds = ins[0].shape[1]
    own = [
        outs[0].at[:, lanes(place.z * ds, ds)],
        outs[1].at[:, lanes(place.z * ds, ds)],
        outs[2].at[rows16(place.z * ins[2].shape[0], ins[2].shape[0])],
        outs[3].at[rows16(place.z * ins[3].shape[0], ins[3].shape[0])],
    ]
    kept = [Through(ins[i], buffers[i], own[i], local.at[i]) for i in range(ITEMS)]
    kept.append(Through(gain, gain_buffer, gains.at[place.z], local.at[ITEMS]))
    gain_slots = [sems.slot() for _ in range(3)]
    shared_slots = [sems.slot() for _ in range(3)]
    for k in (1, 2, 3):
        sems.push(gain, gains.at[place.z], gain_slots[k - 1], place.along(k))
    job = WeightGather(place, sems, mine, outs)
    for copy in kept:
        copy.start()
    for copy in kept:
        copy.turn()

    def late():
        for k in (1, 2, 3):
            sems.push(mine[ITEMS], shared_out.at[:, k - 1], shared_slots[k - 1], place.along(k))

    job.run(late)
    for k in (1, 2, 3):
        sems.arrived(gains.at[place.shard_at(4 - k)], gain_slots[k - 1], place.along(4 - k))
        sems.arrived(shared_out.at[:, k - 1], shared_slots[k - 1], place.along(4 - k))
    sems.drain()
    for copy in kept:
        copy.wait()


def gather_weights(q, kr, kvb, out, sh, gain, fast):
    if not fast:
        every = lambda w, axis: lax.all_gather(w, "shard", axis=axis, tiled=True)
        return (
            every(q, 1),
            every(kr, 1),
            every(kvb, 0),
            every(out, 0),
            every(sh, 1),
            lax.all_gather(gain, "shard", axis=0),
        )
    shape = jax.ShapeDtypeStruct
    *whole, rest, gains = pl.pallas_call(
        gather_kernel,
        in_specs=[pl.BlockSpec(memory_space=HBM)] * 6,
        out_specs=[pl.BlockSpec(memory_space=HBM)] * 6,
        out_shape=[
            shape((q.shape[0], q.shape[1] * 4), bf16),
            shape((kr.shape[0], kr.shape[1] * 4), bf16),
            shape((kvb.shape[0] * 4, kvb.shape[1]), bf16),
            shape((out.shape[0] * 4, out.shape[1]), bf16),
            shape((3, 3, sh.shape[1], sh.shape[2] // 8), bf16),
            shape((4,) + gain.shape, bf16),
        ],
        scratch_shapes=[pltpu.VMEM(w.shape, bf16) for w in (q, kr, kvb, out, gain)]
        + [
            pltpu.SemaphoreType.DMA((GATHER_SEMS,)),
            pltpu.SemaphoreType.DMA((GATHER_SEMS,)),
            pltpu.SemaphoreType.DMA((ITEMS + 1,)),
        ],
        compiler_params=pltpu.CompilerParams(
            collective_id=0, has_side_effects=True, vmem_limit_bytes=32 << 20
        ),
        name="gather_weights",
    )(q, kr, kvb, out, sh, gain)
    rest = lax.all_gather(rest, "rep", axis=3, tiled=True)
    return (*whole, rest.reshape(3, -1, sh.shape[2]), gains)


def along_z(tensor, step):
    return lax.ppermute(tensor, "shard", [(i, (i + step) % 4) for i in range(4)])


def over(tensor, mask):
    return lax.ppermute(tensor, "rep", [(i, i ^ mask) for i in range(8)])


def z_all(tensor, fast):
    if not fast:
        return lax.all_gather(tensor, "shard", axis=1, tiled=True)
    return jnp.concatenate([tensor] + [along_z(tensor, k) for k in (1, 2, 3)], axis=1)


def z_home(tensor, fast):
    if not fast:
        return lax.psum_scatter(tensor.astype(f32), "shard", scatter_dimension=1, tiled=True)
    rows = tensor.shape[1] // 4
    blocks = [lax.slice_in_dim(tensor, k * rows, (k + 1) * rows, axis=1) for k in range(4)]
    got = [along_z(blocks[k], -k).astype(f32) for k in (1, 2, 3)]
    return blocks[0].astype(f32) + got[0] + got[1] + got[2]


def front_kernel(
    x_ref,
    again_ref,
    kgain_ref,
    kr_ref,
    cos_ref,
    sin_ref,
    mat_ref,
    ha_ref,
    latent_ref,
    q_ref,
    lat_ref,
    k1_ref,
    k2_ref,
    tiles,
    pack,
    packs,
    send,
    recv,
    load,
):
    place = Place()
    sems = Sems(send, recv)
    size = tiles.shape[1]

    def fetch(t):
        return pltpu.make_async_copy(
            mat_ref.at[t * size : (t + 1) * size], tiles.at[t % 2], load.at[t % 2]
        )

    fetch(0).start()
    greet([place.along(k) for k in (1, 2, 3)])

    def normed(t, carry):
        span = pl.ds(pl.multiple_of(t * 32, 32), 32)
        x = x_ref[span].astype(f32)
        ha_ref[span] = (x * rms_scale(x) * again_ref[...]).astype(bf16)
        return carry

    lax.fori_loop(0, x_ref.shape[0] // 32, normed, 0)
    ha = ha_ref[...]
    kv_down = dot(ha, kr_ref[...], 1, 1)
    latent = kv_down[:, :RANK]
    latent_ref[...] = latent
    micros, rows, _ = pack.shape
    normal = (latent * rms_scale(latent) * kgain_ref[...]).astype(bf16)
    first = kv_down[:, RANK : RANK + HALF_ROPE]
    second = kv_down[:, RANK + HALF_ROPE : RANK + ROPE]
    cosine, sine = cos_ref[:, :HALF_ROPE], sin_ref[:, :HALF_ROPE]
    turned = (
        (first * cosine - second * sine).astype(bf16),
        (second * cosine + first * sine).astype(bf16),
    )
    for micro in range(micros):
        span = slice(micro * rows, (micro + 1) * rows)
        pack[micro, :, :RANK] = normal[span]
        pack[micro, :, RANK : RANK + HALF_ROPE] = turned[0][span]
        pack[micro, :, RANK + HALF_ROPE : RANK + ROPE] = turned[1][span]
        pack[micro, :, RANK + ROPE :] = jnp.zeros((rows, ROPE), bf16)
    block = lambda k: packs.at[:, k * rows : (k + 1) * rows]
    for k in (1, 2, 3):
        sems.push(pack, block(k), k - 1, place.along(k))

    count = mat_ref.shape[0] // size
    held = None
    for t in range(count):
        fetch(t).wait()
        if t + 1 < count:
            fetch(t + 1).start()
        value = dot(ha, tiles[t % 2], 1, 1)
        if t < count - 2:
            q_ref[:, t * size : (t + 1) * size] = value.astype(bf16)
        elif held is None:
            held = value
        else:
            cosine, sine = cos_ref[...], sin_ref[...]
            q_ref[:, (t - 1) * size : t * size] = (held * cosine - value * sine).astype(bf16)
            q_ref[:, t * size : (t + 1) * size] = (value * cosine + held * sine).astype(bf16)

    for k in (1, 2, 3):
        sems.arrived(block(k), k - 1, place.along(4 - k))
    for micro in range(micros):
        for k in range(4):
            span = slice(k * rows, (k + 1) * rows)
            part = pack[micro] if k == 0 else packs[micro, span]
            lat_ref[micro, span] = part[:, :RANK]
            for ref, start in ((k1_ref, RANK), (k2_ref, RANK + HALF_ROPE)):
                lanes32 = part[:, start : start + HALF_ROPE]
                ref[micro, span] = jnp.concatenate([lanes32] * HEAD_GROUP, axis=1)
    sems.drain()


def front(x, again, kgain, kr, cosine, sine, mat, micros):
    toks, wide = x.shape
    length = 4 * (toks // micros)
    shape = jax.ShapeDtypeStruct
    vm, dma = pltpu.VMEM, pltpu.SemaphoreType.DMA
    size = HEADS * HALF_ROPE
    packed = RANK + 2 * ROPE
    vmem = pl.BlockSpec(memory_space=pltpu.VMEM)
    return pl.pallas_call(
        front_kernel,
        in_specs=[vmem] * 6 + [pl.BlockSpec(memory_space=HBM)],
        out_specs=[vmem] * 6,
        out_shape=[
            shape((toks, wide), bf16),
            shape((toks, RANK), f32),
            shape((toks, mat.shape[0]), bf16),
            shape((micros, length, RANK), bf16),
            shape((micros, length, GROUP_LANES), bf16),
            shape((micros, length, GROUP_LANES), bf16),
        ],
        scratch_shapes=[
            vm((2, size, wide), bf16),
            vm((micros, toks // micros, packed), bf16),
            vm((micros, length, packed), bf16),
            dma((3,)),
            dma((3,)),
            dma((2,)),
        ],
        compiler_params=pltpu.CompilerParams(
            collective_id=9, has_side_effects=True, vmem_limit_bytes=40 << 20
        ),
        name="front",
    )(x, again, kgain, kr, cosine, sine, mat)


def swap_kernel(count, axes, *refs):
    ins, outs, buffers = (refs[n * count : (n + 1) * count] for n in range(3))
    send, recv, local = refs[3 * count :]
    place = Place()
    sems = Sems(send, recv)
    greet([place.peer])

    def cut(i, core):
        if axes[i] is None:
            return ins[i]
        n = ins[i].shape[axes[i]] // 2
        if axes[i] == 0:
            return ins[i].at[rows16(core * n, n)]
        return ins[i].at[:, lanes(core * n, n)]

    for i in range(count):
        sems.push(cut(i, 1 - place.core), outs[i].at[1], sems.slot(), place.peer)
    kept = [
        Through(cut(i, place.core), buffers[i], outs[i].at[0], local.at[i]) for i in range(count)
    ]
    for copy in kept:
        copy.start()
    for copy in kept:
        copy.turn()
    for i in range(count):
        sems.arrived(outs[i].at[1], i, place.peer)
    sems.drain()
    for copy in kept:
        copy.wait()


def core_swap(arrays, axes, fast, ident):
    count = len(arrays)
    if not fast:
        reps = lax.axis_size("rep")
        core = lax.axis_index("rep") % 2
        res = []
        for a, axis in zip(arrays, axes):
            keep = give = a
            if axis is not None:
                n = a.shape[axis] // 2
                keep = lax.dynamic_slice_in_dim(a, core * n, n, axis)
                give = lax.dynamic_slice_in_dim(a, (1 - core) * n, n, axis)
            got = lax.ppermute(give, "rep", [(i, i + 1 - 2 * (i % 2)) for i in range(reps)])
            res.append(jnp.stack([keep, got]))
        return res
    shapes = [
        tuple(n // 2 if d == axis else n for d, n in enumerate(a.shape))
        for a, axis in zip(arrays, axes)
    ]
    return pl.pallas_call(
        functools.partial(swap_kernel, count, axes),
        in_specs=[pl.BlockSpec(memory_space=HBM)] * count,
        out_specs=[pl.BlockSpec(memory_space=HBM)] * count,
        out_shape=[jax.ShapeDtypeStruct((2,) + s, a.dtype) for s, a in zip(shapes, arrays)],
        scratch_shapes=[pltpu.VMEM(s, a.dtype) for s, a in zip(shapes, arrays)]
        + [
            pltpu.SemaphoreType.DMA((count,)),
            pltpu.SemaphoreType.DMA((count,)),
            pltpu.SemaphoreType.DMA((count,)),
        ],
        compiler_params=pltpu.CompilerParams(
            collective_id=ident, has_side_effects=True, vmem_limit_bytes=32 << 20
        ),
        name="core_swap",
    )(*arrays)


def add_rows(dst, terms):
    lead = dst.shape[:-2]
    rows = max(n for n in (16, 32, 48, 64, 80) if dst.shape[-2] % n == 0)
    steps = dst.shape[-2] // rows

    def body(step, carry):
        span = pl.ds(pl.multiple_of(step * rows, rows), rows)
        where = (slice(None),) * len(lead) + (span,)
        total = terms[0][where].astype(f32)
        for t in terms[1:]:
            total = total + t[where].astype(f32)
        dst[where] = total.astype(dst.dtype)
        return carry

    lax.fori_loop(0, steps, body, 0)


def reduce_anywhere(q, kr, kvb, out, sh, ex, gain):
    core = lax.axis_index("rep") % 2

    def whole(g, axis):
        wide = jnp.zeros(g.shape[:axis] + (g.shape[axis] * 2,) + g.shape[axis + 1 :], f32)
        return lax.dynamic_update_slice_in_dim(wide, g.astype(f32), core * g.shape[axis], axis)

    def total(g, axis, along):
        g = lax.psum_scatter(whole(g, axis), "shard", scatter_dimension=along, tiled=True)
        return lax.psum(g, "rep")

    return (
        total(q, 0, 1),
        total(kr, 0, 1),
        total(kvb, 1, 0),
        total(out, 1, 0),
        total(sh, 2, 1),
        lax.psum(whole(ex, 2), "rep"),
        lax.psum(lax.psum_scatter(gain, "shard", scatter_dimension=0, tiled=True), "rep")[0],
    )


class Unit:
    def __init__(self, job, name, u, axis, part, got1, got2, own=None, home=None, got3=None, last=None):
        self.job, self.name, self.u = job, name, u
        self.axis, self.other = axis, "y" if axis == "x" else "x"
        self.part, self.got1, self.got2, self.own = part, got1, got2, own
        self.home, self.got3, self.last = home, got3, last
        self.slots = [job.sems.slot() for _ in range(4)]

    def stage1(self):
        job = self.job
        place = job.place
        for n, chip in enumerate((self.axis, "xy")):
            job.sems.push(
                self.part(place.chips[chip]), self.got1.at[n], self.slots[n], place.across[self.axis]
            )

    def stage2(self):
        place = self.job.place
        if self.own is not None:
            ring, sem = self.own
            self.loads = [
                pltpu.make_async_copy(
                    self.part(place.chips["" if n == 0 else self.other]), ring.at[n], sem.at[n]
                )
                for n in (0, 1)
            ]
            for copy in self.loads:
                copy.start()
            self.mine = [ring.at[0], ring.at[1]]
        else:
            self.mine = [self.part(place.chips[""]), self.part(place.chips[self.other])]

    def stage3(self):
        sems, place = self.job.sems, self.job.place
        for n in (1, 0):
            if self.own is not None:
                self.loads[n].wait()
            sems.arrived(self.got1.at[n], self.slots[n], place.across[self.axis])
            add_rows(self.got1.at[n], [self.got1.at[n], self.mine[n]])
            if n == 1:
                sems.push(self.got1.at[1], self.got2, self.slots[2], place.across[self.other])

    def stage4(self):
        sems, place = self.job.sems, self.job.place
        sems.arrived(self.got2, self.slots[2], place.across[self.other])
        add_rows(self.got1.at[0], [self.got1.at[0], self.got2])
        if self.home:
            sems.push(self.got1.at[0], self.got3.at[self.home - 1], self.slots[3], place.along(self.home))

    def stage5(self):
        if self.last is None:
            return
        job = self.job
        place = job.place
        for unit in job.units:
            if unit.name == self.name and unit.home:
                got = unit.got3.at[unit.home - 1]
                job.sems.arrived(got, unit.slots[3], place.along(4 - unit.home))
        if self.got3 is not None:
            add_rows(self.got1.at[0], [self.got1.at[0]] + [self.got3.at[n] for n in range(3)])
        src, part, half, sem, by = self.last
        self.stay = pltpu.make_async_copy(src, part(place.core, place.chip), sem)
        self.stay.start()
        self.spread = PlaneGather(job.sems, place, part, half, by)
        self.spread.first(src)

    def stage6(self):
        if self.last is not None:
            self.spread.second()

    def stage7(self):
        if self.last is not None:
            self.stay.wait()
            self.spread.third()

    def stage8(self):
        if self.last is not None:
            self.spread.fourth()


class Pump:
    LAGS = (0, 4, 2, 4, 3, 2, 2, 2)

    def __init__(self, place, sems):
        self.place, self.sems = place, sems
        self.units = []
        self.at = [0] * 8

    def tick(self, flush=False):
        for n in range(8):
            ahead = len(self.units) if n == 0 else self.at[n - 1]
            if self.at[n] < ahead - (0 if flush else self.LAGS[n]):
                getattr(self.units[self.at[n]], "stage%d" % (n + 1))()
                self.at[n] += 1

    def ahead(self, count):
        for _ in range(min(count, len(self.units) - self.at[0])):
            self.units[self.at[0]].stage1()
            self.at[0] += 1

    def run(self, count):
        for _ in range(count):
            self.tick()

    def end(self):
        while self.at[-1] < len(self.units):
            before = list(self.at)
            self.tick()
            if self.at == before:
                self.tick(True)


BACK_IN = (
    "gs0",
    "gs1",
    "gs2",
    "ge0",
    "ge1",
    "ge2",
    "gout",
    "q",
    "kvb",
    "kq",
    "kkr",
    "x",
    "mid",
    "lat",
    "k1",
    "k2",
    "seen",
    "do",
    "ha",
    "latent",
    "kgain",
    "again",
    "fgain",
    "cos",
    "sin",
    "rtr",
)
BACK_HBM = 13
BACK_OUT = (
    "oq",
    "okr",
    "okvb",
    "oout",
    "osh",
    "osd",
    "oex",
    "zsh",
    "ogain",
    "ograd",
)
BACK_SLOTS = 6 + 3 + 5 + 10 + 28 * 4 + 7 * 4
EARLY = 2


def back_kernel(scale, names, *refs):
    r = dict(zip(names, refs))
    place = Place()
    sems = Sems(r["send"], r["recv"])
    others = [place.peer]
    for axes in ("x", "y", "xy"):
        for flip in (place.core, 1 - place.core):
            others.append((place.chips[axes] * 2 + flip, place.z))
    greet(others + [place.along(k) for k in (1, 2, 3)])
    load = r["load"]
    pump = Pump(place, sems)
    core = place.core
    toks = r["ha"].shape[0]
    rows = toks // 2

    shared = [r["gs0"], r["gs1"], r["gs2"]]
    experts = [r["ge0"], r["ge1"], r["ge2"]]
    ff = shared[0].shape[0] // 4
    shared_slots = [[sems.slot() for _ in range(3)] for _ in range(EARLY)]
    for j in range(EARLY):
        for k in (1, 2, 3):
            sems.push(
                shared[j].at[k * ff : (k + 1) * ff],
                r["zsh"].at[k - 1, j],
                shared_slots[j][k - 1],
                place.along(4 - k),
            )
    swap = {name: sems.slot() for name in ("ha", "kvb", "q", "kvd", "rtr")}
    sems.push(r["ha"], r["s_ha"], swap["ha"], place.peer)
    sems.push(r["rtr"], r["s_rtr"], swap["rtr"], place.peer)
    begin = [
        pltpu.make_async_copy(r["q"], r["qs"], load.at[0]),
        pltpu.make_async_copy(r["kvb"], r["kvbs"], load.at[1]),
    ]
    for copy in begin:
        copy.start()

    def out_split(o, by_rows):
        if by_rows:
            half = o.shape[0] // 2
            n = half // 4
            return (
                lambda c, chip: o.at[rows16(c * half + chip * n, n)],
                lambda c: o.at[rows16(c * half, half)],
            )
        half = o.shape[-1] // 2
        n = half // 4
        lead = (slice(None),) * (len(o.shape) - 1)
        return (
            lambda c, chip: o.at[(*lead, lanes(c * half + chip * n, n))],
            lambda c: o.at[(*lead, lanes(c * half, half))],
        )

    rings = 0

    def ring(shape_ref):
        nonlocal rings
        slot = rings % 4
        rings += 1
        return slot

    def add_matrices(name, sources, out, by, ringed):
        count = len(sources)
        for u in range(count):
            n = sources[u].shape[-1] // 4
            own = None
            if ringed:
                slot = ring(None)
                own = (r["ring_" + name].at[slot], r["ringsem"].at[slot])
            last = None
            if u == count - 1:
                last = (r["got1_" + name].at[:, 0], *out_split(out, False), r["keep"].at[len(pump.units) % 8], by)
            pump.units.append(
                Unit(
                    pump,
                    name,
                    u,
                    "x" if u % 2 == 0 else "y",
                    lambda chip, u=u: sources[u].at[:, lanes(chip * n, n)],
                    r["got1_" + name].at[u],
                    r["got2_" + name].at[u],
                    own=own,
                    last=last,
                )
            )

    def add_sharded(name, part_of, out, by_rows, by, ringed=None):
        for n, k in enumerate((1, 2, 3, 4)):
            u, s = k % 4, place.shard_at(k)
            own = None
            if ringed:
                slot = ring(None)
                own = (r["ring_" + ringed].at[slot], r["ringsem"].at[slot])
            last = None
            if k == 4:
                last = (r["got1_" + name].at[0, 0], *out_split(out, by_rows), r["keep"].at[len(pump.units) % 8], by)
            pump.units.append(
                Unit(
                    pump,
                    name,
                    u,
                    "x" if n % 2 == 0 else "y",
                    lambda chip, s=s, k=k: part_of(s, k, chip),
                    r["got1_" + name].at[u],
                    r["got2_" + name].at[u],
                    own=own,
                    home=k % 4,
                    got3=r["got3_" + name],
                    last=last,
                )
            )

    add_matrices("ex", [t.at[e] for t in experts for e in range(EXP_WIN)], r["oex"], "x", True)
    block = r["gout"].shape[0] // 4
    n_out = r["gout"].shape[1] // 4
    add_sharded(
        "out",
        lambda s, k, chip: r["gout"].at[rows16(s * block, block), lanes(chip * n_out, n_out)],
        r["oout"],
        False,
        "y",
        "out",
    )
    n_sd = shared[EARLY].shape[1] // 4
    add_sharded(
        "sd",
        lambda s, k, chip: shared[EARLY].at[
            (4 - k) % 4 * ff : ((4 - k) % 4 + 1) * ff, lanes(chip * n_sd, n_sd)
        ],
        r["osd"],
        False,
        "x",
        "ex",
    )
    pump.ahead(4)
    for copy in begin:
        copy.wait()

    qs, kvbs, kvg, acc, dlat, dkvb = (r[n] for n in ("qs", "kvbs", "kvg", "acc", "dlat", "dkvb"))
    n1 = HEADS * NOPE
    n2 = HEADS * (NOPE + HALF_ROPE)
    width = NOPE + VDIM
    lane = lax.broadcasted_iota(jnp.int32, (1, GROUP_LANES), 1)

    def attention_step(group, micro):
        span = slice(micro * rows, (micro + 1) * rows)
        at = group * GROUP_LANES
        lat, k1, k2 = r["lat"][micro], r["k1"][micro], r["k2"][micro]
        q1, q2 = qs[span, n1 + at : n1 + at + GROUP_LANES], qs[span, n2 + at : n2 + at + GROUP_LANES]
        dq1 = jnp.zeros(q1.shape, f32)
        dq2 = jnp.zeros(q2.shape, f32)
        dk1 = jnp.zeros(k1.shape, f32)
        dk2 = jnp.zeros(k2.shape, f32)
        for pair in (0, 1):
            cols = slice((group * 4 + pair * 2) * width, (group * 4 + pair * 2 + 2) * width)
            weight = kvbs[:, cols]
            kv = dot(lat, weight, 1, 0).astype(bf16)
            for n in (0, 1):
                head = pair * 2 + n
                here = slice((group * 4 + head) * NOPE, (group * 4 + head + 1) * NOPE)
                mine = (lane >= head * HALF_ROPE) & (lane < (head + 1) * HALF_ROPE)
                q_head = qs[span, here]
                k_head = kv[:, n * width : n * width + NOPE]
                v_head = kv[:, n * width + NOPE : (n + 1) * width]
                q1m = jnp.where(mine, q1, jnp.zeros_like(q1))
                q2m = jnp.where(mine, q2, jnp.zeros_like(q2))
                scores = dot(q_head, k_head, 1, 1) + dot(q1m, k1, 1, 1) + dot(q2m, k2, 1, 1)
                scores = jnp.where(r["seen"][...] > 0.0, scores * scale, masked_score)
                expo = jnp.exp(scores - jnp.max(scores, axis=-1, keepdims=True))
                probs = expo / jnp.sum(expo, axis=-1, keepdims=True)
                d_out = r["do"][micro, :, here]
                dprobs = dot(d_out, v_head, 1, 1)
                delta = jnp.sum(probs * dprobs, axis=-1, keepdims=True)
                ds = (probs * (dprobs - delta)).astype(bf16)
                qs[span, here] = (dot(ds, k_head, 1, 0) * scale).astype(bf16)
                dq1 = dq1 + jnp.where(mine, dot(ds, k1, 1, 0), 0.0)
                dq2 = dq2 + jnp.where(mine, dot(ds, k2, 1, 0), 0.0)
                dk1 = dk1 + dot(ds, q1m, 0, 0)
                dk2 = dk2 + dot(ds, q2m, 0, 0)
                kvg[:, n * width : n * width + NOPE] = (dot(ds, q_head, 0, 0) * scale).astype(bf16)
                kvg[:, n * width + NOPE : (n + 1) * width] = dot(
                    probs.astype(bf16), d_out, 0, 0
                ).astype(bf16)
            terms = kvg[...]
            if group == 0 and pair == 0:
                dlat[micro] = dot(terms, weight, 1, 1)
            else:
                dlat[micro] += dot(terms, weight, 1, 1)
            part = dot(lat, terms, 0, 0)
            hold = slice(pair * 2 * width, (pair + 1) * 2 * width)
            if micro == 0:
                acc[:, hold] = part
            else:
                dkvb[:, cols] = (acc[:, hold] + part).astype(bf16)
        dq1, dq2 = dq1 * scale, dq2 * scale
        cosine, sine = r["cos"][...], r["sin"][...]
        qs[span, n1 + at : n1 + at + GROUP_LANES] = (dq1 * cosine + dq2 * sine).astype(bf16)
        qs[span, n2 + at : n2 + at + GROUP_LANES] = (dq2 * cosine - dq1 * sine).astype(bf16)
        for ref, value in ((r["dk1"], dk1), (r["dk2"], dk2)):
            if group == 0:
                ref[micro] = value * scale
            else:
                ref[micro] += value * scale

    for group in range(HEADS // HEAD_GROUP):
        for micro in (0, 1):
            attention_step(group, micro)
            pump.run(1)

    pack, zs = r["pack"], r["zs"]
    fold = lambda t: sum(t[:, n * HALF_ROPE : (n + 1) * HALF_ROPE] for n in range(HEAD_GROUP))
    for micro in (0, 1):
        pack[micro, :, :RANK] = dlat[micro].astype(bf16)
        pack[micro, :, RANK : RANK + HALF_ROPE] = fold(r["dk1"][micro]).astype(bf16)
        pack[micro, :, RANK + HALF_ROPE : RANK + ROPE] = fold(r["dk2"][micro]).astype(bf16)
        pack[micro, :, RANK + ROPE :] = jnp.zeros((pack.shape[1], ROPE), bf16)
    z_slots = [sems.slot() for _ in range(3)]
    for k in (1, 2, 3):
        sems.push(pack.at[:, k * rows : (k + 1) * rows], zs.at[k - 1], z_slots[k - 1], place.along(4 - k))
    half_q, half_kvb = qs.shape[1] // 2, dkvb.shape[1] // 2
    sems.push(qs.at[:, lanes((1 - core) * half_q, half_q)], r["s_q"], swap["q"], place.peer)
    kvb_push = sems.push(
        dkvb.at[:, lanes((1 - core) * half_kvb, half_kvb)], r["s_kvb"], swap["kvb"], place.peer
    )
    pump.run(1)

    sems.arrived(r["s_kvb"], swap["kvb"], place.peer)
    add_rows(r["s_kvb"], [r["s_kvb"], dkvb.at[:, lanes(core * half_kvb, half_kvb)]])
    n_kvb, b_kvb = half_kvb // 4, dkvb.shape[0] // 4
    add_sharded(
        "kvb",
        lambda s, k, chip: r["s_kvb"].at[rows16(s * b_kvb, b_kvb), lanes(chip * n_kvb, n_kvb)],
        r["okvb"],
        False,
        "x",
    )
    sems.arrived(r["s_ha"], swap["ha"], place.peer)
    sems.arrived(r["s_q"], swap["q"], place.peer)
    gq, ha, s_ha = r["gq"], r["ha"], r["s_ha"]

    def q_tile(t, carry):
        own = qs[:, lanes(core * half_q + t * 128, 128)]
        got = r["s_q"][:, lanes(t * 128, 128)]
        gq[rows16(t * 128, 128)] = (dot(own, ha[...], 0, 0) + dot(got, s_ha[...], 0, 0)).astype(bf16)
        return carry

    for part in range(4):
        lax.fori_loop(part * 3, part * 3 + 3, q_tile, 0)
        pump.run(1)
    r_q, c_q = gq.shape[0] // 4, gq.shape[1] // 4
    add_sharded(
        "q",
        lambda s, k, chip: gq.at[rows16(chip * r_q, r_q), lanes(s * c_q, c_q)],
        r["oq"],
        True,
        "y",
    )
    pump.run(4)

    for k in (1, 2, 3):
        sems.arrived(zs.at[k - 1], z_slots[k - 1], place.along(k))
    kvd, gains = r["kvd"], r["gains"]
    kv_gain_grad = jnp.zeros((1, RANK), f32)
    for micro in (0, 1):
        span = slice(micro * rows, (micro + 1) * rows)
        total = pack[micro, :rows].astype(f32)
        for k in range(3):
            total = total + zs[k, micro].astype(f32)
        upstream, latent = total[:, :RANK], r["latent"][span]
        inv = rms_scale(latent)
        scaled = upstream * r["kgain"][...]
        inner = jnp.mean(scaled * latent, axis=-1, keepdims=True)
        kvd[span, :RANK] = (inv * scaled - latent * (inv * inv * inv) * inner).astype(bf16)
        kv_gain_grad = kv_gain_grad + jnp.sum(upstream * latent * inv, axis=0, keepdims=True)
        g1, g2 = total[:, RANK : RANK + HALF_ROPE], total[:, RANK + HALF_ROPE : RANK + ROPE]
        cosine, sine = r["cos"][:, :HALF_ROPE], r["sin"][:, :HALF_ROPE]
        kvd[span, RANK : RANK + HALF_ROPE] = (g1 * cosine + g2 * sine).astype(bf16)
        kvd[span, RANK + HALF_ROPE : RANK + ROPE] = (g2 * cosine - g1 * sine).astype(bf16)
        kvd[span, RANK + ROPE :] = jnp.zeros((rows, ROPE), bf16)
    sems.push(kvd, r["s_kvd"], swap["kvd"], place.peer)

    tile = 384
    tiles = [("kq", t * tile, tile) for t in range(qs.shape[1] // tile)]
    tiles += [("kkr", 0, tile), ("kkr", tile, r["kkr"].shape[0] - tile)]
    wide = ha.shape[1]
    half_w = wide // 2

    def fetch(t):
        name, start, n = tiles[t]
        return pltpu.make_async_copy(
            r[name].at[start : start + n],
            kvbs.at[:n, (t % 2) * wide : (t % 2 + 1) * wide],
            load.at[2 + t % 2],
        )

    fetch(0).start()
    for t, (name, start, n) in enumerate(tiles):
        fetch(t).wait()
        if t + 1 < len(tiles):
            fetch(t + 1).start()
        left = (qs if name == "kq" else kvd)[:, start : start + n]
        for half in (0, 1):
            base = (t % 2) * wide + half * half_w
            value = dot(left, kvbs[:n, base : base + half_w], 1, 0)
            where = slice(half * toks, (half + 1) * toks)
            if t == 0:
                acc[where] = value
            else:
                acc[where] += value
        if t % 2 == 1:
            pump.run(1)

    cols = shared[0].shape[1]
    for j in range(EARLY):
        for k in (1, 2, 3):
            sems.arrived(r["zsh"].at[k - 1, j], shared_slots[j][k - 1], place.along(k))
        copies = [pltpu.make_async_copy(shared[j].at[:ff], kvbs.at[:ff, :cols], load.at[6])]
        for k in range(3):
            copies.append(
                pltpu.make_async_copy(
                    r["zsh"].at[k, j], kvbs.at[:ff, (k + 1) * cols : (k + 2) * cols], load.at[7 + k]
                )
            )
        for copy in copies:
            copy.start()
        for copy in copies:
            copy.wait()
        add_rows(r["gshs"].at[j], [kvbs.at[:ff, k * cols : (k + 1) * cols] for k in range(4)])
    add_matrices("sh", [r["gshs"].at[j] for j in range(EARLY)], r["osh"], "y", False)
    pump.run(2)

    sems.arrived(r["s_kvd"], swap["kvd"], place.peer)
    sems.arrived(r["s_rtr"], swap["rtr"], place.peer)
    sems.settle(kvb_push)
    half_kr = r["kkr"].shape[0] // 2
    r_kr, c_kr = half_kr // 4, wide // 4
    edges = sorted(set(list(range(0, 2 * half_kr + 1, 128)) + [half_kr]))
    for start, stop in zip(edges[:-1], edges[1:]):
        value = dot(kvd[:, start:stop], ha[...], 0, 0)
        value = value + dot(r["s_kvd"][:, start:stop], s_ha[...], 0, 0)
        n = start // half_kr
        if stop == 2 * half_kr:
            first = RANK + ROPE - start
            both = r["rtr"][...].astype(f32) + r["s_rtr"][...].astype(f32)
            value = jnp.concatenate([value[:first], both])
        dkvb[start - n * half_kr : stop - n * half_kr, n * wide : (n + 1) * wide] = value.astype(bf16)
    add_sharded(
        "kr",
        lambda s, k, chip: dkvb.at[rows16(chip * r_kr, r_kr), lanes(core * wide + s * c_kr, c_kr)],
        r["okr"],
        True,
        "x",
    )
    pump.run(2)

    again = r["again"][...]
    attn_gain_grad = jnp.zeros((1, wide), f32)
    step = 32
    for start in range(0, toks, step):
        fetched = [
            pltpu.make_async_copy(r[a].at[start : start + step], r[b], load.at[4 + n])
            for n, (a, b) in enumerate((("x", "xb"), ("mid", "mb")))
        ]
        for copy in fetched:
            copy.start()
        for copy in fetched:
            copy.wait()
        x = r["xb"][...].astype(f32)
        upstream = jnp.concatenate(
            [acc[start : start + step], acc[toks + start : toks + start + step]], axis=1
        )
        inv = rms_scale(x)
        scaled = upstream * again
        inner = jnp.mean(scaled * x, axis=-1, keepdims=True)
        part = inv * scaled - x * (inv * inv * inv) * inner
        r["ograd"][start : start + step] = (r["mb"][...] + part).astype(bf16)
        attn_gain_grad = attn_gain_grad + jnp.sum(upstream * x * inv, axis=0, keepdims=True)
        pump.run(1)
    n_a, n_k = wide // 4, RANK // 4
    gains[...] = jnp.zeros(gains.shape, f32)
    for s in range(4):
        gains[s, 0:1, :n_a] = attn_gain_grad[:, s * n_a : (s + 1) * n_a]
        gains[s, 0:1, n_a : 2 * n_a] = r["fgain"][:, s * n_a : (s + 1) * n_a]
        gains[s, 0:1, 2 * n_a :] = kv_gain_grad[:, s * n_k : (s + 1) * n_k]
    gain_slots = [sems.slot() for _ in range(3 + 7)]
    gz, gp, gs = r["gz"], r["gp"], r["gs"]
    for k in (1, 2, 3):
        sems.push(gains.at[place.shard_at(k)], gz.at[k - 1], gain_slots[k - 1], place.along(k))
    pump.run(2)

    for k in (1, 2, 3):
        sems.arrived(gz.at[k - 1], gain_slots[k - 1], place.along(4 - k))
    gs[...] = gains[place.z] + gz[0] + gz[1] + gz[2]
    for n, device in enumerate(others):
        sems.push(gs, gp.at[n], gain_slots[3 + n], device)
    pump.end()
    total = gs[...]
    for n, device in enumerate(others):
        sems.arrived(gp.at[n], gain_slots[3 + n], device)
        total = total + gp[n]
    r["ogain"][...] = total
    sems.drain()


def back_all(args, scale):
    shape = jax.ShapeDtypeStruct
    gout, q, kvb, kq, kkr = (args[n] for n in ("gout", "q", "kvb", "kq", "kkr"))
    toks, wide = args["ha"].shape
    micros, length, rank = args["lat"].shape
    fe, ff = args["ge0"].shape[1], args["gs0"].shape[0] // 4
    mats = 3 * EXP_WIN
    rows = toks // micros
    n_a = wide // 4
    gain_shape = (8, 2 * n_a + rank // 4)
    outs = dict(
        oq=shape((q.shape[1], wide // 4), bf16),
        okr=shape((kkr.shape[0], wide // 4), bf16),
        okvb=shape((rank // 4, kvb.shape[1]), bf16),
        oout=shape((gout.shape[0] // 4, wide), bf16),
        osh=shape((EARLY, ff, wide), bf16),
        osd=shape((ff, wide), bf16),
        oex=shape((mats, fe, wide), bf16),
        zsh=shape((3, EARLY, ff, wide // 2), bf16),
        ogain=shape(gain_shape, f32),
        ograd=shape((toks, wide), bf16),
    )
    vm = pltpu.VMEM
    parts = dict(
        out=(gout.shape[0] // 4, wide // 8),
        sd=(ff, wide // 8),
        kvb=(rank // 4, kvb.shape[1] // 8),
        q=(q.shape[1] // 8, wide // 4),
        kr=(kkr.shape[0] // 8, wide // 4),
    )
    scratch = dict(
        qs=vm(q.shape, bf16),
        kvbs=vm(kvb.shape, bf16),
        kvg=vm((length, 2 * (NOPE + VDIM)), bf16),
        acc=vm((2 * toks, wide // 2), f32),
        dlat=vm((micros, length, rank), f32),
        dk1=vm((micros, length, GROUP_LANES), f32),
        dk2=vm((micros, length, GROUP_LANES), f32),
        dkvb=vm(kvb.shape, bf16),
        pack=vm((micros, length, rank + 2 * ROPE), bf16),
        zs=vm((3, micros, rows, rank + 2 * ROPE), bf16),
        kvd=vm((toks, rank + 2 * ROPE), bf16),
        s_ha=vm((toks, wide), bf16),
        s_q=vm((toks, q.shape[1] // 2), bf16),
        s_kvb=vm((rank, kvb.shape[1] // 2), bf16),
        s_kvd=vm((toks, rank + 2 * ROPE), bf16),
        s_rtr=vm(args["rtr"].shape, bf16),
        gq=vm((q.shape[1] // 2, wide), bf16),
        gshs=vm((EARLY, ff, wide // 2), bf16),
        xb=vm((32, wide), bf16),
        mb=vm((32, wide), f32),
        gains=vm((4,) + gain_shape, f32),
        gz=vm((3,) + gain_shape, f32),
        gp=vm((7,) + gain_shape, f32),
        gs=vm(gain_shape, f32),
        ring_ex=vm((4, 2, fe, wide // 8), bf16),
        ring_out=vm((4, 2) + parts["out"], bf16),
        got1_ex=vm((mats, 2, fe, wide // 8), bf16),
        got2_ex=vm((mats, fe, wide // 8), bf16),
        got1_sh=vm((EARLY, 2, ff, wide // 8), bf16),
        got2_sh=vm((EARLY, ff, wide // 8), bf16),
    )
    for name, part in parts.items():
        scratch["got1_" + name] = vm((4, 2) + part, bf16)
        scratch["got2_" + name] = vm((4,) + part, bf16)
        scratch["got3_" + name] = vm((3,) + part, bf16)
    dma = pltpu.SemaphoreType.DMA
    scratch.update(
        send=dma((BACK_SLOTS,)), recv=dma((BACK_SLOTS,)), load=dma((10,)), keep=dma((8,)), ringsem=dma((4, 2))
    )
    names = (*BACK_IN, *BACK_OUT, *scratch)
    hbm, vmem = pl.BlockSpec(memory_space=HBM), pl.BlockSpec(memory_space=pltpu.VMEM)
    res = pl.pallas_call(
        functools.partial(back_kernel, scale, names),
        in_specs=[hbm] * BACK_HBM + [vmem] * (len(BACK_IN) - BACK_HBM),
        out_specs=[hbm if n not in ("ogain", "ograd") else vmem for n in BACK_OUT],
        out_shape=[outs[n] for n in BACK_OUT],
        scratch_shapes=list(scratch.values()),
        compiler_params=pltpu.CompilerParams(
            collective_id=1, has_side_effects=True, vmem_limit_bytes=61 << 20
        ),
        name="back_all",
    )(*(args[n] for n in BACK_IN))
    return dict(zip(BACK_OUT, res))


def head_split(weight):
    per_head = weight.reshape(HEADS, NOPE + ROPE, weight.shape[1])
    cuts = (0, NOPE, NOPE + HALF_ROPE, NOPE + ROPE)
    return jnp.concatenate(
        [per_head[:, a:b].reshape(-1, weight.shape[1]) for a, b in zip(cuts[:-1], cuts[1:])]
    )


def head_join(weight):
    cols = weight.shape[1]
    nope = weight[: HEADS * NOPE].reshape(HEADS, NOPE, cols)
    first = weight[HEADS * NOPE : HEADS * (NOPE + HALF_ROPE)].reshape(HEADS, HALF_ROPE, cols)
    second = weight[HEADS * (NOPE + HALF_ROPE) :].reshape(HEADS, HALF_ROPE, cols)
    return jnp.concatenate([nope, first, second], axis=1).reshape(-1, cols)


def shards(
    tokens,
    attn_gain,
    q_weight,
    kva_weight,
    kv_gain,
    kvb_weight,
    out_weight,
    ffn_gain,
    router_weight,
    shared_gate,
    shared_up,
    shared_down,
    expert_gate,
    expert_up,
    expert_down,
    expert_ids,
    cotangent,
):
    shard_count = lax.axis_size("shard")
    shard_index = lax.axis_index("shard")
    core = lax.axis_index("rep") % 2
    fast = lax.axis_size("rep") == 8 and shard_count == 4
    micros, rows, width = tokens.shape
    toks = micros * rows
    scale = (NOPE + ROPE) ** (-0.5)
    ga, gk = attn_gain.shape[0], kv_gain.shape[0]

    gain_pack = jnp.concatenate([attn_gain, ffn_gain, kv_gain]).astype(bf16)
    gain_pack = jnp.broadcast_to(gain_pack[None], (16, gain_pack.shape[0]))
    sh_own = jnp.stack([shared_gate, shared_up, shared_down]).astype(bf16)
    query_mat, kr_mat, kvb_mat, out_mat, sh_rest, gains = gather_weights(
        head_split(q_weight).astype(bf16),
        jnp.concatenate([kva_weight, router_weight]).astype(bf16),
        kvb_weight.astype(bf16),
        out_weight.astype(bf16),
        sh_own,
        gain_pack,
        fast,
    )
    gain_rows = gains[:, 0].astype(f32)
    attn_gain_f = gain_rows[:, :ga].reshape(-1)
    ffn_gain_f = gain_rows[:, ga : 2 * ga].reshape(-1)
    kv_gain_f = gain_rows[:, 2 * ga :].reshape(-1)
    kv_down_mat, router_mat = kr_mat[: RANK + ROPE], kr_mat[RANK + ROPE :]
    sh_mats = [sh_own, sh_rest] if fast else [sh_rest]

    def hidden(t, index):
        return jnp.concatenate([dot(t, m[index], 1, 1) for m in sh_mats], axis=1)

    def unhidden(t, index):
        at, total = 0, 0.0
        for m in sh_mats:
            total = total + dot(t[:, at : at + m.shape[1]], m[index], 1, 0)
            at += m.shape[1]
        return total


    x_in = tokens.reshape(toks, width).astype(f32)
    positions = (shard_index * rows + jnp.arange(rows, dtype=jnp.int32)).astype(f32)
    frequency = jnp.exp(
        -jnp.log(rope_base) * (2.0 * jnp.arange(HALF_ROPE, dtype=f32) / ROPE)
    )
    angles = positions[:, None] * frequency[None, :]
    cosine = jnp.tile(jnp.cos(angles), (micros, 1))
    sine = jnp.tile(jnp.sin(angles), (micros, 1))
    cos_all, sin_all = jnp.tile(cosine, (1, HEADS)), jnp.tile(sine, (1, HEADS))
    n1, n2 = HEADS * NOPE, HEADS * (NOPE + HALF_ROPE)
    by_micro = lambda t: t.reshape(micros, rows, t.shape[-1])
    row = lambda t: t.reshape(1, -1)
    if fast:
        h_attn, latent, q_all, lat_all, k1, k2 = front(
            tokens.reshape(toks, width),
            row(attn_gain_f),
            row(kv_gain_f),
            kr_mat,
            cos_all,
            sin_all,
            query_mat,
            micros,
        )
        length = lat_all.shape[1]
    else:
        inv_one = rms_scale(x_in)
        h_attn = (x_in * inv_one * attn_gain_f).astype(bf16)
        q_raw = dot(h_attn, query_mat, 1, 1)
        q_first, q_second = q_raw[:, n1:n2], q_raw[:, n2:]
        qn = by_micro(q_raw[:, :n1].astype(bf16))
        q1 = by_micro((q_first * cos_all - q_second * sin_all).astype(bf16))
        q2 = by_micro((q_second * cos_all + q_first * sin_all).astype(bf16))
        kv_down = dot(h_attn, kv_down_mat, 1, 1)
        latent = kv_down[:, :RANK]
        inv_kv = rms_scale(latent)
        latent_norm = (latent * inv_kv * kv_gain_f).astype(bf16)
        k_first, k_second = kv_down[:, RANK : RANK + HALF_ROPE], kv_down[:, RANK + HALF_ROPE :]
        latent_pack = jnp.concatenate(
            [
                latent_norm,
                (k_first * cosine - k_second * sine).astype(bf16),
                (k_second * cosine + k_first * sine).astype(bf16),
                jnp.zeros((toks, ROPE), bf16),
            ],
            axis=-1,
        )
        packs = z_all(by_micro(latent_pack), fast)
        length = packs.shape[1]
        lat_all = packs[..., :RANK]
        k1 = jnp.tile(packs[..., RANK : RANK + HALF_ROPE], (1, 1, HEAD_GROUP))
        k2 = jnp.tile(packs[..., RANK + HALF_ROPE : RANK + ROPE], (1, 1, HEAD_GROUP))
    key_shard = jnp.arange(length, dtype=jnp.int32) // rows
    if fast:
        key_shard = (shard_index - key_shard) % 4
    key_block = (key_shard * rows + jnp.arange(length, dtype=jnp.int32) % rows) // MASK_BLOCK
    seen = (key_block <= (shard_index * rows) // MASK_BLOCK).astype(f32).reshape(1, length)
    if fast:
        attended = attend_packed(seen, by_micro(q_all), lat_all, k1, k2, kvb_mat, scale)
    else:
        attended = attend(seen, qn, q1, q2, lat_all, k1, k2, kvb_mat, scale)
    attended = attended.reshape(toks, -1)

    x_mid = x_in + dot(attended, out_mat, 1, 0)
    inv_two = rms_scale(x_mid)
    h_ffn = (x_mid * inv_two * ffn_gain_f).astype(bf16)
    router_probs = jax.nn.softmax(dot(h_ffn, router_mat, 1, 1), axis=-1)
    grad_b = cotangent.reshape(toks, width)

    member = jnp.any(
        expert_ids[:, :, None, :] == jnp.arange(EXP_WIN, dtype=jnp.int32)[None, None, :, None], axis=-1
    ).astype(jnp.int32)
    placed = jnp.cumsum(member, axis=1) - 1
    hits = (member[:, :, :, None] == 1) & (
        placed[:, :, :, None] == jnp.arange(CAP, dtype=jnp.int32)
    )
    select = jnp.transpose(hits, (2, 0, 3, 1)).astype(f32)
    select_b = select.astype(bf16)
    h3, c3 = by_micro(h_ffn), by_micro(grad_b)
    gather_slots = lambda t: jnp.einsum(
        "emct,mtd->emcd", select_b, t, preferred_element_type=f32
    ).astype(bf16)
    flat = lambda t: t.reshape(EXP_WIN, micros * CAP, t.shape[-1])
    tall = lambda t: t.reshape(-1, t.shape[-1])
    picked_all = z_all(flat(gather_slots(c3)), fast)
    rows_all = z_all(flat(gather_slots(h3)), fast)

    gate_pre, up_pre = hidden(h_ffn, 0), hidden(h_ffn, 1)
    shared_hidden = (jax.nn.silu(gate_pre) * up_pre).astype(bf16)
    shared_hidden_grad = hidden(grad_b, 2)
    gate_grad_b, up_grad_b = swiglu_back(gate_pre, up_pre, shared_hidden_grad)
    hf_s, cot_s, *sh_s = core_swap(
        [h_ffn, grad_b, gate_grad_b, up_grad_b, shared_hidden],
        (1, 1, None, None, None),
        fast,
        7,
    )
    grad_sh = [
        dot(tall(a), tall(b), 0, 0).astype(bf16) for a, b in zip(sh_s, (hf_s, hf_s, cot_s))
    ]

    picked_all = picked_all.astype(f32)
    slot_probs = jax.nn.softmax(
        jnp.einsum("end,xd->enx", rows_all, router_mat, preferred_element_type=f32), axis=-1
    )
    gates_all = jnp.stack([slot_probs[e, :, e] for e in range(EXP_WIN)])[..., None]
    dy_all = (gates_all * picked_all).astype(bf16)
    eg, eu, ed = expert_gate.astype(bf16), expert_up.astype(bf16), expert_down.astype(bf16)
    bdot = lambda a, b, ca, cb: lax.dot_general(
        a, b, (((ca,), (cb,)), ((0,), (0,))), preferred_element_type=f32
    )
    expert_pre = bdot(rows_all, eg, 2, 2)
    expert_upv = bdot(rows_all, eu, 2, 2)
    expert_hidden = (jax.nn.silu(expert_pre) * expert_upv).astype(bf16)
    expert_part = bdot(expert_hidden, ed, 2, 1)
    gate_part = jnp.sum(picked_all * expert_part, axis=-1, keepdims=True)
    gate_high = gate_part.astype(bf16)
    gate_low = (gate_part - gate_high.astype(f32)).astype(bf16)
    expert_hidden_grad = bdot(dy_all, ed, 2, 2)
    expert_gate_b, expert_up_b = swiglu_back(expert_pre, expert_upv, expert_hidden_grad)
    slot_part = (bdot(expert_gate_b, eg, 2, 1) + bdot(expert_up_b, eu, 2, 1)).astype(bf16)
    slot_part = jnp.concatenate(
        [slot_part, gate_high, gate_low, jnp.zeros(slot_part.shape[:2] + (126,), bf16)], axis=-1
    )
    slot_back = z_home(slot_part, fast)
    expert_back = z_home(expert_part.astype(bf16), fast)

    row_s, dy_s, *ex_s = core_swap(
        [tall(t) for t in (rows_all, dy_all, expert_gate_b, expert_up_b, expert_hidden)],
        (1, 1, None, None, None),
        fast,
        8,
    )
    by_expert = lambda t: t.reshape(2, EXP_WIN, -1, t.shape[-1])
    edot = lambda a, b: jnp.einsum(
        "senf,send->efd", by_expert(a), by_expert(b), preferred_element_type=f32
    ).astype(bf16)
    grad_ex = [edot(a, b) for a, b in zip(ex_s, (row_s, row_s, dy_s))]

    ffn_grad = unhidden(gate_grad_b, 0) + unhidden(up_grad_b, 1)
    back = lambda t: t.reshape(EXP_WIN, micros, CAP, t.shape[-1])
    slot_grad = back(slot_back[..., :width])
    gate_weight_grad = back(slot_back[..., width : width + 2]).sum(axis=-1)
    ffn_grad = ffn_grad + jnp.einsum(
        "emct,emcd->mtd", select, slot_grad, precision=highest
    ).reshape(toks, width)
    probs_grad = jnp.einsum("emct,emc->mte", select, gate_weight_grad, precision=highest)
    probs_grad = jnp.pad(
        probs_grad.reshape(toks, EXP_WIN), ((0, 0), (0, EXPERTS - EXP_WIN))
    )
    logit_grad = (
        router_probs * (probs_grad - jnp.sum(router_probs * probs_grad, axis=-1, keepdims=True))
    ).astype(bf16)
    ffn_grad = ffn_grad + dot(logit_grad, router_mat, 1, 0)
    mid_part, ffn_gain_grad = norm_back(x_mid, inv_two, ffn_gain_f, ffn_grad)
    mid_grad = grad_b.astype(f32) + mid_part
    attn_out_grad = mid_grad.astype(bf16)
    attended_grad = by_micro(dot(attn_out_grad, out_mat, 1, 1).astype(bf16))

    att_s, og_s = core_swap([attended, attn_out_grad], (None, 1), fast, 2)
    grad_out = dot(tall(att_s), tall(og_s), 0, 0).astype(bf16)

    expert_out = back(expert_back)
    slot_gates = jnp.einsum(
        "emct,mte->emc", select, by_micro(router_probs)[..., :EXP_WIN], precision=highest
    )
    routed = jnp.einsum("emct,emcd->mtd", select, slot_gates[..., None] * expert_out, precision=highest)
    layer_output = x_mid + unhidden(shared_hidden, 2) + routed.reshape(toks, width)
    layer_output = layer_output.astype(bf16)

    lane_rows = lambda t: t.reshape(shard_count, -1)
    if fast:
        group_tab = lambda t: jnp.tile(t[:rows], (1, HEAD_GROUP))
        res = back_all(
            dict(
                gs0=grad_sh[0],
                gs1=grad_sh[1],
                gs2=grad_sh[2],
                ge0=grad_ex[0],
                ge1=grad_ex[1],
                ge2=grad_ex[2],
                gout=grad_out,
                q=q_all,
                kvb=kvb_mat,
                kq=query_mat,
                kkr=kr_mat,
                x=tokens.reshape(toks, width),
                mid=mid_grad,
                lat=lat_all,
                k1=k1,
                k2=k2,
                seen=seen,
                do=attended_grad,
                ha=h_attn,
                latent=latent,
                kgain=row(kv_gain_f),
                again=row(attn_gain_f),
                fgain=row(ffn_gain_grad),
                cos=group_tab(cosine),
                sin=group_tab(sine),
                rtr=dot(logit_grad, h_ffn, 0, 0).astype(bf16),
            ),
            scale,
        )
        gq, gkr, gkvb, gout = (res[n] for n in ("oq", "okr", "okvb", "oout"))
        gsh = (res["osh"][0], res["osh"][1], res["osd"])
        gex, gg = res["oex"], res["ogain"][0]
        input_grad = res["ograd"]
    else:
        dqn, dq1, dq2, dlat, dk1, dk2, dkvb = attend_back(
            seen, qn, q1, q2, lat_all, k1, k2, kvb_mat, attended_grad, scale
        )
        fold = lambda t: jnp.sum(t.reshape(micros, length, HEAD_GROUP, HALF_ROPE), axis=2)
        back_pack = jnp.concatenate(
            [dlat, fold(dk1), fold(dk2), jnp.zeros((micros, length, ROPE), f32)], axis=-1
        ).astype(bf16)
        own_back = z_home(back_pack, fast).reshape(toks, -1)
        latent_grad, kv_gain_grad = norm_back(latent, inv_kv, kv_gain_f, own_back[:, :RANK])
        g1, g2 = own_back[:, RANK : RANK + HALF_ROPE], own_back[:, RANK + HALF_ROPE : RANK + ROPE]
        kv_down_grad = jnp.concatenate(
            [latent_grad, g1 * cosine + g2 * sine, g2 * cosine - g1 * sine], axis=-1
        ).astype(bf16)
        dq1, dq2 = dq1.reshape(toks, -1), dq2.reshape(toks, -1)
        q_raw_grad = jnp.concatenate(
            [
                dqn.reshape(toks, -1),
                (dq1 * cos_all + dq2 * sin_all).astype(bf16),
                (dq2 * cos_all - dq1 * sin_all).astype(bf16),
            ],
            axis=-1,
        )
        attn_in_grad = dot(q_raw_grad, query_mat, 1, 0) + dot(kv_down_grad, kv_down_mat, 1, 0)
        x_part, attn_gain_grad = norm_back(x_in, inv_one, attn_gain_f, attn_in_grad)
        input_grad = (mid_grad + x_part).astype(bf16)

        kr_grad = jnp.concatenate(
            [dot(kv_down_grad, h_attn, 0, 0), dot(logit_grad, h_ffn, 0, 0)]
        ).astype(bf16)
        h_s, qg_s, krg_s, kvbg_s = core_swap(
            [h_attn, q_raw_grad, kr_grad, dkvb], (None, 1, 0, 1), fast, 6
        )
        grad_q = dot(tall(qg_s), tall(h_s), 0, 0).astype(bf16)
        grad_kr = (krg_s[0].astype(f32) + krg_s[1].astype(f32)).astype(bf16)
        grad_kvb = (kvbg_s[0].astype(f32) + kvbg_s[1].astype(f32)).astype(bf16)
        gain_grad = jnp.concatenate(
            [lane_rows(attn_gain_grad), lane_rows(ffn_gain_grad), lane_rows(kv_gain_grad)], axis=1
        )
        gain_len = gain_grad.shape[1]
        gain_grad = jnp.pad(gain_grad, ((0, 0), (0, 16 * 128 - gain_len))).reshape(-1, 16, 128)
        gq, gkr, gkvb, gout, gsh, gex, gg = reduce_anywhere(
            grad_q, grad_kr, grad_kvb, grad_out, jnp.stack(grad_sh), jnp.concatenate(grad_ex), gain_grad
        )
        gg = gg.reshape(-1)
    wide = lambda t: t.astype(f32)
    return (
        by_micro(layer_output),
        by_micro(input_grad),
        gg[:ga],
        wide(head_join(gq)),
        wide(gkr[: RANK + ROPE]),
        gg[2 * ga : 2 * ga + gk],
        wide(gkvb),
        wide(gout),
        gg[ga : 2 * ga],
        wide(gkr[RANK + ROPE :]),
        wide(gsh[0]),
        wide(gsh[1]),
        wide(gsh[2]),
        wide(gex[:2]),
        wide(gex[2:4]),
        wide(gex[4:]),
    )


def solution(mesh):
    token_spec = P(None, ("rep", "shard"), None)
    row_spec, col_spec, gain_spec = P("shard", None), P(None, "shard"), P("shard")
    expert_spec = P(None, "shard", None)
    weight_specs = (
        gain_spec,
        col_spec,
        col_spec,
        gain_spec,
        row_spec,
        row_spec,
        gain_spec,
        col_spec,
        row_spec,
        row_spec,
        row_spec,
        expert_spec,
        expert_spec,
        expert_spec,
    )
    return jax.shard_map(
        shards,
        mesh=mesh,
        in_specs=(token_spec,) + weight_specs + (token_spec, token_spec),
        out_specs=(token_spec, token_spec) + weight_specs,
        check_vma=False,
    )
```
